32 devices in a mesh: dp: 8 (over z, x), sub: 4 (over y, core).
Axes of the slice: x: 2, y: 2, z: 4, core: 2. Of those that a mesh axis runs over, the one named last changes fastest.
Arguments:
- tokens: bfloat16 [32768, 512], P(('dp', 'sub')), may hold values from -6 to 6
- cotangent: bfloat16 [32768, 512], P(('dp', 'sub')), may hold values from -6 to 6
- item_lengths: int32 [32, 8], P(('dp', 'sub')), may hold values from 0 to 1024, as said below
- joint_weight: bfloat16 [512, 1536], P(('dp', 'sub')), may hold values from -0.25 to 0.25
- output_weight: bfloat16 [512, 512], P(('dp', 'sub')), may hold values from -1.5 to 1.5
- expand_weight: bfloat16 [512, 2048], P(('dp', 'sub')), may hold values from -0.25 to 0.25
- reduce_weight: bfloat16 [2048, 512], P(('dp', 'sub')), may hold values from -0.125 to 0.125
- attn_gain: bfloat16 [512], P(('dp', 'sub')), may hold values from 0.099609375 to 1.8984375
- attn_shift: bfloat16 [512], P(('dp', 'sub')), may hold values from -3 to 3
- ffn_gain: bfloat16 [512], P(('dp', 'sub')), may hold values from 0.099609375 to 1.8984375
- ffn_shift: bfloat16 [512], P(('dp', 'sub')), may hold values from -3 to 3
- expand_bias: bfloat16 [2048], P(('dp', 'sub')), may hold values from -3 to 3
- reduce_bias: bfloat16 [512], P(('dp', 'sub')), may hold values from -3 to 3
Outputs:
- mixed: bfloat16 [32768, 512], P(('dp', 'sub'))
- token_grad: bfloat16 [32768, 512], P(('dp', 'sub'))
- joint_grad: float32 [512, 1536], P(('dp', 'sub'))
- output_grad: float32 [512, 512], P(('dp', 'sub'))
- expand_grad: float32 [512, 2048], P(('dp', 'sub'))
- reduce_grad: float32 [2048, 512], P(('dp', 'sub'))
- attn_gain_grad: float32 [512], P(('dp', 'sub'))
- attn_shift_grad: float32 [512], P(('dp', 'sub'))
- ffn_gain_grad: float32 [512], P(('dp', 'sub'))
- ffn_shift_grad: float32 [512], P(('dp', 'sub'))
- expand_bias_grad: float32 [2048], P(('dp', 'sub'))
- reduce_bias_grad: float32 [512], P(('dp', 'sub'))
The draws below stay inside these ranges and needn't reach their ends.
Inputs may be any that keep to these rules, and one draw needn't show every extreme that they name: item_lengths[d, i] is the length of item i of device d, 0 for an empty slot; nonzero lengths are 64 or more; a device's items, each rounded up to a multiple of 16, fit in its 1024 slots; device 0's first item has 1024 tokens.
All inputs are finite; a program needn't handle non-finite values.
Results may differ from the reference program's by a relative error of at most 0.011.
Values may be sent and summed in bfloat16 or wider, within the bound.
No kernel may reach another device: no remote copies, remote signals or barrier semaphores. Data moves between devices by JAX's collectives and lax.ppermute only.
A program may use at most 256 MiB of HBM per device.

```python
import math
import jax
import jax.numpy as jnp
from jax import lax

D = 512
HEADS = 8
FF = 2048
BLOCK = 16
LEVELS = 7
MAXLEN = 1024
MINLEN = 64
ITEMS = 8
TOK_DEV = 1024
TOKENS = 32768
DEVICES = 32


def draw_item_lengths(key, part):
    key = jax.random.fold_in(key, 11)
    first, second, third = jax.random.split(key, 3)
    doublings = (MAXLEN // MINLEN).bit_length() - 1
    shape = (DEVICES, ITEMS)
    power = jnp.minimum(jax.random.randint(first, shape, 0, doublings + 1), jax.random.randint(second, shape, 0, doublings + 1))
    base = jnp.left_shift(jnp.full(shape, MINLEN, jnp.int32), power)
    length = jnp.minimum(base + jax.random.randint(third, shape, 0, base), MAXLEN)
    length = length.at[0, 0].set(MAXLEN)
    padded = (length + BLOCK - 1) // BLOCK * BLOCK
    kept = jnp.cumsum(padded, axis=1) <= TOK_DEV
    return jnp.where(kept, length, 0).astype(jnp.int32)


def spiked(values, key, source, target, shards_of, factor):
    def block_of(axis_at):
        return (jnp.arange(values.shape[axis_at]) // (values.shape[axis_at] // shards_of)).reshape((-1,) + (1,) * (values.ndim - 1 - axis_at))

    one_side = jax.random.permutation(key, shards_of)[block_of(target)]
    far = (block_of(target) + shards_of // 2) % shards_of
    return jnp.where((block_of(source) == one_side) | (block_of(source) == far), factor * values, values)


def levels(rng, extent, cuts, low, top_value):
    loudness, own = 1.0, jax.random.fold_in(rng, 6)
    for axis_at, blocks in cuts:
        heights = jnp.exp(jax.random.uniform(jax.random.fold_in(own, axis_at), (blocks,), jnp.float32, low / len(cuts), top_value / len(cuts)))
        loudness = loudness * jnp.repeat(heights, extent[axis_at] // blocks).reshape([-1 if axis == axis_at else 1 for axis in range(len(extent))])
    return loudness


def bell_draw(key, dims, scale, most, shards=(), kind=jnp.bfloat16):
    array = jax.random.normal(key, dims, jnp.float32) * scale
    if len(shards) > 0:
        array = levels(key, dims, shards, -0.22, 0.18) * array
    return jnp.clip(array, min=-most, max=most).astype(kind)


def noise_with(key, dims, deviation, reach, shards, heavy, kind=jnp.bfloat16):
    result = deviation * jax.random.normal(key, dims, jnp.float32)
    if shards:
        result = result * levels(key, dims, shards, -0.22, 0.18)
    return jnp.clip(spiked(result, jax.random.fold_in(key, 3), *heavy), -reach, reach).astype(kind)


def setup_inputs(seed: int = 0) -> dict:
    streams_of = jax.random.split(jax.random.key(seed), 14)
    return {
        "tokens": bell_draw(streams_of[0], (TOKENS, D), 1.0, 6.0, ((0, 32),)),
        "cotangent": noise_with(streams_of[1], (TOKENS, D), 1.0, 6.0, ((0, 32),), (0, 1, 32, 2.75)),
        "item_lengths": draw_item_lengths(jax.random.fold_in(streams_of[13], 71), 0),
        "joint_weight": bell_draw(streams_of[3], (D, 3 * D), D ** -0.5, 0.25, ((0, 32),)),
        "output_weight": bell_draw(streams_of[4], (D, D), (D // 32) ** -0.5, 1.5, ((0, 32),)),
        "expand_weight": bell_draw(streams_of[5], (D, FF), D ** -0.5, 0.25, ((0, 32),)),
        "reduce_weight": bell_draw(streams_of[6], (FF, D), FF ** -0.5, 0.125, ((0, 32),)),
        "attn_gain": jnp.clip(1.0 + 0.18 * jax.random.normal(streams_of[7], (D,), jnp.float32), 0.099609375, 1.8984375).astype(jnp.bfloat16),
        "attn_shift": bell_draw(streams_of[8], (D,), 0.3, 3.0, ((0, 32),)),
        "ffn_gain": jnp.clip(1.0 + 0.18 * jax.random.normal(streams_of[9], (D,), jnp.float32), 0.099609375, 1.8984375).astype(jnp.bfloat16),
        "ffn_shift": bell_draw(streams_of[10], (D,), 0.3, 3.0, ((0, 32),)),
        "expand_bias": bell_draw(streams_of[11], (FF,), 0.5, 3.0, ((0, 32),)),
        "reduce_bias": bell_draw(streams_of[12], (D,), 0.2, 3.0, ((0, 32),)),
    }


LOG_TWO = math.log(2.0)
NEGATIVE = -1e+30

@jax.custom_vjp
def low(v):
    return lax.optimization_barrier(v.astype(jnp.bfloat16)).astype(jnp.float32)

@jax.custom_vjp
def low_back(v):
    return v

def low_keep(v):
    return (low(v), None)

def low_pass(kept, grad):
    return (grad,)

def back_keep(v):
    return (v, None)

def back_low(kept, grad):
    return (low(grad),)
low.defvjp(low_keep, low_pass)
low_back.defvjp(back_keep, back_low)

def matmul(left, right):
    return jnp.dot(left, right, preferred_element_type=jnp.float32, precision=lax.Precision.HIGHEST)

def layer_norm(values, gain, shift):
    centre = values - lax.optimization_barrier(jnp.mean(values, axis=-1, keepdims=True))
    spread = lax.rsqrt(lax.optimization_barrier(jnp.mean(centre * centre, axis=-1, keepdims=True)) + 1e-05)
    return centre * spread * gain + shift

def token_ids(lengths, seq_len):
    padded = (lengths + BLOCK - 1) // BLOCK * BLOCK
    ends = jnp.cumsum(padded)
    starts = ends - padded
    position = jnp.arange(seq_len, dtype=jnp.int32)
    inside = (position[:, None] >= starts[None, :]) & (position[:, None] < (starts + lengths)[None, :])
    live = jnp.any(inside, axis=1)
    number = jnp.arange(lengths.shape[0], dtype=jnp.int32)
    item = lax.optimization_barrier(jnp.sum(jnp.where(inside, number[None, :], 0), axis=1))
    segment = jnp.where(live, item, -1 - position)
    return (live.astype(jnp.float32), segment.astype(jnp.int32))

def level_mask(segment, seq_len, level):
    factor = 2 ** level
    width = BLOCK * factor
    blocks = seq_len // width
    grouped = segment.reshape(seq_len // factor, factor)
    smallest = lax.optimization_barrier(jnp.min(grouped, axis=1))
    largest = lax.optimization_barrier(jnp.max(grouped, axis=1))
    absent = -3 * seq_len
    coarse_id = jnp.where(smallest == largest, smallest, absent).reshape(blocks, BLOCK)
    padded = jnp.pad(coarse_id, ((1, 1), (0, 0)), constant_values=absent)
    window = jnp.concatenate([padded[:-2], padded[1:-1], padded[2:]], axis=1)
    valid = window[:, None, :] == segment.reshape(blocks, width)[:, :, None]
    if level > 0:
        half = width // 2
        position = jnp.arange(seq_len, dtype=jnp.int32).reshape(blocks, width)
        lower = (position // half - 1) * half
        start = ((jnp.arange(blocks, dtype=jnp.int32)[:, None] - 1) * BLOCK + jnp.arange(3 * BLOCK, dtype=jnp.int32)[None, :]) * factor
        covered = (start[:, None, :] >= lower[:, :, None]) & (start[:, None, :] < lower[:, :, None] + 3 * half)
        valid = valid & jnp.logical_not(covered)
    return valid

def windows(coarse_values, blocks):
    heads, dim = (coarse_values.shape[1], coarse_values.shape[2])
    grouped = coarse_values.reshape(blocks, BLOCK, heads, dim)
    padded = jnp.pad(grouped, ((1, 1), (0, 0), (0, 0), (0, 0)))
    return jnp.concatenate([padded[:-2], padded[1:-1], padded[2:]], axis=1)

def from_rows(rows, blocks, width):
    return rows.reshape(blocks, width, -1).transpose(0, 2, 1)[..., None]

def attend(query, keys, values, segment):
    seq_len, heads, dim = query.shape
    factor_scale = dim ** (-0.5)
    scores = []
    value_windows = []
    flat_scores = []
    for level in range(LEVELS):
        factor = 2 ** level
        width = BLOCK * factor
        blocks = seq_len // width
        valid = level_mask(segment, seq_len, level)
        if level == 0:
            key_coarse, value_coarse = (keys, values)
        else:
            key_coarse = low(lax.optimization_barrier(jnp.mean(keys.reshape(seq_len // factor, factor, heads, dim), axis=1)))
            value_coarse = low(lax.optimization_barrier(jnp.mean(values.reshape(seq_len // factor, factor, heads, dim), axis=1)))
        raw = jnp.einsum('bwhd,bjhd->bhwj', query.reshape(blocks, width, heads, dim), windows(key_coarse, blocks), precision=lax.Precision.HIGHEST)
        score = low_back(raw * factor_scale + level * LOG_TWO)
        masked = jnp.where(valid[:, None], score, NEGATIVE)
        scores.append(masked)
        flat_scores.append(masked.transpose(0, 2, 1, 3).reshape(seq_len, heads, -1))
        value_windows.append(windows(value_coarse, blocks))
    log_total = jax.nn.logsumexp(jnp.concatenate(flat_scores, axis=-1), axis=-1)
    context = jnp.zeros((seq_len, heads, dim), jnp.float32)
    for level in range(LEVELS):
        width = BLOCK * 2 ** level
        blocks = seq_len // width
        weight = low(jnp.exp(scores[level] - from_rows(log_total, blocks, width)))
        part = jnp.einsum('bhwj,bjhd->bwhd', weight, value_windows[level], precision=lax.Precision.HIGHEST)
        context = context + part.reshape(seq_len, heads, dim)
    return context.reshape(seq_len, heads * dim)

def forward(values, weights, lengths):
    joint, output_w, expand, reduce_w, attn_gain, attn_shift, ffn_gain, ffn_shift, expand_bias, reduce_bias = weights
    seq_len = values.shape[0]
    live, segment = token_ids(lengths, seq_len)
    first_in = low(layer_norm(values, attn_gain, attn_shift))
    joint_out = low(low_back(matmul(first_in, joint)))
    query = joint_out[:, :D].reshape(seq_len, HEADS, D // HEADS)
    keys = joint_out[:, D:2 * D].reshape(seq_len, HEADS, D // HEADS)
    vals = joint_out[:, 2 * D:].reshape(seq_len, HEADS, D // HEADS)
    context = low(low_back(attend(query, keys, vals, segment)))
    hidden = values + low_back(matmul(context, output_w)) * live[:, None]
    second_in = low(layer_norm(hidden, ffn_gain, ffn_shift))
    expanded = low_back(matmul(second_in, expand) + expand_bias)
    activated = low(jax.nn.gelu(expanded, approximate=False))
    return hidden + low_back(matmul(activated, reduce_w) + reduce_bias) * live[:, None]

def reference(tokens, cotangent, item_lengths, joint_weight, output_weight, expand_weight, reduce_weight, attn_gain, attn_shift, ffn_gain, ffn_shift, expand_bias, reduce_bias):
    params = tuple((p.astype(jnp.float32) for p in (joint_weight, output_weight, expand_weight, reduce_weight, attn_gain, attn_shift, ffn_gain, ffn_shift, expand_bias, reduce_bias)))
    slot_tokens = tokens.reshape(DEVICES, TOK_DEV, D)
    slot_cot = cotangent.reshape(DEVICES, TOK_DEV, D)

    def one_slot(totals, inputs):
        slot_x, slot_c, lengths = inputs

        def run(values, weights):
            return forward(values, weights, lengths)
        outputs, pullback = jax.vjp(jax.checkpoint(run), slot_x.astype(jnp.float32), params)
        value_grad, weight_grads = pullback(slot_c.astype(jnp.float32))
        totals = tuple((a + b for a, b in zip(totals, weight_grads)))
        return (totals, (outputs.astype(jnp.bfloat16), value_grad.astype(jnp.bfloat16)))
    zeros = tuple((jnp.zeros_like(p) for p in params))
    totals, outs = lax.scan(one_slot, zeros, (slot_tokens, slot_cot, item_lengths))
    mixed = outs[0].reshape(TOKENS, D)
    token_grad = outs[1].reshape(TOKENS, D)
    return (mixed, token_grad, totals[0], totals[1], totals[2], totals[3], totals[4], totals[5], totals[6], totals[7], totals[8], totals[9])
```

```python
import functools
import math

import jax
import jax.numpy as jnp
import numpy as np
from jax import lax
from jax.experimental import pallas as pl
from jax.experimental.pallas import tpu as pltpu
from jax.sharding import PartitionSpec as P

HEADS = 8
BLOCK = 16
LEVELS = 7
TILE = 128
GROUPS = 2
LOG_TWO = math.log(2.0)
NEGATIVE = -1e30
ROOT_HALF = 1.0 / math.sqrt(2.0)
DENSITY = 1.0 / math.sqrt(2.0 * math.pi)
AXES = ("dp", "sub")
BF = jnp.bfloat16
F32 = jnp.float32
MIB = 1 << 20


class Level:
    def __init__(self, level, seq, base):
        self.level = level
        self.factor = 1 << level
        self.count = seq // self.factor
        self.width = BLOCK * self.factor
        self.blocks = seq // self.width
        self.pad = BLOCK if self.blocks > 2 else 0
        self.base = base
        self.rows = self.count + 2 * self.pad
        if self.width <= TILE:
            self.window = TILE // self.factor + 2 * BLOCK
        else:
            self.window = min(3, self.blocks) * BLOCK

    def first(self, tile):
        if self.width <= TILE:
            return tile * (TILE // self.factor)
        if self.blocks > 2:
            return (tile // (self.width // TILE)) * BLOCK
        return 0

    def row(self, tile):
        first = self.first(tile)
        return pl.multiple_of(self.base + first, BLOCK) if not isinstance(first, int) else self.base + first


def geometry(seq):
    levels, base = [], 0
    for level in range(LEVELS):
        levels.append(Level(level, seq, base))
        base += levels[-1].rows
    return levels, base, sum(v.window for v in levels)


def pooling(seq):
    levels, total, _ = geometry(seq)
    near = [v for v in levels[1:] if v.width <= TILE]
    far = [v for v in levels[1:] if v.width > TILE]
    near_rows = sum(TILE // v.factor for v in near)
    fine = np.zeros((near_rows, TILE), np.float32)
    row = 0
    for v in near:
        for j in range(TILE // v.factor):
            fine[row, j * v.factor : (j + 1) * v.factor] = 1.0 / v.factor
            row += 1
    far_base = far[0].base
    wide = np.zeros((total - far_base, seq), np.float32)
    for v in far:
        for j in range(v.count):
            wide[v.base - far_base + v.pad + j, j * v.factor : (j + 1) * v.factor] = 1.0 / v.factor
    spread = np.zeros((seq, near_rows + total - far_base), np.float32)
    for t in range(seq // TILE):
        spread[t * TILE : (t + 1) * TILE, :near_rows] = fine.T
    spread[:, near_rows:] = wide.T
    return near, far_base, fine, wide, spread


class Order:
    def __init__(self, devices):
        self.devices = devices
        self.bits = [1 << k for k in reversed(range(devices.bit_length() - 1))]
        self.stepped = devices == 32

    def flip(self, p):
        value = 0
        for k, bit in enumerate(self.bits):
            value = value + ((p >> k) & 1) * bit
        return value


def dot(left, right, contract=(1, 0)):
    return lax.dot_general(
        left, right, (((contract[0],), (contract[1],)), ((), ())), preferred_element_type=F32
    )


def iota(shape, axis):
    return lax.broadcasted_iota(jnp.int32, shape, axis)


def unpack_rows(order, me, source, columns, target, chunk):
    if not order.stepped:
        target[...] = source[:, columns]
        return
    for p in range(order.devices):
        row = pl.multiple_of((me ^ order.flip(p)) * chunk, chunk)
        target[pl.ds(row, chunk), :] = source[p * chunk : (p + 1) * chunk, columns]


def pack_rows(order, me, value, target, columns, chunk, scratch):
    if not order.stepped:
        target[:, columns] = value
        return
    scratch[...] = value
    for p in range(order.devices):
        row = pl.multiple_of((me ^ order.flip(p)) * chunk, chunk)
        target[p * chunk : (p + 1) * chunk, columns] = scratch[pl.ds(row, chunk), :]


def owners(order, me, shape):
    return me ^ order.flip(iota(shape, 0))


def spread_lanes(order, me, block, row, offset, chunk, total):
    n = order.devices
    step = block.shape[0] // n
    pick = (iota((n, block.shape[0]), 1) == iota((n, block.shape[0]), 0) * step + row).astype(BF)
    rows = dot(pick, block).astype(BF)
    lanes = block.shape[1]
    place = (iota((lanes, total), 0) == iota((lanes, total), 1) % chunk + offset).astype(BF)
    wide = dot(rows, place)
    mine = iota((n, total), 1) // chunk == owners(order, me, (n, total))
    return jnp.sum(jnp.where(mine, wide, 0.0), axis=0, keepdims=True)


def fold_lanes(order, me, vector, offset, chunk, lanes):
    n, total = order.devices, vector.shape[1]
    mine = iota((n, total), 1) // chunk == owners(order, me, (n, total))
    wide = jnp.where(mine, vector, 0.0).astype(BF)
    place = (iota((total, lanes), 1) == iota((total, lanes), 0) % chunk + offset).astype(BF)
    return dot(wide, place)


def place_rows(rows, row, step):
    n = rows.shape[0]
    pick = (iota((n * step, n), 0) == iota((n * step, n), 1) * step + row).astype(BF)
    return dot(pick, rows.astype(BF))


def live_column(lens, first, rows):
    position = first + iota((rows, 1), 0)
    start, live = 0, jnp.zeros((rows, 1), jnp.bool_)
    for i in range(lens.shape[1]):
        length = lens[0, i]
        live = live | ((position >= start) & (position < start + length))
        start = start + (length + BLOCK - 1) // BLOCK * BLOCK
    return live


def tile_bias(lens, tile, levels):
    position = tile * TILE + iota((1, TILE), 1)
    low, high, start = position, position + 1, 0
    for i in range(lens.shape[1]):
        length = lens[0, i]
        inside = (position >= start) & (position < start + length)
        low = jnp.where(inside, start, low)
        high = jnp.where(inside, start + length, high)
        start = start + (length + BLOCK - 1) // BLOCK * BLOCK
    parts = []
    for v in levels:
        begin = (v.first(tile) - v.pad + iota((v.window, TILE), 0)) * v.factor
        reach = (position // v.width - 1) * v.width
        valid = (begin >= low) & (begin + v.factor <= high) & (begin >= reach) & (begin < reach + 3 * v.width)
        if v.level > 0:
            half = v.width // 2
            lower = (position // half - 1) * half
            valid = valid & ~((begin >= lower) & (begin < lower + 3 * half))
        parts.append(jnp.where(valid, v.level * LOG_TWO, NEGATIVE))
    return jnp.concatenate(parts, axis=0)


def window_of(ref, tile, levels, lanes):
    return jnp.concatenate([ref[pl.ds(v.row(tile), v.window), lanes] for v in levels], axis=0)


def two_heads(rows):
    dim = rows.shape[1] // 2
    first = iota(rows.shape, 1) < dim
    zero = jnp.zeros_like(rows)
    return jnp.concatenate([jnp.where(first, rows, zero), jnp.where(first, zero, rows)], axis=0)


def own_heads(both):
    dim = both.shape[0] // 2
    return jnp.concatenate([both[:dim, :TILE], both[dim:, TILE:]], axis=0).T


def normalize(values):
    centre = values - jnp.mean(values, axis=-1, keepdims=True)
    scale = lax.rsqrt(jnp.mean(centre * centre, axis=-1, keepdims=True) + 1e-05)
    return centre * scale, scale


def norm_back(grad, normed, scale, gain):
    scaled = grad * gain
    return scale * (
        scaled
        - jnp.mean(scaled, axis=-1, keepdims=True)
        - normed * jnp.mean(scaled * normed, axis=-1, keepdims=True)
    )


def attend_kernel(
    order, seq, first_group, me_ref, lens_ref, x_ref, w_ref, vec_ref, fine_ref, wide_ref, *refs
):
    if first_group:
        p_ref, ctx_ref, q_ref, kx_ref, vx_ref, in_ref, w_scr = refs
    else:
        p_ref, ctx_ref, q_ref, kx_ref, vx_ref, w_scr = refs
    levels, total, _ = geometry(seq)
    near, far_base, *_ = pooling_shape(seq)
    tile = pl.program_id(0)
    lanes = q_ref.shape[1]
    me = me_ref[0]

    @pl.when(tile == 0)
    def _():
        unpack_rows(order, me, w_ref, slice(0, 3 * lanes), w_scr, w_ref.shape[0] // order.devices)
        if first_group:
            if order.stepped:
                chunk = x_ref.shape[1] // order.devices
                block = w_ref[:, 3 * lanes :]
                gain = spread_lanes(order, me, block, 0, 0, chunk, x_ref.shape[1])
                shift = spread_lanes(order, me, block, 0, chunk, chunk, x_ref.shape[1])
            else:
                gain, shift = vec_ref[0:1, :], vec_ref[1:2, :]
        kx_ref[...] = jnp.zeros_like(kx_ref)
        vx_ref[...] = jnp.zeros_like(vx_ref)
        step = 256
        for r in range(0, seq, step):
            if first_group:
                hat, _ = normalize(x_ref[r : r + step, :].astype(F32))
                first_in = (hat * gain + shift).astype(BF)
                in_ref[r : r + step, :] = first_in
            else:
                first_in = x_ref[r : r + step, :]
            joint = dot(first_in, w_scr[...]).astype(BF)
            q_ref[r : r + step, :] = joint[:, :lanes] * jnp.asarray(0.125, BF)
            pad = levels[0].pad
            kx_ref[pad + r : pad + r + step, :] = joint[:, lanes : 2 * lanes]
            vx_ref[pad + r : pad + r + step, :] = joint[:, 2 * lanes :]
        pad = levels[0].pad
        for ref in (kx_ref, vx_ref):
            for t in range(seq // TILE):
                rows = ref[pad + t * TILE : pad + (t + 1) * TILE, :]
                pooled = dot(fine_ref[...], rows).astype(BF)
                at = 0
                for v in near:
                    n = TILE // v.factor
                    ref[v.base + v.pad + t * n : v.base + v.pad + (t + 1) * n, :] = pooled[at : at + n]
                    at += n
            ref[far_base:total, :] = dot(wide_ref[...], ref[pad : pad + seq, :]).astype(BF)

    bias = tile_bias(lens_ref, tile, levels)
    bias = jnp.concatenate([bias, bias], axis=1)
    rows = pl.ds(pl.multiple_of(tile * TILE, TILE), TILE)
    for pair in range(lanes // TILE):
        cols = slice(pair * TILE, (pair + 1) * TILE)
        keys = window_of(kx_ref, tile, levels, cols)
        vals = window_of(vx_ref, tile, levels, cols)
        query = two_heads(q_ref[rows, cols])
        score = dot(keys, query, (1, 1)) + bias
        peak = jnp.max(score, axis=0, keepdims=True)
        weight = jnp.exp(score - peak)
        share = 1.0 / jnp.sum(weight, axis=0, keepdims=True)
        prob = (weight * share).astype(BF)
        p_ref[0, pair] = prob
        ctx_ref[:, cols] = own_heads(dot(vals, prob, (0, 0))).astype(BF)


def ffn_kernel(
    order,
    me_ref,
    lens_ref,
    x_ref,
    cot_ref,
    ctx0_ref,
    ctx1_ref,
    e_ref,
    r_ref,
    vec_ref,
    ebias_ref,
    mixed_ref,
    act_ref,
    eg_ref,
    in_ref,
    branch_ref,
    hg_ref,
    cg_ref,
    sums_ref,
    esum_ref,
    we_scr,
    wo_scr,
    wr_scr,
    vec_scr,
    eb_scr,
):
    tile = pl.program_id(0)
    me = me_ref[0]
    rows, d = x_ref.shape
    ff = we_scr.shape[1]
    half = ctx0_ref.shape[1]

    @pl.when(tile == 0)
    def _():
        chunk = d // order.devices
        unpack_rows(order, me, e_ref, slice(0, ff), we_scr, chunk)
        unpack_rows(order, me, e_ref, slice(ff, ff + d), wo_scr, chunk)
        unpack_rows(order, me, r_ref, slice(0, d), wr_scr, ff // order.devices)
        if order.stepped:
            block = e_ref[:, ff + d :]
            for k in range(3):
                vec_scr[k : k + 1, :] = spread_lanes(order, me, block, 0, k * chunk, chunk, d)
            eb_scr[...] = spread_lanes(order, me, block, 1, 0, ff // order.devices, ff)
        else:
            vec_scr[0:3, :] = vec_ref[2:5, :]
            eb_scr[...] = ebias_ref[...]
        sums_ref[...] = jnp.zeros_like(sums_ref)
        esum_ref[...] = jnp.zeros_like(esum_ref)

    gain, shift, rbias = vec_scr[0:1, :], vec_scr[1:2, :], vec_scr[2:3, :]
    live = live_column(lens_ref, tile * rows, rows).astype(F32)
    out = dot(ctx0_ref[...], wo_scr[:half, :]) + dot(ctx1_ref[...], wo_scr[half:, :])
    hidden = x_ref[...].astype(F32) + live * out
    hat, scale = normalize(hidden)
    second_in = (hat * gain + shift).astype(BF)
    in_ref[...] = second_in
    expanded = dot(second_in, we_scr[...]) + eb_scr[...]
    phi = 0.5 * (1.0 + lax.erf(expanded * ROOT_HALF))
    activated = (expanded * phi).astype(BF)
    act_ref[...] = activated
    slope = phi + expanded * (jnp.exp(-0.5 * expanded * expanded) * DENSITY)
    mixed_ref[...] = (hidden + live * (dot(activated, wr_scr[...]) + rbias)).astype(BF)
    cot = cot_ref[...].astype(F32)
    out_grad = (cot * live).astype(BF)
    expanded_grad = (dot(out_grad, wr_scr[...], (1, 1)) * slope).astype(BF)
    eg_ref[...] = expanded_grad
    second_grad = dot(expanded_grad, we_scr[...], (1, 1))
    sums_ref[0:1, :] += jnp.sum(second_grad * hat, axis=0, keepdims=True)
    sums_ref[1:2, :] += jnp.sum(second_grad, axis=0, keepdims=True)
    sums_ref[2:3, :] += jnp.sum(out_grad.astype(F32), axis=0, keepdims=True)
    esum_ref[...] += jnp.sum(expanded_grad.astype(F32), axis=0, keepdims=True)
    hidden_grad = cot + norm_back(second_grad, hat, scale, gain)
    hg_ref[...] = hidden_grad
    branch = (hidden_grad * live).astype(BF)
    branch_ref[...] = branch
    cg_ref[...] = dot(branch, wo_scr[...], (1, 1)).astype(BF)


def reduce_grad_kernel(order, me_ref, lens_ref, act_ref, cot_ref, out_ref, og_scr):
    step = pl.program_id(0)
    seq, d = cot_ref.shape
    cols = act_ref.shape[1]

    @pl.when(step == 0)
    def _():
        live = live_column(lens_ref, 0, seq).astype(F32)
        og_scr[...] = (cot_ref[...].astype(F32) * live).astype(BF)

    grad = dot(act_ref[...], og_scr[...], (0, 0)).astype(BF)
    chunk = out_ref.shape[0] // order.devices
    for k in range(cols // chunk):
        device = step * (cols // chunk) + k
        at = device
        if order.stepped:
            other, at = me_ref[0] ^ device, 0
            for b, bit in enumerate(order.bits):
                at = at + ((other // bit) & 1) * (1 << b)
        out_ref[pl.ds(pl.multiple_of(at * chunk, chunk), chunk), :] = grad[k * chunk : (k + 1) * chunk]


def expand_grad_kernel(
    order,
    me_ref,
    in_ref,
    eg_ref,
    ctx0_ref,
    ctx1_ref,
    branch_ref,
    sums_ref,
    esum_ref,
    e_ref,
    o_ref,
    scr_e,
    in_scr,
):
    step = pl.program_id(0)
    d = in_ref.shape[1]
    me = me_ref[0]
    chunk = d // order.devices

    @pl.when(step == 0)
    def _():
        in_scr[...] = in_ref[...].T
        both = jnp.concatenate([ctx0_ref[...], ctx1_ref[...]], axis=1)
        out = dot(both, branch_ref[...], (0, 0)).astype(BF)
        pack_rows(order, me, out, o_ref, slice(0, d), chunk, scr_e)
        if order.stepped:
            lanes = o_ref.shape[1] - d
            rows = jnp.zeros((order.devices, lanes), F32)
            for k in range(3):
                rows += fold_lanes(order, me, sums_ref[k : k + 1, :], k * chunk, chunk, lanes)
            ff = esum_ref.shape[1]
            more = fold_lanes(order, me, esum_ref[...], 0, ff // order.devices, lanes)
            o_ref[:, d:] = (place_rows(rows, 0, chunk) + place_rows(more, 1, chunk)).astype(BF)

    grad = dot(in_scr[...], eg_ref[...]).astype(BF)
    pack_rows(order, me, grad, e_ref, slice(None), chunk, scr_e)


def attend_back_kernel(
    order,
    seq,
    last,
    me_ref,
    p_ref,
    q_ref,
    cg_ref,
    kx_ref,
    vx_ref,
    in_ref,
    w_ref,
    spread_ref,
    *refs,
):
    if last:
        x_ref, fig0_ref, hg_ref, w0_ref, vec_ref, j_ref, tg_ref, sums_ref = refs[:8]
        dk_scr, dv_scr, dj_scr, w_scr, j_scr = refs[8:]
    else:
        j_ref, fig_ref = refs[:2]
        dk_scr, dv_scr, dj_scr, w_scr, j_scr = refs[2:]
    levels, total, _ = geometry(seq)
    near, far_base, *_ = pooling_shape(seq)
    tile = pl.program_id(0)
    lanes = q_ref.shape[1]
    me = me_ref[0]

    @pl.when(tile == 0)
    def _():
        dk_scr[...] = jnp.zeros_like(dk_scr)
        dv_scr[...] = jnp.zeros_like(dv_scr)
        unpack_rows(order, me, w_ref, slice(0, 3 * lanes), w_scr, w_ref.shape[0] // order.devices)

    rows = pl.ds(pl.multiple_of(tile * TILE, TILE), TILE)
    for pair in range(lanes // TILE):
        cols = slice(pair * TILE, (pair + 1) * TILE)
        keys = window_of(kx_ref, tile, levels, cols)
        vals = window_of(vx_ref, tile, levels, cols)
        query = two_heads(q_ref[:, cols])
        grad = two_heads(cg_ref[:, cols])
        prob = p_ref[0, pair]
        wide = prob.astype(F32)
        prob_grad = dot(vals, grad, (1, 1))
        inner = jnp.sum(wide * prob_grad, axis=0, keepdims=True)
        score_grad = (wide * (prob_grad - inner)).astype(BF)
        key_grad = dot(score_grad, query)
        val_grad = dot(prob, grad)
        dj_scr[rows, cols] = (own_heads(dot(keys, score_grad, (0, 0))) * 0.125).astype(BF)
        at = 0
        for v in levels:
            span = pl.ds(v.row(tile), v.window)
            dk_scr[span, cols] += key_grad[at : at + v.window]
            dv_scr[span, cols] += val_grad[at : at + v.window]
            at += v.window

    @pl.when(tile == pl.num_programs(0) - 1)
    def _():
        pad = levels[0].pad
        for ref, at in ((dk_scr, lanes), (dv_scr, 2 * lanes)):
            far = ref[far_base:total, :].astype(BF)
            for t in range(seq // TILE):
                parts = []
                for v in near:
                    n = TILE // v.factor
                    base = v.base + v.pad + t * n
                    parts.append(ref[base : base + n, :].astype(BF))
                parts.append(far)
                spread = dot(spread_ref[t * TILE : (t + 1) * TILE, :], jnp.concatenate(parts, axis=0))
                whole = ref[pad + t * TILE : pad + (t + 1) * TILE, :] + spread
                dj_scr[t * TILE : (t + 1) * TILE, at : at + lanes] = whole.astype(BF)
        joint = dot(in_ref[...], dj_scr[...], (0, 0)).astype(BF)
        chunk = joint.shape[0] // order.devices
        pack_rows(order, me, joint, j_ref, slice(0, 3 * lanes), chunk, j_scr)
        step = 256
        d = in_ref.shape[1]
        if last:
            if order.stepped:
                gain = spread_lanes(order, me, w0_ref[:, 3 * lanes :], 0, 0, chunk, d)
            else:
                gain = vec_ref[0:1, :]
            gains = jnp.zeros((1, d), F32)
            shifts = jnp.zeros((1, d), F32)
        for r in range(0, seq, step):
            fig = dot(dj_scr[r : r + step, :], w_scr[...], (1, 1))
            if not last:
                fig_ref[r : r + step, :] = fig
                continue
            fig = fig + fig0_ref[r : r + step, :]
            hat, scale = normalize(x_ref[r : r + step, :].astype(F32))
            gains += jnp.sum(fig * hat, axis=0, keepdims=True)
            shifts += jnp.sum(fig, axis=0, keepdims=True)
            grad = hg_ref[r : r + step, :] + norm_back(fig, hat, scale, gain)
            tg_ref[r : r + step, :] = grad.astype(BF)
        if last:
            sums_ref[0:1, :] = gains
            sums_ref[1:2, :] = shifts
            if order.stepped:
                extra = j_ref.shape[1] - 3 * lanes
                folded = fold_lanes(order, me, gains, 0, chunk, extra)
                folded += fold_lanes(order, me, shifts, chunk, chunk, extra)
                j_ref[:, 3 * lanes :] = place_rows(folded, 0, chunk).astype(BF)


def pooling_shape(seq):
    levels, total, _ = geometry(seq)
    near = [v for v in levels[1:] if v.width <= TILE]
    far = [v for v in levels[1:] if v.width > TILE]
    return near, far[0].base, total


def whole(shape):
    return pl.BlockSpec(shape, lambda i: (0,) * len(shape))


def smem():
    return pl.BlockSpec(memory_space=pltpu.SMEM)


def params(mib=56):
    return pltpu.CompilerParams(dimension_semantics=("arbitrary",), vmem_limit_bytes=mib * MIB)


def shape_of(shape, dtype):
    return jax.ShapeDtypeStruct(shape, dtype)


def attend(order, me, lens, x, w, vec, first_group):
    seq, d = x.shape
    lanes = d // GROUPS
    levels, total, window = geometry(seq)
    _, _, fine, wide, _ = pooling(seq)
    tiles = seq // TILE
    pairs = lanes // TILE
    outs = [
        (shape_of((tiles, pairs, window, 2 * TILE), BF), pl.BlockSpec((1, pairs, window, 2 * TILE), lambda i: (i, 0, 0, 0))),
        (shape_of((seq, lanes), BF), pl.BlockSpec((TILE, lanes), lambda i: (i, 0))),
        (shape_of((seq, lanes), BF), whole((seq, lanes))),
        (shape_of((total, lanes), BF), whole((total, lanes))),
        (shape_of((total, lanes), BF), whole((total, lanes))),
    ]
    if first_group:
        outs.append((shape_of((seq, d), BF), whole((seq, d))))
    return pl.pallas_call(
        functools.partial(attend_kernel, order, seq, first_group),
        grid=(tiles,),
        in_specs=[smem(), smem(), whole(x.shape), whole(w.shape), whole(vec.shape), whole(fine.shape), whole(wide.shape)],
        out_specs=[s for _, s in outs],
        out_shape=[o for o, _ in outs],
        scratch_shapes=[pltpu.VMEM((d, 3 * lanes), BF)],
        compiler_params=params(),
        cost_estimate=pl.CostEstimate(flops=4 * 10**9, bytes_accessed=10 * 10**6, transcendentals=2 * 10**6),
        name="attend",
    )(me, lens, x, w, vec, jnp.asarray(fine, BF), jnp.asarray(wide, BF))


def feed_forward(order, me, lens, x, cot, ctx0, ctx1, e, r, vec, ebias):
    seq, d = x.shape
    ff = r.shape[0]
    rows = 256

    def tiled(width):
        return pl.BlockSpec((rows, width), lambda i: (i, 0))

    outs = [
        (shape_of((seq, d), BF), tiled(d)),
        (shape_of((seq, ff), BF), tiled(ff)),
        (shape_of((seq, ff), BF), tiled(ff)),
        (shape_of((seq, d), BF), tiled(d)),
        (shape_of((seq, d), BF), tiled(d)),
        (shape_of((seq, d), F32), tiled(d)),
        (shape_of((seq, d), BF), tiled(d)),
        (shape_of((8, d), F32), whole((8, d))),
        (shape_of((1, ff), F32), whole((1, ff))),
    ]
    return pl.pallas_call(
        functools.partial(ffn_kernel, order),
        grid=(seq // rows,),
        in_specs=[
            smem(),
            smem(),
            tiled(d),
            tiled(d),
            tiled(ctx0.shape[1]),
            tiled(ctx1.shape[1]),
            whole(e.shape),
            whole(r.shape),
            whole(vec.shape),
            whole(ebias.shape),
        ],
        out_specs=[s for _, s in outs],
        out_shape=[o for o, _ in outs],
        scratch_shapes=[
            pltpu.VMEM((d, ff), BF),
            pltpu.VMEM((d, d), BF),
            pltpu.VMEM((ff, d), BF),
            pltpu.VMEM((8, d), F32),
            pltpu.VMEM((1, ff), F32),
        ],
        compiler_params=params(),
        cost_estimate=pl.CostEstimate(flops=10 * 10**9, bytes_accessed=20 * 10**6, transcendentals=4 * 10**6),
        name="ffn",
    )(me, lens, x, cot, ctx0, ctx1, e, r, vec, ebias)


def reduce_grads(order, me, lens, act, cot):
    seq, d = cot.shape
    ff = act.shape[1]
    cols = 256
    return pl.pallas_call(
        functools.partial(reduce_grad_kernel, order),
        grid=(ff // cols,),
        in_specs=[smem(), smem(), pl.BlockSpec((seq, cols), lambda i: (0, i)), whole((seq, d))],
        out_specs=whole((ff, d)),
        out_shape=shape_of((ff, d), BF),
        scratch_shapes=[pltpu.VMEM((seq, d), BF)],
        compiler_params=params(),
        cost_estimate=pl.CostEstimate(flops=2 * 10**9, bytes_accessed=8 * 10**6, transcendentals=0),
        name="reduce_grad",
    )(me, lens, act, cot)


def expand_grads(order, me, second_in, eg, ctx0, ctx1, branch, sums, esum):
    seq, d = second_in.shape
    ff = eg.shape[1]
    cols = 512
    extra = 128 if order.stepped else 0
    return pl.pallas_call(
        functools.partial(expand_grad_kernel, order),
        grid=(ff // cols,),
        in_specs=[
            smem(),
            whole((seq, d)),
            pl.BlockSpec((seq, cols), lambda i: (0, i)),
            whole(ctx0.shape),
            whole(ctx1.shape),
            whole(branch.shape),
            whole(sums.shape),
            whole(esum.shape),
        ],
        out_specs=[pl.BlockSpec((d, cols), lambda i: (0, i)), whole((d, d + extra))],
        out_shape=[shape_of((d, ff), BF), shape_of((d, d + extra), BF)],
        scratch_shapes=[pltpu.VMEM((d, cols), BF), pltpu.VMEM((d, seq), BF)],
        compiler_params=params(),
        cost_estimate=pl.CostEstimate(flops=3 * 10**9, bytes_accessed=10 * 10**6, transcendentals=0),
        name="expand_grad",
    )(me, second_in, eg, ctx0, ctx1, branch, sums, esum)


def attend_back(order, me, group, prob, q, cg, kx, vx, first_in, w, tail=None):
    seq, d = first_in.shape
    lanes = d // GROUPS
    levels, total, window = geometry(seq)
    spread = pooling(seq)[4]
    tiles, pairs = prob.shape[:2]
    last = tail is not None
    extra = 128 if order.stepped and last else 0
    ins = [
        (me, smem()),
        (prob, pl.BlockSpec((1, pairs, window, 2 * TILE), lambda i: (i, 0, 0, 0))),
        (q, pl.BlockSpec((TILE, lanes), lambda i: (i, 0))),
        (cg, pl.BlockSpec((TILE, lanes), lambda i: (i, group))),
        (kx, whole(kx.shape)),
        (vx, whole(vx.shape)),
        (first_in, whole(first_in.shape)),
        (w, whole(w.shape)),
        (jnp.asarray(spread, BF), whole(spread.shape)),
    ]
    outs = [(shape_of((d, 3 * lanes + extra), BF), whole((d, 3 * lanes + extra)))]
    if last:
        ins += [(a, whole(a.shape)) for a in tail]
        outs.append((shape_of((seq, d), BF), whole((seq, d))))
        outs.append((shape_of((8, d), F32), whole((8, d))))
    else:
        outs.append((shape_of((seq, d), F32), whole((seq, d))))
    return pl.pallas_call(
        functools.partial(attend_back_kernel, order, seq, last),
        grid=(tiles,),
        in_specs=[s for _, s in ins],
        out_specs=[s for _, s in outs],
        out_shape=[o for o, _ in outs],
        scratch_shapes=[
            pltpu.VMEM((total, lanes), F32),
            pltpu.VMEM((total, lanes), F32),
            pltpu.VMEM((seq, 3 * lanes), BF),
            pltpu.VMEM((d, 3 * lanes), BF),
            pltpu.VMEM((d, 3 * lanes), BF),
        ],
        compiler_params=params(),
        cost_estimate=pl.CostEstimate(flops=6 * 10**9, bytes_accessed=15 * 10**6, transcendentals=0),
        name="attend_back",
    )(*[a for a, _ in ins])


def swap(order, value, bit):
    return lax.ppermute(value, AXES, [(i, i ^ bit) for i in range(order.devices)])


def gather_rows(order, value):
    if not order.stepped:
        return lax.all_gather(value, AXES, axis=0, tiled=True)
    for bit in order.bits:
        value = jnp.concatenate([value, swap(order, value, bit)], axis=0)
    return value


def scatter_sum(order, value):
    if not order.stepped:
        return lax.psum_scatter(value.astype(F32), AXES, scatter_dimension=0, tiled=True)
    for bit in reversed(order.bits):
        half = value.shape[0] // 2
        other = swap(order, value[half:], bit)
        value = value[:half].astype(F32) + other.astype(F32)
        if bit != order.bits[0]:
            value = value.astype(BF)
    return value


def local(order, me, gather, scatter, tokens, cotangent, lens, joint, output_w, expand, reduce_w,
          attn_gain, attn_shift, ffn_gain, ffn_shift, expand_bias, reduce_bias):
    seq, d = tokens.shape
    lanes = d // GROUPS
    rows = joint.shape[0]
    ff = expand.shape[1]

    def group_columns(g):
        return [joint[:, k * d + g * lanes : k * d + (g + 1) * lanes] for k in range(3)]

    def as_rows(vectors):
        flat = jnp.concatenate(vectors)
        return jnp.pad(flat, (0, 128 - flat.shape[0]))[None]

    if order.stepped:
        blank = jnp.zeros((rows - 1, 128), BF)
        vec_a = jnp.concatenate([as_rows([attn_gain, attn_shift]), blank], axis=0)
        vec_e = jnp.concatenate(
            [as_rows([ffn_gain, ffn_shift, reduce_bias]), as_rows([expand_bias]), blank[1:]], axis=0
        )
        w0 = gather(jnp.concatenate(group_columns(0) + [vec_a], axis=1))
        w1 = gather(jnp.concatenate(group_columns(1), axis=1))
        e = gather(jnp.concatenate([expand, output_w, vec_e], axis=1))
        r = gather(reduce_w)
        vec = jnp.zeros((8, d), F32)
        ebias = jnp.zeros((1, ff), F32)
    else:
        w0 = gather(jnp.concatenate(group_columns(0), axis=1))
        w1 = gather(jnp.concatenate(group_columns(1), axis=1))
        e = gather(jnp.concatenate([expand, output_w], axis=1))
        r = gather(reduce_w)
        small = [gather(v) for v in (attn_gain, attn_shift, ffn_gain, ffn_shift, reduce_bias)]
        vec = jnp.pad(jnp.stack(small), ((0, 3), (0, 0))).astype(F32)
        ebias = gather(expand_bias)[None].astype(F32)

    p0, ctx0, q0, kx0, vx0, first_in = attend(order, me, lens, tokens, w0, vec, True)
    p1, ctx1, q1, kx1, vx1 = attend(order, me, lens, first_in, w1, vec, False)
    mixed, act, eg, second_in, branch, hg, cg, sums, esum = feed_forward(
        order, me, lens, tokens, cotangent, ctx0, ctx1, e, r, vec, ebias
    )
    rg = reduce_grads(order, me, lens, act, cotangent)
    eg_out, og_out = expand_grads(order, me, second_in, eg, ctx0, ctx1, branch, sums, esum)
    j0, fig0 = attend_back(order, me, 0, p0, q0, cg, kx0, vx0, first_in, w0)
    j1, token_grad, tail_sums = attend_back(
        order, me, 1, p1, q1, cg, kx1, vx1, first_in, w1, (tokens, fig0, hg, w0, vec)
    )
    reduce_grad = scatter(rg)
    expand_out = scatter(jnp.concatenate([eg_out, og_out], axis=1))
    j0 = scatter(j0)
    j1 = scatter(j1)
    parts = []
    for k in range(3):
        parts += [j0[:, k * lanes : (k + 1) * lanes], j1[:, k * lanes : (k + 1) * lanes]]
    joint_grad = jnp.concatenate(parts, axis=1)
    expand_grad = expand_out[:, :ff]
    output_grad = expand_out[:, ff : ff + d]
    if order.stepped:
        tail = j1[0, 3 * lanes :]
        body = expand_out[0, ff + d :]
        small = [tail[:rows], tail[rows : 2 * rows]]
        small += [body[k * rows : (k + 1) * rows] for k in range(3)]
        small.insert(4, expand_out[1, ff + d : ff + d + ff // order.devices])
    else:
        small = [scatter(tail_sums[0]), scatter(tail_sums[1])]
        small += [scatter(sums[0]), scatter(sums[1]), scatter(esum[0]), scatter(sums[2])]
    return (mixed, token_grad, joint_grad, output_grad, expand_grad, reduce_grad, *small)


def shards(order, *args):
    sub = lax.axis_size("sub")
    me = (lax.axis_index("dp") * sub + lax.axis_index("sub")).astype(jnp.int32).reshape(1)
    return local(
        order,
        me,
        functools.partial(gather_rows, order),
        functools.partial(scatter_sum, order),
        *args,
    )


def solution(mesh):
    order = Order(math.prod(mesh.shape[a] for a in AXES))
    wide = P(AXES, None)
    flat = P(AXES)
    return jax.shard_map(
        functools.partial(shards, order),
        mesh=mesh,
        in_specs=(wide,) * 7 + (flat,) * 6,
        out_specs=(wide,) * 6 + (flat,) * 6,
        check_vma=False,
    )
```

```python
import functools
import math

import jax
import jax.numpy as jnp
import numpy as np
from jax import lax
from jax.experimental import pallas as pl
from jax.experimental.pallas import tpu as pltpu
from jax.sharding import PartitionSpec as P

HEADS = 8
BLOCK = 16
LEVELS = 7
TILE = 64
POOL = 128
GROUPS = 2
DIM = 64
STEP = 8
LOG_TWO = math.log(2.0)
NEGATIVE = -1e30
ROOT_HALF = 1.0 / math.sqrt(2.0)
DENSITY = 1.0 / math.sqrt(2.0 * math.pi)
AXES = ("dp", "sub")
BF = jnp.bfloat16
F32 = jnp.float32
MIB = 1 << 20


class Level:
    def __init__(self, level, seq, base):
        self.level = level
        self.factor = 1 << level
        self.count = seq // self.factor
        self.width = BLOCK * self.factor
        self.blocks = seq // self.width
        self.pad = BLOCK if self.blocks > 2 else 0
        self.base = base
        self.rows = self.count + 2 * self.pad

    def pieces(self, tile):
        if self.width < TILE:
            return [(tile * (TILE // self.factor), TILE // self.factor + 2 * BLOCK)]
        block = tile // (self.width // TILE)
        if self.blocks > 2:
            return [(block * BLOCK, BLOCK), ((block + 2) * BLOCK, BLOCK)]
        return [((self.blocks - 1 - block) * BLOCK, BLOCK)]

    def spans(self, tile):
        return [(pl.multiple_of(self.base + first, BLOCK), n) for first, n in self.pieces(tile)]


def geometry(seq):
    levels, base = [], 0
    for level in range(LEVELS):
        levels.append(Level(level, seq, base))
        base += levels[-1].rows
    return levels, base, sum(n for v in levels for _, n in v.pieces(0))


def split_levels(seq):
    levels, _, _ = geometry(seq)
    near = [v for v in levels[1:] if v.width <= POOL]
    far = [v for v in levels[1:] if v.width > POOL]
    return near, far, far[0].base


def spreading(seq):
    levels, total, _ = geometry(seq)
    near, far, far_base = split_levels(seq)
    near_rows = sum(POOL // v.factor for v in near)
    spread = np.zeros((seq, near_rows + total - far_base), np.float32)
    at = 0
    for v in near:
        for t in range(seq):
            spread[t, at + t % POOL // v.factor] = 1.0 / v.factor
        at += POOL // v.factor
    for v in far:
        for t in range(seq):
            spread[t, near_rows + v.base - far_base + v.pad + t // v.factor] = 1.0 / v.factor
    return spread


class Order:
    def __init__(self, devices, turned=False):
        self.devices = devices
        self.bits = [1 << k for k in reversed(range(devices.bit_length() - 1))]
        self.stepped = devices == 32
        if not turned:
            self.turned = Order(devices, True)
        elif self.stepped:
            self.bits[-3:-1] = self.bits[-2], self.bits[-3]

    def flip(self, p):
        value = 0
        for k, bit in enumerate(self.bits):
            value = value + ((p >> k) & 1) * bit
        return value


def dot(left, right, contract=(1, 0)):
    return lax.dot_general(
        left, right, (((contract[0],), (contract[1],)), ((), ())), preferred_element_type=F32
    )


def iota(shape, axis):
    return lax.broadcasted_iota(jnp.int32, shape, axis)


def unpack_rows(order, me, halves, columns, target, chunk, places=slice(None)):
    rows = halves[0].shape[0]
    if not order.stepped:
        target[:rows, places] = halves[0][:, columns]
        target[rows:, places] = halves[1][:, columns]
        return
    for p in range(order.devices):
        half, at = divmod(p * chunk, rows)
        row = pl.multiple_of((me ^ order.flip(p)) * chunk, chunk)
        target[pl.ds(row, chunk), places] = halves[half][at : at + chunk, columns]


def pack_rows(order, me, source, halves, columns, chunk):
    rows = halves[0].shape[0]
    if not order.stepped:
        halves[0][:, columns] = source[:rows]
        halves[1][:, columns] = source[rows:]
        return
    for p in range(order.devices):
        half, at = divmod(p * chunk, rows)
        row = pl.multiple_of((me ^ order.flip(p)) * chunk, chunk)
        halves[half][at : at + chunk, columns] = source[pl.ds(row, chunk), :]


def owners(order, me, shape):
    return me ^ order.flip(iota(shape, 0))


def spread_lanes(order, me, halves, columns, row, offset, chunk, total):
    n = order.devices
    block = jnp.concatenate([half[:, columns] for half in halves], axis=0)
    step = block.shape[0] // n
    pick = (iota((n, block.shape[0]), 1) == iota((n, block.shape[0]), 0) * step + row).astype(BF)
    rows = dot(pick, block).astype(BF)
    lanes = block.shape[1]
    place = (iota((lanes, total), 0) == iota((lanes, total), 1) % chunk + offset).astype(BF)
    wide = dot(rows, place)
    mine = iota((n, total), 1) // chunk == owners(order, me, (n, total))
    return jnp.sum(jnp.where(mine, wide, 0.0), axis=0, keepdims=True)


def fold_lanes(order, me, vector, offset, chunk, lanes):
    n, total = order.devices, vector.shape[1]
    mine = iota((n, total), 1) // chunk == owners(order, me, (n, total))
    wide = jnp.where(mine, vector, 0.0).astype(BF)
    place = (iota((total, lanes), 1) == iota((total, lanes), 0) % chunk + offset).astype(BF)
    return dot(wide, place)


def place_rows(rows, row, step):
    n = rows.shape[0]
    pick = (iota((n * step, n), 0) == iota((n * step, n), 1) * step + row).astype(BF)
    return dot(pick, rows.astype(BF))


def live_column(lens, first, rows):
    position = first + iota((rows, 1), 0)
    start, live = 0, jnp.zeros((rows, 1), jnp.bool_)
    for i in range(lens.shape[1]):
        length = lens[0, i]
        live = live | ((position >= start) & (position < start + length))
        start = start + (length + BLOCK - 1) // BLOCK * BLOCK
    return live


def tile_bias(lens, tile, levels, copies):
    position = tile * TILE + iota((1, copies * TILE), 1) % TILE
    low, high, start = position, position + 1, 0
    for i in range(lens.shape[1]):
        length = lens[0, i]
        inside = (position >= start) & (position < start + length)
        low = jnp.where(inside, start, low)
        high = jnp.where(inside, start + length, high)
        start = start + (length + BLOCK - 1) // BLOCK * BLOCK
    parts = []
    for v in levels:
        reach = (position // v.width - 1) * v.width
        least = jnp.maximum(low, reach)
        most = jnp.minimum(high - v.factor, reach + 3 * v.width - 1)
        half = v.width // 2
        lower = (position // half - 1) * half
        for first, rows in v.pieces(tile):
            begin = (first - v.pad + iota((rows, copies * TILE), 0)) * v.factor
            valid = (begin >= least) & (begin <= most)
            if v.level > 0:
                valid = valid & ((begin < lower) | (begin >= lower + 3 * half))
            parts.append(jnp.where(valid, v.level * LOG_TWO, NEGATIVE))
    return jnp.concatenate(parts, axis=0)


def window_of(ref, tile, levels):
    return jnp.concatenate([ref[pl.ds(at, n), :] for v in levels for at, n in v.spans(tile)], axis=0)


def split_heads(rows):
    head = iota(rows.shape, 1) // DIM
    zero = jnp.zeros_like(rows)
    return jnp.concatenate([jnp.where(head == h, rows, zero) for h in range(rows.shape[1] // DIM)], axis=0)


def own_heads(full):
    heads = full.shape[1] // DIM
    head = iota((TILE, full.shape[1]), 1) // DIM
    own = full[:TILE]
    for h in range(1, heads):
        own = jnp.where(head == h, full[h * TILE : (h + 1) * TILE], own)
    return own


def normalize(values):
    centre = values - jnp.mean(values, axis=-1, keepdims=True)
    scale = lax.rsqrt(jnp.mean(centre * centre, axis=-1, keepdims=True) + 1e-05)
    return centre * scale, scale


def norm_back(grad, normed, scale, gain):
    scaled = grad * gain
    return scale * (
        scaled
        - jnp.mean(scaled, axis=-1, keepdims=True)
        - normed * jnp.mean(scaled * normed, axis=-1, keepdims=True)
    )


def prepare_kernel(seq, lens_ref, bias_ref):
    levels, _, _ = geometry(seq)
    step = pl.program_id(0)
    for t in range(STEP):
        bias_ref[t] = tile_bias(lens_ref, step * STEP + t, levels, bias_ref.shape[2] // TILE)


def means(seq, fine_ref, wide_ref):
    near, far, far_base = split_levels(seq)
    at = 0
    for v in near:
        n = POOL // v.factor
        same = iota((n, POOL), 1) // v.factor == iota((n, POOL), 0)
        fine_ref[at : at + n, :] = jnp.where(same, 1.0 / v.factor, 0.0).astype(BF)
        at += n
    for v in far:
        same = iota((v.rows, seq), 1) // v.factor == iota((v.rows, seq), 0) - v.pad
        base = v.base - far_base
        wide_ref[base : base + v.rows, :] = jnp.where(same, 1.0 / v.factor, 0.0).astype(BF)


def attend_kernel(order, seq, group, me_ref, bias_ref, x_ref, *refs):
    first_group = group == 0
    if first_group:
        lo_ref, hi_ref, vec_ref = refs[:3]
        p_ref, ctx_ref, q_ref, kx_ref, vx_ref, in_ref, w_ref, gain_ref = refs[3:11]
        fine_ref, wide_ref, x_scr, sem = refs[11:]
    else:
        w_ref, p_ref, ctx_ref, q_ref, kx_ref, vx_ref, fine_ref, wide_ref = refs
    levels, total, _ = geometry(seq)
    near, _, far_base = split_levels(seq)
    tile = pl.program_id(0)
    lanes = q_ref.shape[1]
    me = me_ref[0]

    @pl.when(tile == 0)
    def _():
        d = x_ref.shape[1]
        if first_group:
            copy = pltpu.make_async_copy(x_ref, x_scr, sem)
            copy.start()
        means(seq, fine_ref, wide_ref)
        if first_group:
            chunk = d // order.devices
            unpack_rows(order, me, (lo_ref, hi_ref), slice(0, 3 * d), w_ref, chunk)
            if order.stepped:
                tail = slice(3 * d, 3 * d + 128)
                gain = spread_lanes(order, me, (lo_ref, hi_ref), tail, 0, 0, chunk, d)
                shift = spread_lanes(order, me, (lo_ref, hi_ref), tail, 0, chunk, chunk, d)
            else:
                gain, shift = vec_ref[0:1, :], vec_ref[1:2, :]
            gain_ref[...] = jnp.broadcast_to(gain, gain_ref.shape)
            copy.wait()
        kx_ref[...] = jnp.zeros_like(kx_ref)
        vx_ref[...] = jnp.zeros_like(vx_ref)
        step = 256
        pad = levels[0].pad
        for r in range(0, seq, step):
            if first_group:
                hat, _ = normalize(x_scr[r : r + step, :].astype(F32))
                first_in = (hat * gain + shift).astype(BF)
                in_ref[r : r + step, :] = first_in
            else:
                first_in = x_ref[r : r + step, :]
            query, keys, vals = [
                dot(first_in, w_ref[:, k * d + group * lanes : k * d + (group + 1) * lanes]).astype(BF)
                for k in range(3)
            ]
            q_ref[r : r + step, :] = query * jnp.asarray(0.125, BF)
            kx_ref[pad + r : pad + r + step, :] = keys
            vx_ref[pad + r : pad + r + step, :] = vals
        for ref in (kx_ref, vx_ref):
            for t in range(seq // POOL):
                rows = ref[pad + t * POOL : pad + (t + 1) * POOL, :]
                pooled = dot(fine_ref[...], rows).astype(BF)
                at = 0
                for v in near:
                    n = POOL // v.factor
                    ref[v.base + v.pad + t * n : v.base + v.pad + (t + 1) * n, :] = pooled[at : at + n]
                    at += n
            ref[far_base:total, :] = dot(wide_ref[...], ref[pad : pad + seq, :]).astype(BF)

    tiles = range(STEP)
    scores = []
    for t in tiles:
        at = tile * STEP + t
        query = split_heads(q_ref[pl.ds(pl.multiple_of(at * TILE, TILE), TILE), :])
        scores.append(dot(window_of(kx_ref, at, levels), query, (1, 1)))
    probs = []
    for t in tiles:
        bias = jnp.concatenate([bias_ref[t]] * (scores[t].shape[1] // bias_ref.shape[2]), axis=1)
        score = scores[t] + bias
        peak = jnp.max(score, axis=0, keepdims=True)
        weight = jnp.exp(score - peak)
        share = 1.0 / jnp.sum(weight, axis=0, keepdims=True)
        probs.append((weight * share).astype(BF))
        p_ref[t] = probs[t]
    for t in tiles:
        context = dot(probs[t], window_of(vx_ref, tile * STEP + t, levels), (0, 0))
        ctx_ref[t * TILE : (t + 1) * TILE, :] = own_heads(context).astype(BF)


def ffn_block(rows, in_ref, og_ref, act_scr, eg_scr, mix_ref, sg_ref, we, wr, bias, before, behind):
    for r in range(0, in_ref.shape[0], rows):
        part = slice(r, r + rows)
        before(part)
        expanded = dot(in_ref[part, :], we[...]) + bias
        phi = 0.5 * (1.0 + lax.erf(expanded * ROOT_HALF))
        activated = (expanded * phi).astype(BF)
        act_scr[part, :] = activated
        slope = phi + expanded * (jnp.exp(-0.5 * expanded * expanded) * DENSITY)
        expanded_grad = (dot(og_ref[part, :], wr[...], (1, 1)) * slope).astype(BF)
        eg_scr[part, :] = expanded_grad
        mix_ref[part, :] += dot(activated, wr[...])
        sg_ref[part, :] += dot(expanded_grad, we[...], (1, 1))
        behind(part)


def ffn_kernel(order, part, me_ref, lens_ref, *refs):
    first = part == 0
    if first:
        x_ref, cot_ref, ctx0_ref, ctx1_ref, lo1_ref, hi1_ref, vec_ref, ebias_ref = refs[:8]
        hidden_ref, in_ref, og_ref, mix_ref, sg_ref, esum_ref, lo_ref, hi_ref = refs[8:16]
        own = (lo1_ref, hi1_ref)
        we_scr, wr_scr, wo_scr, eb_scr, in_scr, act_scr, eg_scr, grad_scr, vec_scr = refs[16:]
    else:
        cot_ref, hidden_ref, in_ref, og_ref, _, _, esum0_ref, ctx0_ref, ctx1_ref = refs[:9]
        lo1_ref, hi1_ref, lo2_ref, hi2_ref, vec_ref, ebias_ref = refs[9:15]
        mixed_ref, hg_ref, cg_ref, lo_ref, hi_ref, olo_ref, ohi_ref, sums_ref, esum_ref, mix_ref, sg_ref = refs[15:26]
        own = (lo2_ref, hi2_ref)
        we_scr, wr_scr, wo_scr, eb_scr, in_scr, act_scr, eg_scr, grad_scr, vec_scr, branch_scr, mixed_scr, sem = refs[26:]
    step = pl.program_id(0)
    me = me_ref[0]
    seq, d = cot_ref.shape
    rows = 512
    chunk = d // order.devices
    wide = 2 * d
    shared = (lo1_ref, hi1_ref)
    turned = order.turned
    half = ctx0_ref.shape[1]
    tail = slice(5 * d, 5 * d + 128)

    def bias_of(block, at):
        if order.stepped:
            return spread_lanes(order, me, shared, tail, 1, block * chunk, chunk, d)
        return ebias_ref[:, at : at + d]

    @pl.when(step == 0)
    def _():
        unpack_rows(order, me, own, slice(0, wide), we_scr, chunk)
        unpack_rows(order, me, own, slice(wide, 2 * wide), wr_scr, chunk)
        unpack_rows(order, me, shared, slice(2 * wide, 2 * wide + d), wo_scr, chunk)
        for k in range(2):
            block = 2 * part + k
            eb_scr[:, k * d : (k + 1) * d] = bias_of(block, block * d)
        if first:
            if order.stepped:
                gain = spread_lanes(order, me, shared, tail, 0, 0, chunk, d)
                shift = spread_lanes(order, me, shared, tail, 0, chunk, chunk, d)
            else:
                gain, shift = vec_ref[2:3, :], vec_ref[3:4, :]
            vec_scr[0:1, :] = gain
            vec_scr[1:2, :] = shift
            mix_ref[...] = jnp.zeros_like(mix_ref)
            sg_ref[...] = jnp.zeros_like(sg_ref)
        else:
            in_scr[...] = in_ref[...].T
            if order.stepped:
                vec_scr[0:1, :] = spread_lanes(order, me, shared, tail, 0, 0, chunk, d)
                vec_scr[1:2, :] = spread_lanes(order, me, shared, tail, 0, 2 * chunk, chunk, d)
            else:
                vec_scr[0:1, :] = vec_ref[2:3, :]
                vec_scr[1:2, :] = vec_ref[4:5, :]
            sums_ref[...] = jnp.zeros_like(sums_ref)

    def live_rows(span):
        return live_column(lens_ref, span.start, rows).astype(F32)

    def open_rows(span):
        live = live_rows(span)
        out = dot(ctx0_ref[span, :], wo_scr[:half, :]) + dot(ctx1_ref[span, :], wo_scr[half:, :])
        hidden = x_ref[span, :].astype(F32) + live * out
        hidden_ref[span, :] = hidden
        hat, _ = normalize(hidden)
        in_ref[span, :] = (hat * vec_scr[0:1, :] + vec_scr[1:2, :]).astype(BF)
        og_ref[span, :] = (cot_ref[span, :].astype(F32) * live).astype(BF)

    def close_rows(span):
        live = live_rows(span)
        hidden = hidden_ref[span, :]
        mixed_scr[span, :] = (hidden + live * (mix_ref[span, :] + vec_scr[1:2, :])).astype(BF)
        hat, scale = normalize(hidden)
        second_grad = sg_ref[span, :]
        sums_ref[0:1, :] += jnp.sum(second_grad * hat, axis=0, keepdims=True)
        sums_ref[1:2, :] += jnp.sum(second_grad, axis=0, keepdims=True)
        sums_ref[2:3, :] += jnp.sum(og_ref[span, :].astype(F32), axis=0, keepdims=True)
        grad = cot_ref[span, :].astype(F32) + norm_back(second_grad, hat, scale, vec_scr[0:1, :])
        hg_ref[span, :] = grad
        branch = (grad * live).astype(BF)
        branch_scr[span, :] = branch
        cg_ref[span, :] = dot(branch, wo_scr[...], (1, 1)).astype(BF)

    def nothing(span):
        pass

    for k in range(2):

        @pl.when(step == k)
        def _():
            now = slice(k * d, (k + 1) * d)
            ffn_block(
                rows, in_ref, og_ref, act_scr, eg_scr, mix_ref, sg_ref,
                we_scr.at[:, now], wr_scr.at[:, now], eb_scr[:, now],
                open_rows if first and k == 0 else nothing,
                nothing if first or k == 0 else close_rows,
            )
            if first and k == 0:
                in_scr[...] = in_ref[...].T
            esum_ref[:, now] = jnp.sum(eg_scr[...].astype(F32), axis=0, keepdims=True)
            mine = order if first else turned
            grad_scr[...] = dot(in_scr[...], eg_scr[...]).astype(BF)
            pack_rows(mine, me, grad_scr, (lo_ref, hi_ref), now, chunk)
            grad_scr[...] = dot(act_scr[...], og_ref[...], (0, 0)).astype(BF)
            pack_rows(mine, me, grad_scr, (lo_ref, hi_ref), slice(wide + k * d, wide + (k + 1) * d), chunk)

    if first:
        return

    @pl.when(step == pl.num_programs(0) - 1)
    def _():
        copy = pltpu.make_async_copy(mixed_scr, mixed_ref, sem)
        copy.start()
        grad_scr[:half, :] = dot(ctx0_ref[...], branch_scr[...], (0, 0)).astype(BF)
        grad_scr[half:, :] = dot(ctx1_ref[...], branch_scr[...], (0, 0)).astype(BF)
        pack_rows(order, me, grad_scr, (olo_ref, ohi_ref), slice(0, d), chunk)
        if order.stepped:
            small = jnp.zeros((order.devices, 128), F32)
            for k in range(3):
                small += fold_lanes(order, me, sums_ref[k : k + 1, :], k * chunk, chunk, 128)
            more = jnp.zeros((order.devices, 128), F32)
            for k in range(2):
                now = slice(k * d, (k + 1) * d)
                more += fold_lanes(order, me, esum0_ref[:, now], k * chunk, chunk, 128)
                more += fold_lanes(order, me, esum_ref[:, now], (2 + k) * chunk, chunk, 128)
            block = (place_rows(small, 0, chunk) + place_rows(more, 1, chunk)).astype(BF)
            olo_ref[:, d:] = block[: d // 2]
            ohi_ref[:, d:] = block[d // 2 :]
        copy.wait()


def attend_back_kernel(
    order,
    seq,
    group,
    me_ref,
    p_ref,
    q_ref,
    cg_ref,
    kx_ref,
    vx_ref,
    in_ref,
    w_ref,
    spread_ref,
    *refs,
):
    last = group == GROUPS - 1
    if last:
        x_ref, fig0_ref, hg_ref, gain_ref, lo_ref, hi_ref, tg_ref, sums_ref = refs[:8]
        dk_scr, dv_scr, dj_scr, j_scr, tg_scr, sem = refs[8:]
    else:
        olo_ref, ohi_ref, lo_ref, hi_ref, fig_ref = refs[:5]
        dk_scr, dv_scr, dj_scr, j_scr = refs[5:]
    d = in_ref.shape[1]
    chunk = d // order.devices
    levels, total, _ = geometry(seq)
    near, _, far_base = split_levels(seq)
    tile = pl.program_id(0)
    lanes = q_ref.shape[1]
    me = me_ref[0]

    @pl.when(tile == 0)
    def _():
        dk_scr[...] = jnp.zeros_like(dk_scr)
        dv_scr[...] = jnp.zeros_like(dv_scr)
        if not last:
            lo_ref[:, 3 * lanes :] = olo_ref[...]
            hi_ref[:, 3 * lanes :] = ohi_ref[...]

    tiles = range(STEP)
    grads, prob_grads, score_grads = [], [], []
    for t in tiles:
        grads.append(split_heads(cg_ref[t * TILE : (t + 1) * TILE, :]))
        prob_grads.append(dot(window_of(vx_ref, tile * STEP + t, levels), grads[t], (1, 1)))
    for t in tiles:
        prob = p_ref[t].astype(F32)
        inner = jnp.sum(prob * prob_grads[t], axis=0, keepdims=True)
        score_grads.append((prob * (prob_grads[t] - inner)).astype(BF))
    for t in tiles:
        now = tile * STEP + t
        query_grad = own_heads(dot(score_grads[t], window_of(kx_ref, now, levels), (0, 0)))
        dj_scr[pl.ds(pl.multiple_of(now * TILE, TILE), TILE), :lanes] = (query_grad * 0.125).astype(BF)
    for t in tiles:
        now = tile * STEP + t
        key_grad = dot(score_grads[t], split_heads(q_ref[t * TILE : (t + 1) * TILE, :]))
        val_grad = dot(p_ref[t], grads[t])
        at = 0
        for v in levels:
            for row, n in v.spans(now):
                dk_scr[pl.ds(row, n), :] += key_grad[at : at + n]
                dv_scr[pl.ds(row, n), :] += val_grad[at : at + n]
                at += n

    @pl.when(tile == pl.num_programs(0) - 1)
    def _():
        pad = levels[0].pad
        for ref, at in ((dk_scr, lanes), (dv_scr, 2 * lanes)):
            far = ref[far_base:total, :].astype(BF)
            for t in range(seq // POOL):
                parts = []
                for v in near:
                    n = POOL // v.factor
                    base = v.base + v.pad + t * n
                    parts.append(ref[base : base + n, :].astype(BF))
                parts.append(far)
                spread = dot(spread_ref[t * POOL : (t + 1) * POOL, :], jnp.concatenate(parts, axis=0))
                whole = ref[pad + t * POOL : pad + (t + 1) * POOL, :] + spread
                dj_scr[t * POOL : (t + 1) * POOL, at : at + lanes] = whole.astype(BF)
        j_scr[...] = dot(in_ref[...], dj_scr[...], (0, 0)).astype(BF)
        mine = order.turned if last else order
        pack_rows(mine, me, j_scr, (lo_ref, hi_ref), slice(0, 3 * lanes), chunk)
        step = 256
        if last:
            gain = gain_ref[0:1, :]
            gains = jnp.zeros((1, d), F32)
            shifts = jnp.zeros((1, d), F32)
        for r in range(0, seq, step):
            fig = sum(
                dot(
                    dj_scr[r : r + step, k * lanes : (k + 1) * lanes],
                    w_ref[:, k * d + group * lanes : k * d + (group + 1) * lanes],
                    (1, 1),
                )
                for k in range(3)
            )
            if not last:
                fig_ref[r : r + step, :] = fig
                continue
            fig = fig + fig0_ref[r : r + step, :]
            hat, scale = normalize(x_ref[r : r + step, :].astype(F32))
            gains += jnp.sum(fig * hat, axis=0, keepdims=True)
            shifts += jnp.sum(fig, axis=0, keepdims=True)
            grad = hg_ref[r : r + step, :] + norm_back(fig, hat, scale, gain)
            tg_scr[r : r + step, :] = grad.astype(BF)
        if last:
            copy = pltpu.make_async_copy(tg_scr, tg_ref, sem)
            copy.start()
            sums_ref[0:1, :] = gains
            sums_ref[1:2, :] = shifts
            if order.stepped:
                folded = fold_lanes(mine, me, gains, 0, chunk, 128)
                folded += fold_lanes(mine, me, shifts, chunk, chunk, 128)
                block = place_rows(folded, 0, chunk).astype(BF)
                lo_ref[:, 3 * lanes :] = block[: d // 2]
                hi_ref[:, 3 * lanes :] = block[d // 2 :]
            copy.wait()


def whole(shape):
    return pl.BlockSpec(shape, lambda i: (0,) * len(shape))


def smem():
    return pl.BlockSpec(memory_space=pltpu.SMEM)


def launch(name, kernel, steps, ins, outs, scratch, after=(), mib=8, cost=2 * 10**10, aliases=()):
    n = len(ins)

    def body(*refs):
        kernel(*refs[:n], *refs[n + len(after) :])

    return pl.pallas_call(
        body,
        grid=(steps,),
        in_specs=[s for _, s in ins] + [pl.BlockSpec(memory_space=pl.ANY)] * len(after),
        out_specs=[s for _, s in outs],
        out_shape=[o for o, _ in outs],
        scratch_shapes=scratch,
        compiler_params=pltpu.CompilerParams(
            dimension_semantics=("arbitrary",), vmem_limit_bytes=mib * MIB
        ),
        cost_estimate=pl.CostEstimate(flops=cost, bytes_accessed=0, transcendentals=0),
        input_output_aliases=dict(aliases),
        name=name,
    )(*[a for a, _ in ins], *after)


def out(shape, dtype, spec=None):
    return jax.ShapeDtypeStruct(shape, dtype), whole(shape) if spec is None else spec


def in_hbm(shape, dtype):
    return pltpu.HBM(shape, dtype), pl.BlockSpec(memory_space=pltpu.HBM)


def full(array):
    return array, whole(array.shape)


def by_rows(rows, width, column=0):
    return pl.BlockSpec((rows, width), lambda i: (i, column))


def by_columns(rows, width):
    return pl.BlockSpec((rows, width), lambda i: (0, i))


def by_tiles(shape):
    return pl.BlockSpec((STEP, *shape[1:]), lambda i: (i, 0, 0))


def fixed_columns(rows, width, column):
    return pl.BlockSpec((rows, width), lambda i: (0, column))


def prepare(lens, seq, after=()):
    _, _, window = geometry(seq)
    shape = (seq // TILE, window, 128)
    return launch(
        "prepare",
        functools.partial(prepare_kernel, seq),
        seq // TILE // STEP,
        [(lens, smem())],
        [out(shape, F32, by_tiles(shape))],
        [],
        after,
        cost=0,
    )[0]


def by_blocks(source, width, chunk, blocks):
    group = 128 // chunk
    lane = iota((source.shape[0], 128), 1) // chunk
    columns = []
    for at in range(0, blocks * width, 128):
        column = None
        for k in range(group):
            device, block = (at % width) // chunk + k, at // width
            lanes = (device * blocks + block) * chunk
            piece = source[:, lanes // 128 * 128 : lanes // 128 * 128 + 128]
            shift = (k * chunk - lanes) % 128
            if shift:
                piece = pltpu.roll(piece, shift, 1)
            column = piece if column is None else jnp.where(lane == k, piece, column)
        columns.append(column)
    return columns


def from_blocks(parts, width, chunk, blocks):
    group = 128 // chunk
    lane = iota((parts[0].shape[0], 128), 1) // chunk
    columns = []
    for at in range(0, blocks * width, 128):
        column = None
        for k in range(group):
            device, block = divmod(at // chunk + k, blocks)
            lanes = device * chunk
            piece = parts[block][:, lanes // 128 * 128 : lanes // 128 * 128 + 128]
            shift = (k * chunk - lanes) % 128
            if shift:
                piece = pltpu.roll(piece, shift, 1)
            column = piece if column is None else jnp.where(lane == k, piece, column)
        columns.append(column)
    return columns


def pack_kernel(joint_ref, expand_ref, output_ref, reduce_ref, *refs):
    small, (a_ref, e1_ref, e2_ref, scr), lines, sems = refs[:6], refs[6:10], refs[10:16], refs[16]
    chunk, d = output_ref.shape
    wide = joint_ref.shape[1]
    targets = [
        (expand_ref, scr),
        (joint_ref, a_ref.at[:, :wide]),
        (output_ref, e1_ref.at[:, 4 * d : 5 * d]),
    ]
    for k in range(4):
        target = (e1_ref, e2_ref)[k // 2].at[:, (2 + k % 2) * d : (3 + k % 2) * d]
        targets.append((reduce_ref.at[k * chunk : (k + 1) * chunk, :], target))
    targets += zip(small, lines)
    copies = [pltpu.make_async_copy(a, b, sems.at[i]) for i, (a, b) in enumerate(targets)]
    for copy in copies:
        copy.start()
    for copy in copies:
        copy.wait()

    def line(vectors):
        flat = jnp.concatenate([v[...].reshape(1, v.shape[0]).astype(F32) for v in vectors], axis=1)
        gap = jnp.zeros((1, 128 - flat.shape[1]), F32)
        return jnp.concatenate([flat, gap], axis=1)

    def block(parts):
        gap = jnp.zeros((chunk - len(parts), 128), F32)
        return jnp.concatenate(parts + [gap], axis=0).astype(BF)

    a_ref[:, wide:] = block([line(lines[:2])])
    e1_ref[:, 5 * d :] = block([line(lines[2:5]), line(lines[5:])])
    columns = by_blocks(scr[...].astype(F32), d, chunk, 4)
    for i, column in enumerate(columns):
        target = (e1_ref, e2_ref)[i * 128 // (2 * d)]
        at = i * 128 % (2 * d)
        target[:, at : at + 128] = column.astype(BF)


def pack(joint, expand, output, reduce, small):
    rows, wide = joint.shape
    d = output.shape[1]
    return launch(
        "pack",
        pack_kernel,
        1,
        [
            (pltpu.with_memory_space_constraint(a, pltpu.HBM), pl.BlockSpec(memory_space=pltpu.HBM))
            for a in (joint, expand, output, reduce, *small)
        ],
        [out((rows, wide + 128), BF), out((rows, 5 * d + 128), BF), out((rows, 4 * d), BF)],
        [pltpu.VMEM(expand.shape, BF)]
        + [pltpu.VMEM(v.shape, BF) for v in small]
        + [pltpu.SemaphoreType.DMA((13,))],
        mib=4,
        cost=0,
    )


def finish_kernel(one_ref, two_ref, expand_ref, reduce_ref, output_ref, *small):
    chunk, d = output_ref.shape
    parts = [one_ref[:, :d], one_ref[:, d : 2 * d], two_ref[:, :d], two_ref[:, d : 2 * d]]
    for i, column in enumerate(from_blocks(parts, d, chunk, 4)):
        expand_ref[:, i * 128 : (i + 1) * 128] = column
    for k in range(4):
        source = (one_ref, two_ref)[k // 2]
        reduce_ref[k * chunk : (k + 1) * chunk, :] = source[:, (2 + k % 2) * d : (3 + k % 2) * d]
    at = two_ref.shape[1] - 128
    output_ref[...] = two_ref[:, at - d : at]
    for k in range(3):
        small[k][...] = two_ref[0:1, at + k * chunk : at + (k + 1) * chunk].reshape(chunk)
    small[3][...] = two_ref[1:2, at : at + 4 * chunk].reshape(4 * chunk)


def finish(one, two, after):
    rows, d = one.shape[0], one.shape[1] // 4
    return launch(
        "finish",
        finish_kernel,
        1,
        [full(one), full(two)],
        [out((rows, 4 * d), F32), out((4 * rows, d), F32), out((rows, d), F32)]
        + [out((rows,), F32)] * 3
        + [out((4 * rows,), F32)],
        [],
        after,
    )


def close_kernel(lanes, before_ref, keep_ref, other_ref, joint_ref, gain_ref, shift_ref):
    total = keep_ref[...].astype(F32) + other_ref[...].astype(F32)
    chunk, d = joint_ref.shape[0], joint_ref.shape[1] // 3
    at = 4 * d
    for k in range(3):
        joint_ref[:, k * d : k * d + lanes] = before_ref[:, at + k * lanes : at + (k + 1) * lanes]
        joint_ref[:, k * d + lanes : (k + 1) * d] = total[:, k * lanes : (k + 1) * lanes]
    gain_ref[...] = total[0:1, 3 * lanes : 3 * lanes + chunk].reshape(chunk)
    shift_ref[...] = total[0:1, 3 * lanes + chunk : 3 * lanes + 2 * chunk].reshape(chunk)


def close(before, pair, d):
    rows = before.shape[0]
    return launch(
        "close",
        functools.partial(close_kernel, d // GROUPS),
        1,
        [full(before), full(pair[0]), full(pair[1])],
        [out((rows, 3 * d), F32)] + [out((rows,), F32)] * 2,
        [],
        cost=0,
    )


def merge_kernel(plan, *refs):
    n = sum(1 if kind == "carry" else 2 * count for kind, count in plan)
    ins, outs = list(refs[:n]), list(refs[n:])
    for kind, count in plan:
        if kind == "carry":
            outs.pop(0)[...] = ins.pop(0)[...]
            continue
        targets = [outs.pop(0) for _ in range(2 if kind == "add" else 1)]
        at = 0
        for _ in range(count):
            first, second = ins.pop(0), ins.pop(0)
            rows, width = first.shape
            columns = slice(at, at + width)
            at += width
            if kind == "join":
                targets[0][:rows, columns] = first[...]
                targets[0][rows:, columns] = second[...]
                continue
            total = first[...].astype(F32) + second[...].astype(F32)
            if kind == "last":
                targets[0][:, columns] = total
                continue
            targets[0][:, columns] = total[: rows // 2].astype(BF)
            targets[1][:, columns] = total[rows // 2 :].astype(BF)


def merge(plan, arrays, after):
    outs = []
    for (kind, _), pairs in zip(plan, arrays, strict=True):
        rows = pairs[0][0].shape[0]
        width = sum(p[0].shape[1] for p in pairs)
        if kind == "carry":
            outs.append(out((rows, width), pairs[0][0].dtype))
        elif kind == "join":
            outs.append(out((2 * rows, width), BF))
        elif kind == "last":
            outs.append(out((rows, width), F32))
        else:
            outs += [out((rows // 2, width), BF)] * 2
    return launch(
        "merge",
        functools.partial(merge_kernel, plan),
        1,
        [full(a) for pairs in arrays for pair in pairs for a in pair],
        outs,
        [],
        after,
        cost=0,
    )


def attend(order, me, group, bias, x, weights, vec, after=()):
    seq, d = x.shape
    lanes = d // GROUPS
    _, total, window = geometry(seq)
    tiles = seq // TILE
    cols = lanes // DIM * TILE
    near, _, far_base = split_levels(seq)
    scratch = [
        pltpu.VMEM((sum(POOL // v.factor for v in near), POOL), BF),
        pltpu.VMEM((total - far_base, seq), BF),
    ]
    ins = [(me, smem()), (bias, by_tiles(bias.shape))]
    if group == 0:
        x = pltpu.with_memory_space_constraint(x, pltpu.HBM)
        ins.append((x, pl.BlockSpec(memory_space=pltpu.HBM)))
        scratch += [pltpu.VMEM((seq, d), BF), pltpu.SemaphoreType.DMA]
    else:
        ins.append(full(x))
    ins += [full(w) for w in weights]
    outs = [
        out((tiles, window, cols), BF, by_tiles((tiles, window, cols))),
        out((seq, lanes), BF, by_rows(STEP * TILE, lanes)),
        out((seq, lanes), BF),
        out((total, lanes), BF),
        out((total, lanes), BF),
    ]
    if group == 0:
        ins.append(full(vec))
        outs += [out((seq, d), BF), out((d, 3 * d), BF), out((8, d), F32)]
    return launch(
        "attend",
        functools.partial(attend_kernel, order, seq, group),
        tiles // STEP,
        ins,
        outs,
        scratch,
        after,
        cost=2 * 10**10 if group == 0 else 0,
    )


def ffn_scratch(seq, d):
    return [
        pltpu.VMEM((d, 2 * d), BF),
        pltpu.VMEM((d, 2 * d), BF),
        pltpu.VMEM((d, d), BF),
        pltpu.VMEM((1, 2 * d), F32),
        pltpu.VMEM((d, seq), BF),
        pltpu.VMEM((seq, d), BF),
        pltpu.VMEM((seq, d), BF),
        pltpu.VMEM((d, d), BF),
        pltpu.VMEM((8, d), F32),
    ]


def ffn_first(order, me, lens, x, cot, ctx0, ctx1, e1, vec, ebias, after=()):
    seq, d = x.shape
    return launch(
        "ffn_first",
        functools.partial(ffn_kernel, order, 0),
        2,
        [(me, smem()), (lens, smem())]
        + [full(a) for a in (x, cot, ctx0, ctx1, *e1, vec, ebias)],
        [
            out((seq, d), F32),
            out((seq, d), BF),
            out((seq, d), BF),
            out((seq, d), F32),
            out((seq, d), F32),
            out((1, 2 * d), F32),
            out((d // 2, 4 * d), BF),
            out((d // 2, 4 * d), BF),
        ],
        ffn_scratch(seq, d),
        after,
        mib=12,
    )


def ffn_second(order, me, lens, cot, kept, ctx0, ctx1, e1, e2, vec, ebias, after=()):
    seq, d = cot.shape
    width = d + (128 if order.stepped else 0)
    return launch(
        "ffn_second",
        functools.partial(ffn_kernel, order, 1),
        2,
        [(me, smem()), (lens, smem())]
        + [full(a) for a in (cot, *kept, ctx0, ctx1, *e1, *e2, vec, ebias)],
        [
            in_hbm((seq, d), BF),
            out((seq, d), F32),
            out((seq, d), BF),
            out((d // 2, 4 * d), BF),
            out((d // 2, 4 * d), BF),
            out((d // 2, width), BF),
            out((d // 2, width), BF),
            out((8, d), F32),
            out((1, 2 * d), F32),
            out((seq, d), F32),
            out((seq, d), F32),
        ],
        ffn_scratch(seq, d) + [pltpu.VMEM((seq, d), BF), pltpu.VMEM((seq, d), BF), pltpu.SemaphoreType.DMA],
        after,
        aliases={3: 1, 6: 9, 7: 10},
        mib=14,
    )


def attend_back(order, me, group, prob, q, cg, kx, vx, first_in, weights, more, after=()):
    seq, d = first_in.shape
    lanes = d // GROUPS
    levels, total, _ = geometry(seq)
    spread = spreading(seq)
    last = group == GROUPS - 1
    extra = (128 if order.stepped else 0) if last else more[0].shape[1]
    ins = [
        (me, smem()),
        (prob, by_tiles(prob.shape)),
        (q, by_rows(STEP * TILE, lanes)),
        (cg, by_rows(STEP * TILE, lanes, group)),
        full(kx),
        full(vx),
        full(first_in),
        full(weights),
        full(jnp.asarray(spread, BF)),
    ]
    ins += [full(a) for a in more]
    outs = [out((d // 2, 3 * lanes + extra), BF)] * 2
    if last:
        outs += [in_hbm((seq, d), BF), out((8, d), F32)]
    else:
        outs.append(out((seq, d), F32))
    return launch(
        "attend_back",
        functools.partial(attend_back_kernel, order, seq, group),
        prob.shape[0] // STEP,
        ins,
        outs,
        [
            pltpu.VMEM((total, lanes), F32),
            pltpu.VMEM((total, lanes), F32),
            pltpu.VMEM((seq, 3 * lanes), BF),
            pltpu.VMEM((d, 3 * lanes), BF),
        ]
        + ([pltpu.VMEM((seq, d), BF), pltpu.SemaphoreType.DMA] if last else []),
        after,
        mib=17,
    )


class Gather:
    def __init__(self, order, value):
        self.order, self.bits, self.have, self.other = order, list(order.bits), value, None
        if not order.stepped:
            half = value.shape[0] // 2
            self.have, self.other, self.bits = value[:half], value[half:], []

    def send(self):
        if self.bits:
            self.other = swap(self.order, self.have, self.bits.pop(0))

    def kind(self):
        return "join", 1

    def pairs(self):
        return [(self.have, self.other)]

    def pair(self):
        return self.have, self.other

    def take(self, outs):
        self.have = outs.pop(0)


class Scatter:
    def __init__(self, order, halves):
        self.order, self.bits, self.halves, self.other = order, order.bits[::-1], halves, None
        self.done = None
        self.beside = []
        if not order.stepped:
            self.done = jnp.concatenate(halves, axis=0).astype(F32)

    def send(self):
        if self.order.stepped:
            self.other = swap(self.order, self.halves[1], self.bits.pop(0))

    def kind(self):
        return "add" if self.bits else "last", 1 + len(self.beside)

    def pairs(self):
        return [(self.halves[0], self.other)] + self.beside

    def absorb(self, chain):
        if self.order.stepped:
            self.beside += chain.pairs()

    def take(self, outs):
        self.beside = []
        if self.bits:
            self.halves = outs.pop(0), outs.pop(0)
        else:
            self.done = outs.pop(0)


def swap(order, value, bit):
    return lax.ppermute(value, AXES, [(i, i ^ bit) for i in range(order.devices)])


def advance(order, chains, after=(), carry=None):
    if not order.stepped:
        return () if carry is None else ((), carry)
    plan = [c.kind() for c in chains]
    arrays = [c.pairs() for c in chains]
    if carry is not None:
        plan.append(("carry", 1))
        arrays.append([(carry,)])
    outs = list(merge(plan, arrays, after))
    marks = tuple(outs)
    if carry is not None:
        carry = outs.pop()
    for c in chains:
        c.take(outs)
        if c.bits:
            c.send()
    return marks[:1] if carry is None else (marks[:1], carry)


def local(order, me, tokens, cotangent, lens, joint_w, output_w, expand_w, reduce_w,
          attn_gain, attn_shift, ffn_gain, ffn_shift, expand_bias, reduce_bias):
    seq, d = tokens.shape
    lanes = d // GROUPS
    rows = joint_w.shape[0]
    ff = expand_w.shape[1]
    vec = jnp.zeros((8, d), F32)
    ebias = jnp.zeros((1, ff), F32)
    if order.stepped:
        small = [attn_gain, attn_shift, ffn_gain, ffn_shift, reduce_bias, expand_bias]
        first, second, third = pack(joint_w, expand_w, output_w, reduce_w, small)
        joint = Gather(order, first)
        e1 = Gather(order, second)
        e2 = Gather(order, third)
    else:
        small = [attn_gain, attn_shift, ffn_gain, ffn_shift, reduce_bias]
        small = [lax.all_gather(v, AXES, tiled=True) for v in small]
        vec = jnp.pad(jnp.stack(small), ((0, 3), (0, 0))).astype(F32)
        ebias = lax.all_gather(expand_bias, AXES, tiled=True)[None].astype(F32)
        e, o, r = [lax.all_gather(w, AXES, axis=0, tiled=True) for w in (expand_w, output_w, reduce_w)]
        r = [r[k * d : (k + 1) * d] for k in range(4)]
        joint = Gather(order, lax.all_gather(joint_w, AXES, axis=0, tiled=True))
        e1 = Gather(order, jnp.concatenate([e[:, : 2 * d], r[0], r[1], o], axis=1))
        e2 = Gather(order, jnp.concatenate([e[:, 2 * d :], r[2], r[3]], axis=1))
    joint.send()
    mark = advance(order, [joint])
    e1.send()
    mark = advance(order, [joint, e1], mark)
    e2.send()
    mark = advance(order, [joint, e1, e2], mark)
    bias = prepare(lens, seq, mark)
    mark = advance(order, [joint, e1, e2], (bias,))
    p0, ctx0, q0, kx0, vx0, first_in, w, gain = attend(order, me, 0, bias, tokens, joint.pair(), vec, mark)
    p1, ctx1, q1, kx1, vx1 = attend(order, me, 1, bias, first_in, (w,), vec, (ctx0,))
    mark = advance(order, [e1, e2], (ctx1,))
    *kept, lo, hi = ffn_first(
        order, me, lens, tokens, cotangent, ctx0, ctx1, e1.pair(), vec, ebias, mark
    )
    t1 = Scatter(order, (lo, hi))
    mark = advance(order, [e2], (lo,))
    t1.send()
    mark = advance(order, [t1], mark)
    mixed, hg, cg, lo, hi, olo, ohi, sums, esum, _, _ = ffn_second(
        order, me, lens, cotangent, kept, ctx0, ctx1, e1.pair(), e2.pair(), vec, ebias, mark
    )
    mark = advance(order, [t1], (cg,))
    t2 = Scatter(order.turned, (lo, hi))
    t2.send()
    lo, hi, fig = attend_back(order, me, 0, p0, q0, cg, kx0, vx0, first_in, w, (olo, ohi), mark)
    mark, hi = advance(order, [t1, t2], (fig,), hi)
    j0 = Scatter(order, (lo, hi))
    j0.send()
    mark = advance(order, [j0], mark)
    lo, hi, token_grad, tail_sums = attend_back(
        order, me, 1, p1, q1, cg, kx1, vx1, first_in, w, (tokens, fig, hg, gain), mark
    )
    mark, hi = advance(order, [t1, t2, j0], (tail_sums,), hi)
    j1 = Scatter(order.turned, (lo, hi))
    j1.send()
    mark = advance(order, [j1], mark)
    t2.absorb(j0)
    mark = advance(order, [t2], mark)
    mark = advance(order, [j1], mark)
    mark = advance(order, [t2, t1], mark)
    mark = advance(order, [j1], mark)
    mark = advance(order, [j1], mark)
    if order.stepped:
        advance(order, [t2], mark)
        expand_grad, reduce_grad, output_grad, *small = finish(t1.done, t2.done, mark)
        joint_grad, *first_small = close(t2.done, j1.pairs()[0], d)
        small = [*first_small, small[0], small[1], small[3], small[2]]
    else:
        parts = []
        for k in range(3):
            parts += [c.done[:, k * lanes : (k + 1) * lanes] for c in (j0, j1)]
        joint_grad = jnp.concatenate(parts, axis=1)
        one, two = t1.done, t2.done
        expand_grad = lax.psum_scatter(
            jnp.concatenate([one[:, : 2 * d], two[:, : 2 * d]], axis=1), AXES, scatter_dimension=0, tiled=True
        )
        reduce_grad = lax.psum_scatter(
            jnp.concatenate([t[:, k * d : (k + 1) * d] for t in (one, two) for k in (2, 3)], axis=0),
            AXES,
            scatter_dimension=0,
            tiled=True,
        )
        output_grad = lax.psum_scatter(j0.done[:, 3 * lanes :], AXES, scatter_dimension=0, tiled=True)
        joint_grad = lax.psum_scatter(joint_grad, AXES, scatter_dimension=0, tiled=True)
        esums = jnp.concatenate([kept[5][0], esum[0]])
        vectors = [tail_sums[0], tail_sums[1], sums[0], sums[1], esums, sums[2]]
        small = [lax.psum_scatter(v, AXES, scatter_dimension=0, tiled=True) for v in vectors]
    return (mixed, token_grad, joint_grad, output_grad, expand_grad, reduce_grad, *small)


def shards(order, *args):
    sub = lax.axis_size("sub")
    me = (lax.axis_index("dp") * sub + lax.axis_index("sub")).astype(jnp.int32).reshape(1)
    return local(order, me, *args)


def solution(mesh):
    order = Order(math.prod(mesh.shape[a] for a in AXES))
    wide = P(AXES, None)
    flat = P(AXES)
    return jax.shard_map(
        functools.partial(shards, order),
        mesh=mesh,
        in_specs=(wide,) * 7 + (flat,) * 6,
        out_specs=(wide,) * 6 + (flat,) * 6,
        check_vma=False,
    )
```

```python
import functools
import math

import jax
import jax.numpy as jnp
import numpy as np
from jax import lax
from jax.experimental import pallas as pl
from jax.experimental.pallas import tpu as pltpu
from jax.sharding import PartitionSpec as P

HEADS = 8
BLOCK = 16
LEVELS = 7
TILE = 64
POOL = 128
GROUPS = 2
DIM = 64
STEP = 8
LOG_TWO = math.log(2.0)
NEGATIVE = -1e30
ROOT_HALF = 1.0 / math.sqrt(2.0)
DENSITY = 1.0 / math.sqrt(2.0 * math.pi)
AXES = ("dp", "sub")
BF = jnp.bfloat16
F32 = jnp.float32
MIB = 1 << 20


class Level:
    def __init__(self, level, seq, base):
        self.level = level
        self.factor = 1 << level
        self.count = seq // self.factor
        self.width = BLOCK * self.factor
        self.blocks = seq // self.width
        self.pad = BLOCK if self.blocks > 2 else 0
        self.base = base
        self.rows = self.count + 2 * self.pad

    def pieces(self, tile):
        if self.width < TILE:
            return [(tile * (TILE // self.factor), TILE // self.factor + 2 * BLOCK)]
        block = tile // (self.width // TILE)
        if self.blocks > 2:
            return [(block * BLOCK, BLOCK), ((block + 2) * BLOCK, BLOCK)]
        return [((self.blocks - 1 - block) * BLOCK, BLOCK)]

    def spans(self, tile):
        return [(pl.multiple_of(self.base + first, BLOCK), n) for first, n in self.pieces(tile)]


def geometry(seq):
    levels, base = [], 0
    for level in range(LEVELS):
        levels.append(Level(level, seq, base))
        base += levels[-1].rows
    return levels, base, sum(n for v in levels for _, n in v.pieces(0))


def split_levels(seq):
    levels, _, _ = geometry(seq)
    near = [v for v in levels[1:] if v.width <= POOL]
    far = [v for v in levels[1:] if v.width > POOL]
    return near, far, far[0].base


def spreading(seq):
    levels, total, _ = geometry(seq)
    near, far, far_base = split_levels(seq)
    near_rows = sum(POOL // v.factor for v in near)
    spread = np.zeros((seq, near_rows + total - far_base), np.float32)
    at = 0
    for v in near:
        for t in range(seq):
            spread[t, at + t % POOL // v.factor] = 1.0 / v.factor
        at += POOL // v.factor
    for v in far:
        for t in range(seq):
            spread[t, near_rows + v.base - far_base + v.pad + t // v.factor] = 1.0 / v.factor
    return spread


class Order:
    def __init__(self, devices, turned=False):
        self.devices = devices
        self.bits = [1 << k for k in reversed(range(devices.bit_length() - 1))]
        self.stepped = devices == 32
        if not turned:
            self.turned = Order(devices, True)
        elif self.stepped:
            self.bits[-3:-1] = self.bits[-2], self.bits[-3]

    def flip(self, p):
        value = 0
        for k, bit in enumerate(self.bits):
            value = value + ((p >> k) & 1) * bit
        return value


def dot(left, right, contract=(1, 0)):
    return lax.dot_general(
        left, right, (((contract[0],), (contract[1],)), ((), ())), preferred_element_type=F32
    )


def iota(shape, axis):
    return lax.broadcasted_iota(jnp.int32, shape, axis)


def unpack_rows(order, me, halves, columns, target, chunk, places=slice(None)):
    rows = halves[0].shape[0]
    if not order.stepped:
        target[:rows, places] = halves[0][:, columns]
        target[rows:, places] = halves[1][:, columns]
        return
    for p in range(order.devices):
        half, at = divmod(p * chunk, rows)
        row = pl.multiple_of((me ^ order.flip(p)) * chunk, chunk)
        target[pl.ds(row, chunk), places] = halves[half][at : at + chunk, columns]


def pack_rows(order, me, source, halves, columns, chunk):
    rows = halves[0].shape[0]
    if not order.stepped:
        halves[0][:, columns] = source[:rows]
        halves[1][:, columns] = source[rows:]
        return
    for p in range(order.devices):
        half, at = divmod(p * chunk, rows)
        row = pl.multiple_of((me ^ order.flip(p)) * chunk, chunk)
        halves[half][at : at + chunk, columns] = source[pl.ds(row, chunk), :]


def owners(order, me, shape):
    return me ^ order.flip(iota(shape, 0))


def spread_lanes(order, me, halves, columns, row, offset, chunk, total):
    n = order.devices
    block = jnp.concatenate([half[:, columns] for half in halves], axis=0)
    step = block.shape[0] // n
    pick = (iota((n, block.shape[0]), 1) == iota((n, block.shape[0]), 0) * step + row).astype(BF)
    rows = dot(pick, block).astype(BF)
    lanes = block.shape[1]
    place = (iota((lanes, total), 0) == iota((lanes, total), 1) % chunk + offset).astype(BF)
    wide = dot(rows, place)
    mine = iota((n, total), 1) // chunk == owners(order, me, (n, total))
    return jnp.sum(jnp.where(mine, wide, 0.0), axis=0, keepdims=True)


def fold_lanes(order, me, vector, offset, chunk, lanes):
    n, total = order.devices, vector.shape[1]
    mine = iota((n, total), 1) // chunk == owners(order, me, (n, total))
    wide = jnp.where(mine, vector, 0.0).astype(BF)
    place = (iota((total, lanes), 1) == iota((total, lanes), 0) % chunk + offset).astype(BF)
    return dot(wide, place)


def place_rows(rows, row, step):
    n = rows.shape[0]
    pick = (iota((n * step, n), 0) == iota((n * step, n), 1) * step + row).astype(BF)
    return dot(pick, rows.astype(BF))


def live_column(lens, first, rows):
    position = first + iota((rows, 1), 0)
    start, live = 0, jnp.zeros((rows, 1), jnp.bool_)
    for i in range(lens.shape[1]):
        length = lens[0, i]
        live = live | ((position >= start) & (position < start + length))
        start = start + (length + BLOCK - 1) // BLOCK * BLOCK
    return live


def tile_bias(lens, tile, levels, copies):
    position = tile * TILE + iota((1, copies * TILE), 1) % TILE
    low, high, start = position, position + 1, 0
    for i in range(lens.shape[1]):
        length = lens[0, i]
        inside = (position >= start) & (position < start + length)
        low = jnp.where(inside, start, low)
        high = jnp.where(inside, start + length, high)
        start = start + (length + BLOCK - 1) // BLOCK * BLOCK
    parts = []
    for v in levels:
        reach = (position // v.width - 1) * v.width
        least = jnp.maximum(low, reach)
        most = jnp.minimum(high - v.factor, reach + 3 * v.width - 1)
        half = v.width // 2
        lower = (position // half - 1) * half
        for first, rows in v.pieces(tile):
            begin = (first - v.pad + iota((rows, copies * TILE), 0)) * v.factor
            valid = (begin >= least) & (begin <= most)
            if v.level > 0:
                valid = valid & ((begin < lower) | (begin >= lower + 3 * half))
            parts.append(jnp.where(valid, v.level * LOG_TWO, NEGATIVE))
    return jnp.concatenate(parts, axis=0)


def window_of(ref, tile, levels):
    return jnp.concatenate([ref[pl.ds(at, n), :] for v in levels for at, n in v.spans(tile)], axis=0)


def split_heads(rows):
    head = iota(rows.shape, 1) // DIM
    zero = jnp.zeros_like(rows)
    return jnp.concatenate([jnp.where(head == h, rows, zero) for h in range(rows.shape[1] // DIM)], axis=0)


def own_heads(full):
    heads = full.shape[1] // DIM
    head = iota((TILE, full.shape[1]), 1) // DIM
    own = full[:TILE]
    for h in range(1, heads):
        own = jnp.where(head == h, full[h * TILE : (h + 1) * TILE], own)
    return own


def normalize(values):
    centre = values - jnp.mean(values, axis=-1, keepdims=True)
    scale = lax.rsqrt(jnp.mean(centre * centre, axis=-1, keepdims=True) + 1e-05)
    return centre * scale, scale


def norm_back(grad, normed, scale, gain):
    scaled = grad * gain
    return scale * (
        scaled
        - jnp.mean(scaled, axis=-1, keepdims=True)
        - normed * jnp.mean(scaled * normed, axis=-1, keepdims=True)
    )


def prepare_kernel(seq, lens_ref, bias_ref):
    levels, _, _ = geometry(seq)
    step = pl.program_id(0)
    for t in range(STEP):
        bias_ref[t] = tile_bias(lens_ref, step * STEP + t, levels, bias_ref.shape[2] // TILE)


def means(seq, fine_ref, wide_ref):
    near, far, far_base = split_levels(seq)
    at = 0
    for v in near:
        n = POOL // v.factor
        same = iota((n, POOL), 1) // v.factor == iota((n, POOL), 0)
        fine_ref[at : at + n, :] = jnp.where(same, 1.0 / v.factor, 0.0).astype(BF)
        at += n
    for v in far:
        same = iota((v.rows, seq), 1) // v.factor == iota((v.rows, seq), 0) - v.pad
        base = v.base - far_base
        wide_ref[base : base + v.rows, :] = jnp.where(same, 1.0 / v.factor, 0.0).astype(BF)


def attend_kernel(order, seq, group, me_ref, bias_ref, x_ref, *refs):
    first_group = group == 0
    if first_group:
        lo_ref, hi_ref, vec_ref = refs[:3]
        p_ref, ctx_ref, q_ref, kx_ref, vx_ref, in_ref, w_ref, gain_ref = refs[3:11]
        fine_ref, wide_ref = refs[11:]
    else:
        w_ref, p_ref, ctx_ref, q_ref, kx_ref, vx_ref, fine_ref, wide_ref = refs
    levels, total, _ = geometry(seq)
    near, _, far_base = split_levels(seq)
    tile = pl.program_id(0)
    lanes = q_ref.shape[1]
    me = me_ref[0]

    @pl.when(tile == 0)
    def _():
        d = x_ref.shape[1]
        means(seq, fine_ref, wide_ref)
        if first_group:
            chunk = d // order.devices
            unpack_rows(order, me, (lo_ref, hi_ref), slice(0, 3 * d), w_ref, chunk)
            if order.stepped:
                tail = slice(3 * d, 3 * d + 128)
                gain = spread_lanes(order, me, (lo_ref, hi_ref), tail, 0, 0, chunk, d)
                shift = spread_lanes(order, me, (lo_ref, hi_ref), tail, 0, chunk, chunk, d)
            else:
                gain, shift = vec_ref[0:1, :], vec_ref[1:2, :]
            gain_ref[...] = jnp.broadcast_to(gain, gain_ref.shape)
        kx_ref[...] = jnp.zeros_like(kx_ref)
        vx_ref[...] = jnp.zeros_like(vx_ref)
        step = 256
        pad = levels[0].pad
        for r in range(0, seq, step):
            if first_group:
                hat, _ = normalize(x_ref[r : r + step, :].astype(F32))
                first_in = (hat * gain + shift).astype(BF)
                in_ref[r : r + step, :] = first_in
            else:
                first_in = x_ref[r : r + step, :]
            query, keys, vals = [
                dot(first_in, w_ref[:, k * d + group * lanes : k * d + (group + 1) * lanes]).astype(BF)
                for k in range(3)
            ]
            q_ref[r : r + step, :] = query * jnp.asarray(0.125, BF)
            kx_ref[pad + r : pad + r + step, :] = keys
            vx_ref[pad + r : pad + r + step, :] = vals
        for ref in (kx_ref, vx_ref):
            for t in range(seq // POOL):
                rows = ref[pad + t * POOL : pad + (t + 1) * POOL, :]
                pooled = dot(fine_ref[...], rows).astype(BF)
                at = 0
                for v in near:
                    n = POOL // v.factor
                    ref[v.base + v.pad + t * n : v.base + v.pad + (t + 1) * n, :] = pooled[at : at + n]
                    at += n
            ref[far_base:total, :] = dot(wide_ref[...], ref[pad : pad + seq, :]).astype(BF)

    tiles = range(STEP)
    scores = []
    for t in tiles:
        at = tile * STEP + t
        query = split_heads(q_ref[pl.ds(pl.multiple_of(at * TILE, TILE), TILE), :])
        scores.append(dot(window_of(kx_ref, at, levels), query, (1, 1)))
    probs = []
    for t in tiles:
        bias = jnp.concatenate([bias_ref[t]] * (scores[t].shape[1] // bias_ref.shape[2]), axis=1)
        score = scores[t] + bias
        peak = jnp.max(score, axis=0, keepdims=True)
        weight = jnp.exp(score - peak)
        share = 1.0 / jnp.sum(weight, axis=0, keepdims=True)
        probs.append((weight * share).astype(BF))
        p_ref[t] = probs[t]
    for t in tiles:
        context = dot(probs[t], window_of(vx_ref, tile * STEP + t, levels), (0, 0))
        ctx_ref[t * TILE : (t + 1) * TILE, :] = own_heads(context).astype(BF)


def ffn_block(rows, in_ref, og_ref, act_scr, eg_scr, mix_ref, sg_ref, we, wr, bias):
    for r in range(0, in_ref.shape[0], rows):
        part = slice(r, r + rows)
        expanded = dot(in_ref[part, :], we[...]) + bias
        phi = 0.5 * (1.0 + lax.erf(expanded * ROOT_HALF))
        activated = (expanded * phi).astype(BF)
        act_scr[part, :] = activated
        slope = phi + expanded * (jnp.exp(-0.5 * expanded * expanded) * DENSITY)
        expanded_grad = (dot(og_ref[part, :], wr[...], (1, 1)) * slope).astype(BF)
        eg_scr[part, :] = expanded_grad
        mix_ref[part, :] += dot(activated, wr[...])
        sg_ref[part, :] += dot(expanded_grad, we[...], (1, 1))


def ffn_kernel(order, part, me_ref, lens_ref, *refs):
    first = part == 0
    if first:
        x_ref, cot_ref, ctx0_ref, ctx1_ref, lo1_ref, hi1_ref, vec_ref, ebias_ref = refs[:8]
        hidden_ref, in_ref, og_ref, mix_ref, sg_ref, esum_ref, lo_ref, hi_ref = refs[8:16]
        own = (lo1_ref, hi1_ref)
        we_scr, wr_scr, wo_scr, eb_scr, in_scr, act_scr, eg_scr, grad_scr, vec_scr = refs[16:]
    else:
        cot_ref, hidden_ref, in_ref, og_ref, _, _, esum0_ref, ctx0_ref, ctx1_ref = refs[:9]
        lo1_ref, hi1_ref, lo2_ref, hi2_ref, vec_ref, ebias_ref = refs[9:15]
        mixed_ref, hg_ref, cg_ref, lo_ref, hi_ref, olo_ref, ohi_ref, sums_ref, esum_ref, mix_ref, sg_ref = refs[15:26]
        own = (lo2_ref, hi2_ref)
        we_scr, wr_scr, wo_scr, eb_scr, in_scr, act_scr, eg_scr, grad_scr, vec_scr, branch_scr = refs[26:]
    step = pl.program_id(0)
    me = me_ref[0]
    seq, d = cot_ref.shape
    rows = 512
    chunk = d // order.devices
    wide = 2 * d
    shared = (lo1_ref, hi1_ref)
    turned = order.turned
    half = ctx0_ref.shape[1]
    tail = slice(5 * d, 5 * d + 128)

    def bias_of(block, at):
        if order.stepped:
            return spread_lanes(order, me, shared, tail, 1, block * chunk, chunk, d)
        return ebias_ref[:, at : at + d]

    def live_rows(span):
        return live_column(lens_ref, span.start, rows).astype(F32)

    def open_rows(span):
        live = live_rows(span)
        out = dot(ctx0_ref[span, :], wo_scr[:half, :]) + dot(ctx1_ref[span, :], wo_scr[half:, :])
        hidden = x_ref[span, :].astype(F32) + live * out
        hidden_ref[span, :] = hidden
        hat, _ = normalize(hidden)
        in_ref[span, :] = (hat * vec_scr[0:1, :] + vec_scr[1:2, :]).astype(BF)
        og_ref[span, :] = (cot_ref[span, :].astype(F32) * live).astype(BF)

    def close_rows(span):
        live = live_rows(span)
        hidden = hidden_ref[span, :]
        mixed_ref[span, :] = (hidden + live * (mix_ref[span, :] + vec_scr[1:2, :])).astype(BF)
        hat, scale = normalize(hidden)
        second_grad = sg_ref[span, :]
        sums_ref[0:1, :] += jnp.sum(second_grad * hat, axis=0, keepdims=True)
        sums_ref[1:2, :] += jnp.sum(second_grad, axis=0, keepdims=True)
        sums_ref[2:3, :] += jnp.sum(og_ref[span, :].astype(F32), axis=0, keepdims=True)
        grad = cot_ref[span, :].astype(F32) + norm_back(second_grad, hat, scale, vec_scr[0:1, :])
        hg_ref[span, :] = grad
        branch = (grad * live).astype(BF)
        branch_scr[span, :] = branch
        cg_ref[span, :] = dot(branch, wo_scr[...], (1, 1)).astype(BF)

    @pl.when(step == 0)
    def _():
        unpack_rows(order, me, own, slice(0, wide), we_scr, chunk)
        unpack_rows(order, me, own, slice(wide, 2 * wide), wr_scr, chunk)
        unpack_rows(order, me, shared, slice(2 * wide, 2 * wide + d), wo_scr, chunk)
        for k in range(2):
            block = 2 * part + k
            eb_scr[:, k * d : (k + 1) * d] = bias_of(block, block * d)
        if first:
            if order.stepped:
                gain = spread_lanes(order, me, shared, tail, 0, 0, chunk, d)
                shift = spread_lanes(order, me, shared, tail, 0, chunk, chunk, d)
            else:
                gain, shift = vec_ref[2:3, :], vec_ref[3:4, :]
            vec_scr[0:1, :] = gain
            vec_scr[1:2, :] = shift
            mix_ref[...] = jnp.zeros_like(mix_ref)
            sg_ref[...] = jnp.zeros_like(sg_ref)
        else:
            in_scr[...] = in_ref[...].T
            if order.stepped:
                vec_scr[0:1, :] = spread_lanes(order, me, shared, tail, 0, 0, chunk, d)
                vec_scr[1:2, :] = spread_lanes(order, me, shared, tail, 0, 2 * chunk, chunk, d)
            else:
                vec_scr[0:1, :] = vec_ref[2:3, :]
                vec_scr[1:2, :] = vec_ref[4:5, :]
            sums_ref[...] = jnp.zeros_like(sums_ref)
        if first:
            for r in range(0, seq, rows):
                open_rows(slice(r, r + rows))
            in_scr[...] = in_ref[...].T

    now = pl.ds(pl.multiple_of(step * d, d), d)
    ffn_block(
        rows, in_ref, og_ref, act_scr, eg_scr, mix_ref, sg_ref, we_scr.at[:, now], wr_scr.at[:, now], eb_scr[:, now]
    )
    esum_ref[:, now] = jnp.sum(eg_scr[...].astype(F32), axis=0, keepdims=True)
    mine = order if first else turned
    grad_scr[...] = dot(in_scr[...], eg_scr[...]).astype(BF)
    pack_rows(mine, me, grad_scr, (lo_ref, hi_ref), now, chunk)
    grad_scr[...] = dot(act_scr[...], og_ref[...], (0, 0)).astype(BF)
    pack_rows(mine, me, grad_scr, (lo_ref, hi_ref), pl.ds(pl.multiple_of(wide + step * d, d), d), chunk)

    if first:
        return

    @pl.when(step == pl.num_programs(0) - 1)
    def _():
        for r in range(0, seq, rows):
            close_rows(slice(r, r + rows))
        grad_scr[:half, :] = dot(ctx0_ref[...], branch_scr[...], (0, 0)).astype(BF)
        grad_scr[half:, :] = dot(ctx1_ref[...], branch_scr[...], (0, 0)).astype(BF)
        pack_rows(order, me, grad_scr, (olo_ref, ohi_ref), slice(0, d), chunk)
        if order.stepped:
            small = jnp.zeros((order.devices, 128), F32)
            for k in range(3):
                small += fold_lanes(order, me, sums_ref[k : k + 1, :], k * chunk, chunk, 128)
            more = jnp.zeros((order.devices, 128), F32)
            for k in range(2):
                now = slice(k * d, (k + 1) * d)
                more += fold_lanes(order, me, esum0_ref[:, now], k * chunk, chunk, 128)
                more += fold_lanes(order, me, esum_ref[:, now], (2 + k) * chunk, chunk, 128)
            block = (place_rows(small, 0, chunk) + place_rows(more, 1, chunk)).astype(BF)
            olo_ref[:, d:] = block[: d // 2]
            ohi_ref[:, d:] = block[d // 2 :]


def attend_back_kernel(
    order,
    seq,
    group,
    me_ref,
    p_ref,
    q_ref,
    cg_ref,
    kx_ref,
    vx_ref,
    in_ref,
    w_ref,
    spread_ref,
    *refs,
):
    last = group == GROUPS - 1
    if last:
        x_ref, fig0_ref, hg_ref, gain_ref, lo_ref, hi_ref, tg_ref, sums_ref = refs[:8]
        dk_scr, dv_scr, dj_scr, j_scr = refs[8:]
    else:
        olo_ref, ohi_ref, lo_ref, hi_ref, fig_ref = refs[:5]
        dk_scr, dv_scr, dj_scr, j_scr = refs[5:]
    d = in_ref.shape[1]
    chunk = d // order.devices
    levels, total, _ = geometry(seq)
    near, _, far_base = split_levels(seq)
    tile = pl.program_id(0)
    lanes = q_ref.shape[1]
    me = me_ref[0]

    @pl.when(tile == 0)
    def _():
        dk_scr[...] = jnp.zeros_like(dk_scr)
        dv_scr[...] = jnp.zeros_like(dv_scr)
        if not last:
            lo_ref[:, 3 * lanes :] = olo_ref[...]
            hi_ref[:, 3 * lanes :] = ohi_ref[...]

    tiles = range(STEP)
    grads, prob_grads, score_grads = [], [], []
    for t in tiles:
        grads.append(split_heads(cg_ref[t * TILE : (t + 1) * TILE, :]))
        prob_grads.append(dot(window_of(vx_ref, tile * STEP + t, levels), grads[t], (1, 1)))
    for t in tiles:
        prob = p_ref[t].astype(F32)
        inner = jnp.sum(prob * prob_grads[t], axis=0, keepdims=True)
        score_grads.append((prob * (prob_grads[t] - inner)).astype(BF))
    for t in tiles:
        now = tile * STEP + t
        query_grad = own_heads(dot(score_grads[t], window_of(kx_ref, now, levels), (0, 0)))
        dj_scr[pl.ds(pl.multiple_of(now * TILE, TILE), TILE), :lanes] = (query_grad * 0.125).astype(BF)
    for t in tiles:
        now = tile * STEP + t
        key_grad = dot(score_grads[t], split_heads(q_ref[t * TILE : (t + 1) * TILE, :]))
        val_grad = dot(p_ref[t], grads[t])
        at = 0
        for v in levels:
            for row, n in v.spans(now):
                dk_scr[pl.ds(row, n), :] += key_grad[at : at + n]
                dv_scr[pl.ds(row, n), :] += val_grad[at : at + n]
                at += n

    @pl.when(tile == pl.num_programs(0) - 1)
    def _():
        pad = levels[0].pad
        for ref, at in ((dk_scr, lanes), (dv_scr, 2 * lanes)):
            far = ref[far_base:total, :].astype(BF)
            for t in range(seq // POOL):
                parts = []
                for v in near:
                    n = POOL // v.factor
                    base = v.base + v.pad + t * n
                    parts.append(ref[base : base + n, :].astype(BF))
                parts.append(far)
                spread = dot(spread_ref[t * POOL : (t + 1) * POOL, :], jnp.concatenate(parts, axis=0))
                whole = ref[pad + t * POOL : pad + (t + 1) * POOL, :] + spread
                dj_scr[t * POOL : (t + 1) * POOL, at : at + lanes] = whole.astype(BF)
        j_scr[...] = dot(in_ref[...], dj_scr[...], (0, 0)).astype(BF)
        mine = order.turned if last else order
        pack_rows(mine, me, j_scr, (lo_ref, hi_ref), slice(0, 3 * lanes), chunk)
        step = 256
        if last:
            gain = gain_ref[0:1, :]
            gains = jnp.zeros((1, d), F32)
            shifts = jnp.zeros((1, d), F32)
        for r in range(0, seq, step):
            fig = sum(
                dot(
                    dj_scr[r : r + step, k * lanes : (k + 1) * lanes],
                    w_ref[:, k * d + group * lanes : k * d + (group + 1) * lanes],
                    (1, 1),
                )
                for k in range(3)
            )
            if not last:
                fig_ref[r : r + step, :] = fig
                continue
            fig = fig + fig0_ref[r : r + step, :]
            hat, scale = normalize(x_ref[r : r + step, :].astype(F32))
            gains += jnp.sum(fig * hat, axis=0, keepdims=True)
            shifts += jnp.sum(fig, axis=0, keepdims=True)
            grad = hg_ref[r : r + step, :] + norm_back(fig, hat, scale, gain)
            tg_ref[r : r + step, :] = grad.astype(BF)
        if last:
            sums_ref[0:1, :] = gains
            sums_ref[1:2, :] = shifts
            if order.stepped:
                folded = fold_lanes(mine, me, gains, 0, chunk, 128)
                folded += fold_lanes(mine, me, shifts, chunk, chunk, 128)
                block = place_rows(folded, 0, chunk).astype(BF)
                lo_ref[:, 3 * lanes :] = block[: d // 2]
                hi_ref[:, 3 * lanes :] = block[d // 2 :]


def whole(shape):
    return pl.BlockSpec(shape, lambda i: (0,) * len(shape))


def smem():
    return pl.BlockSpec(memory_space=pltpu.SMEM)


def launch(name, kernel, steps, ins, outs, scratch, after=(), mib=8, cost=2 * 10**10, aliases=()):
    n = len(ins)

    def body(*refs):
        kernel(*refs[:n], *refs[n + len(after) :])

    return pl.pallas_call(
        body,
        grid=(steps,),
        in_specs=[s for _, s in ins] + [pl.BlockSpec(memory_space=pl.ANY)] * len(after),
        out_specs=[s for _, s in outs],
        out_shape=[o for o, _ in outs],
        scratch_shapes=scratch,
        compiler_params=pltpu.CompilerParams(
            dimension_semantics=("arbitrary",), vmem_limit_bytes=mib * MIB
        ),
        cost_estimate=pl.CostEstimate(flops=cost, bytes_accessed=0, transcendentals=0),
        input_output_aliases=dict(aliases),
        name=name,
    )(*[a for a, _ in ins], *after)


def out(shape, dtype, spec=None):
    return jax.ShapeDtypeStruct(shape, dtype), whole(shape) if spec is None else spec


def in_hbm(shape, dtype):
    return pltpu.HBM(shape, dtype), whole(shape)


def from_hbm(array):
    return pltpu.with_memory_space_constraint(array, pltpu.HBM), whole(array.shape)


def full(array):
    return array, whole(array.shape)


def by_rows(rows, width, column=0):
    return pl.BlockSpec((rows, width), lambda i: (i, column))


def by_columns(rows, width):
    return pl.BlockSpec((rows, width), lambda i: (0, i))


def by_tiles(shape):
    return pl.BlockSpec((STEP, *shape[1:]), lambda i: (i, 0, 0))


def fixed_columns(rows, width, column):
    return pl.BlockSpec((rows, width), lambda i: (0, column))


def prepare(lens, seq, after=()):
    _, _, window = geometry(seq)
    shape = (seq // TILE, window, 128)
    return launch(
        "prepare",
        functools.partial(prepare_kernel, seq),
        seq // TILE // STEP,
        [(lens, smem())],
        [out(shape, F32, by_tiles(shape))],
        [],
        after,
        cost=0,
    )[0]


def by_blocks(source, width, chunk, blocks):
    group = 128 // chunk
    lane = iota((source.shape[0], 128), 1) // chunk
    columns = []
    for at in range(0, blocks * width, 128):
        column = None
        for k in range(group):
            device, block = (at % width) // chunk + k, at // width
            lanes = (device * blocks + block) * chunk
            piece = source[:, lanes // 128 * 128 : lanes // 128 * 128 + 128]
            shift = (k * chunk - lanes) % 128
            if shift:
                piece = pltpu.roll(piece, shift, 1)
            column = piece if column is None else jnp.where(lane == k, piece, column)
        columns.append(column)
    return columns


def from_blocks(parts, width, chunk, blocks):
    group = 128 // chunk
    lane = iota((parts[0].shape[0], 128), 1) // chunk
    columns = []
    for at in range(0, blocks * width, 128):
        column = None
        for k in range(group):
            device, block = divmod(at // chunk + k, blocks)
            lanes = device * chunk
            piece = parts[block][:, lanes // 128 * 128 : lanes // 128 * 128 + 128]
            shift = (k * chunk - lanes) % 128
            if shift:
                piece = pltpu.roll(piece, shift, 1)
            column = piece if column is None else jnp.where(lane == k, piece, column)
        columns.append(column)
    return columns


def pack_kernel(joint_ref, expand_ref, output_ref, reduce_ref, *refs):
    small, (a_ref, e1_ref, e2_ref) = refs[:6], refs[6:]
    chunk, d = output_ref.shape
    wide = joint_ref.shape[1]

    def line(vectors):
        flat = jnp.concatenate([v[...].reshape(1, v.shape[0]).astype(F32) for v in vectors], axis=1)
        gap = jnp.zeros((1, 128 - flat.shape[1]), F32)
        return jnp.concatenate([flat, gap], axis=1)

    def block(parts):
        gap = jnp.zeros((chunk - len(parts), 128), F32)
        return jnp.concatenate(parts + [gap], axis=0).astype(BF)

    a_ref[:, :wide] = joint_ref[...]
    a_ref[:, wide:] = block([line(small[:2])])
    columns = by_blocks(expand_ref[...].astype(F32), d, chunk, 4)
    for i, column in enumerate(columns):
        target = (e1_ref, e2_ref)[i * 128 // (2 * d)]
        at = i * 128 % (2 * d)
        target[:, at : at + 128] = column.astype(BF)
    for k in range(4):
        target = (e1_ref, e2_ref)[k // 2]
        target[:, (2 + k % 2) * d : (3 + k % 2) * d] = reduce_ref[k * chunk : (k + 1) * chunk, :]
    e1_ref[:, 4 * d : 5 * d] = output_ref[...]
    e1_ref[:, 5 * d :] = block([line(small[2:5]), line(small[5:])])


def pack(joint, expand, output, reduce, small):
    rows, wide = joint.shape
    d = output.shape[1]
    return launch(
        "pack",
        pack_kernel,
        1,
        [from_hbm(a) for a in (joint, expand, output, reduce, *small)],
        [out((rows, wide + 128), BF), out((rows, 5 * d + 128), BF), out((rows, 4 * d), BF)],
        [],
        mib=4,
        cost=0,
    )


def finish_kernel(one_ref, two_ref, expand_ref, reduce_ref, output_ref, *small):
    chunk, d = output_ref.shape
    parts = [one_ref[:, :d], one_ref[:, d : 2 * d], two_ref[:, :d], two_ref[:, d : 2 * d]]
    for i, column in enumerate(from_blocks(parts, d, chunk, 4)):
        expand_ref[:, i * 128 : (i + 1) * 128] = column
    for k in range(4):
        source = (one_ref, two_ref)[k // 2]
        reduce_ref[k * chunk : (k + 1) * chunk, :] = source[:, (2 + k % 2) * d : (3 + k % 2) * d]
    at = two_ref.shape[1] - 128
    output_ref[...] = two_ref[:, at - d : at]
    for k in range(3):
        small[k][...] = two_ref[0:1, at + k * chunk : at + (k + 1) * chunk].reshape(chunk)
    small[3][...] = two_ref[1:2, at : at + 4 * chunk].reshape(4 * chunk)


def finish(one, two, after):
    rows, d = one.shape[0], one.shape[1] // 4
    return launch(
        "finish",
        finish_kernel,
        1,
        [full(one), full(two)],
        [out((rows, 4 * d), F32), out((4 * rows, d), F32), out((rows, d), F32)]
        + [out((rows,), F32)] * 3
        + [out((4 * rows,), F32)],
        [],
        after,
    )


def close_kernel(lanes, before_ref, keep_ref, other_ref, joint_ref, gain_ref, shift_ref):
    total = keep_ref[...].astype(F32) + other_ref[...].astype(F32)
    chunk, d = joint_ref.shape[0], joint_ref.shape[1] // 3
    at = 4 * d
    for k in range(3):
        joint_ref[:, k * d : k * d + lanes] = before_ref[:, at + k * lanes : at + (k + 1) * lanes]
        joint_ref[:, k * d + lanes : (k + 1) * d] = total[:, k * lanes : (k + 1) * lanes]
    gain_ref[...] = total[0:1, 3 * lanes : 3 * lanes + chunk].reshape(chunk)
    shift_ref[...] = total[0:1, 3 * lanes + chunk : 3 * lanes + 2 * chunk].reshape(chunk)


def close(before, pair, d):
    rows = before.shape[0]
    return launch(
        "close",
        functools.partial(close_kernel, d // GROUPS),
        1,
        [full(before), full(pair[0]), full(pair[1])],
        [out((rows, 3 * d), F32)] + [out((rows,), F32)] * 2,
        [],
        cost=0,
    )


def merge_kernel(plan, *refs):
    n = sum(1 if kind == "carry" else 2 * count for kind, count in plan)
    ins, outs = list(refs[:n]), list(refs[n:])
    for kind, count in plan:
        if kind == "carry":
            outs.pop(0)[...] = ins.pop(0)[...]
            continue
        targets = [outs.pop(0) for _ in range(2 if kind == "add" else 1)]
        at = 0
        for _ in range(count):
            first, second = ins.pop(0), ins.pop(0)
            rows, width = first.shape
            columns = slice(at, at + width)
            at += width
            if kind == "join":
                targets[0][:rows, columns] = first[...]
                targets[0][rows:, columns] = second[...]
                continue
            total = first[...].astype(F32) + second[...].astype(F32)
            if kind == "last":
                targets[0][:, columns] = total
                continue
            targets[0][:, columns] = total[: rows // 2].astype(BF)
            targets[1][:, columns] = total[rows // 2 :].astype(BF)


def merge(plan, arrays, after):
    outs = []
    for (kind, _), pairs in zip(plan, arrays, strict=True):
        rows = pairs[0][0].shape[0]
        width = sum(p[0].shape[1] for p in pairs)
        if kind == "carry":
            outs.append(out((rows, width), pairs[0][0].dtype))
        elif kind == "join":
            outs.append(out((2 * rows, width), BF))
        elif kind == "last":
            outs.append(out((rows, width), F32))
        else:
            outs += [out((rows // 2, width), BF)] * 2
    return launch(
        "merge",
        functools.partial(merge_kernel, plan),
        1,
        [full(a) for pairs in arrays for pair in pairs for a in pair],
        outs,
        [],
        after,
        cost=0,
    )


def attend(order, me, group, bias, x, weights, vec, after=()):
    seq, d = x.shape
    lanes = d // GROUPS
    _, total, window = geometry(seq)
    tiles = seq // TILE
    cols = lanes // DIM * TILE
    near, _, far_base = split_levels(seq)
    scratch = [
        pltpu.VMEM((sum(POOL // v.factor for v in near), POOL), BF),
        pltpu.VMEM((total - far_base, seq), BF),
    ]
    ins = [(me, smem()), (bias, by_tiles(bias.shape))]
    if group == 0:
        ins.append(from_hbm(x))
    else:
        ins.append(full(x))
    ins += [full(w) for w in weights]
    outs = [
        out((tiles, window, cols), BF, by_tiles((tiles, window, cols))),
        out((seq, lanes), BF, by_rows(STEP * TILE, lanes)),
        out((seq, lanes), BF),
        out((total, lanes), BF),
        out((total, lanes), BF),
    ]
    if group == 0:
        ins.append(full(vec))
        outs += [out((seq, d), BF), out((d, 3 * d), BF), out((8, d), F32)]
    return launch(
        "attend",
        functools.partial(attend_kernel, order, seq, group),
        tiles // STEP,
        ins,
        outs,
        scratch,
        after,
        cost=2 * 10**10 if group == 0 else 0,
    )


def ffn_scratch(seq, d):
    return [
        pltpu.VMEM((d, 2 * d), BF),
        pltpu.VMEM((d, 2 * d), BF),
        pltpu.VMEM((d, d), BF),
        pltpu.VMEM((1, 2 * d), F32),
        pltpu.VMEM((d, seq), BF),
        pltpu.VMEM((seq, d), BF),
        pltpu.VMEM((seq, d), BF),
        pltpu.VMEM((d, d), BF),
        pltpu.VMEM((8, d), F32),
    ]


def ffn_first(order, me, lens, x, cot, ctx0, ctx1, e1, vec, ebias, after=()):
    seq, d = x.shape
    return launch(
        "ffn_first",
        functools.partial(ffn_kernel, order, 0),
        2,
        [(me, smem()), (lens, smem())]
        + [full(a) for a in (x, cot, ctx0, ctx1, *e1, vec, ebias)],
        [
            out((seq, d), F32),
            out((seq, d), BF),
            out((seq, d), BF),
            out((seq, d), F32),
            out((seq, d), F32),
            out((1, 2 * d), F32),
            out((d // 2, 4 * d), BF),
            out((d // 2, 4 * d), BF),
        ],
        ffn_scratch(seq, d),
        after,
        mib=12,
    )


def ffn_second(order, me, lens, cot, kept, ctx0, ctx1, e1, e2, vec, ebias, after=()):
    seq, d = cot.shape
    width = d + (128 if order.stepped else 0)
    return launch(
        "ffn_second",
        functools.partial(ffn_kernel, order, 1),
        2,
        [(me, smem()), (lens, smem())]
        + [full(a) for a in (cot, *kept, ctx0, ctx1, *e1, *e2, vec, ebias)],
        [
            in_hbm((seq, d), BF),
            out((seq, d), F32),
            out((seq, d), BF),
            out((d // 2, 4 * d), BF),
            out((d // 2, 4 * d), BF),
            out((d // 2, width), BF),
            out((d // 2, width), BF),
            out((8, d), F32),
            out((1, 2 * d), F32),
            out((seq, d), F32),
            out((seq, d), F32),
        ],
        ffn_scratch(seq, d) + [pltpu.VMEM((seq, d), BF)],
        after,
        aliases={3: 1, 6: 9, 7: 10},
        mib=14,
    )


def attend_back(order, me, group, prob, q, cg, kx, vx, first_in, weights, more, after=()):
    seq, d = first_in.shape
    lanes = d // GROUPS
    levels, total, _ = geometry(seq)
    spread = spreading(seq)
    last = group == GROUPS - 1
    extra = (128 if order.stepped else 0) if last else more[0].shape[1]
    ins = [
        (me, smem()),
        (prob, by_tiles(prob.shape)),
        (q, by_rows(STEP * TILE, lanes)),
        (cg, by_rows(STEP * TILE, lanes, group)),
        full(kx),
        full(vx),
        full(first_in),
        full(weights),
        full(jnp.asarray(spread, BF)),
    ]
    ins += [full(a) for a in more]
    outs = [out((d // 2, 3 * lanes + extra), BF)] * 2
    if last:
        outs += [in_hbm((seq, d), BF), out((8, d), F32)]
    else:
        outs.append(out((seq, d), F32))
    return launch(
        "attend_back",
        functools.partial(attend_back_kernel, order, seq, group),
        prob.shape[0] // STEP,
        ins,
        outs,
        [
            pltpu.VMEM((total, lanes), F32),
            pltpu.VMEM((total, lanes), F32),
            pltpu.VMEM((seq, 3 * lanes), BF),
            pltpu.VMEM((d, 3 * lanes), BF),
        ],
        after,
        mib=17,
    )


class Gather:
    def __init__(self, order, value):
        self.order, self.bits, self.have, self.other = order, list(order.bits), value, None
        if not order.stepped:
            half = value.shape[0] // 2
            self.have, self.other, self.bits = value[:half], value[half:], []

    def send(self):
        if self.bits:
            self.other = swap(self.order, self.have, self.bits.pop(0))

    def kind(self):
        return "join", 1

    def pairs(self):
        return [(self.have, self.other)]

    def pair(self):
        return self.have, self.other

    def take(self, outs):
        self.have = outs.pop(0)


class Scatter:
    def __init__(self, order, halves):
        self.order, self.bits, self.halves, self.other = order, order.bits[::-1], halves, None
        self.done = None
        self.beside = []
        if not order.stepped:
            self.done = jnp.concatenate(halves, axis=0).astype(F32)

    def send(self):
        if self.order.stepped:
            self.other = swap(self.order, self.halves[1], self.bits.pop(0))

    def kind(self):
        return "add" if self.bits else "last", 1 + len(self.beside)

    def pairs(self):
        return [(self.halves[0], self.other)] + self.beside

    def absorb(self, chain):
        if self.order.stepped:
            self.beside += chain.pairs()

    def take(self, outs):
        self.beside = []
        if self.bits:
            self.halves = outs.pop(0), outs.pop(0)
        else:
            self.done = outs.pop(0)


def swap(order, value, bit):
    return lax.ppermute(value, AXES, [(i, i ^ bit) for i in range(order.devices)])


def advance(order, chains, after=(), carry=None):
    if not order.stepped:
        return () if carry is None else ((), carry)
    plan = [c.kind() for c in chains]
    arrays = [c.pairs() for c in chains]
    if carry is not None:
        plan.append(("carry", 1))
        arrays.append([(carry,)])
    outs = list(merge(plan, arrays, after))
    marks = tuple(outs)
    if carry is not None:
        carry = outs.pop()
    for c in chains:
        c.take(outs)
        if c.bits:
            c.send()
    return marks[:1] if carry is None else (marks[:1], carry)


def local(order, me, tokens, cotangent, lens, joint_w, output_w, expand_w, reduce_w,
          attn_gain, attn_shift, ffn_gain, ffn_shift, expand_bias, reduce_bias):
    seq, d = tokens.shape
    lanes = d // GROUPS
    rows = joint_w.shape[0]
    ff = expand_w.shape[1]
    vec = jnp.zeros((8, d), F32)
    ebias = jnp.zeros((1, ff), F32)
    if order.stepped:
        small = [attn_gain, attn_shift, ffn_gain, ffn_shift, reduce_bias, expand_bias]
        first, second, third = pack(joint_w, expand_w, output_w, reduce_w, small)
        joint = Gather(order, first)
        e1 = Gather(order, second)
        e2 = Gather(order, third)
    else:
        small = [attn_gain, attn_shift, ffn_gain, ffn_shift, reduce_bias]
        small = [lax.all_gather(v, AXES, tiled=True) for v in small]
        vec = jnp.pad(jnp.stack(small), ((0, 3), (0, 0))).astype(F32)
        ebias = lax.all_gather(expand_bias, AXES, tiled=True)[None].astype(F32)
        e, o, r = [lax.all_gather(w, AXES, axis=0, tiled=True) for w in (expand_w, output_w, reduce_w)]
        r = [r[k * d : (k + 1) * d] for k in range(4)]
        joint = Gather(order, lax.all_gather(joint_w, AXES, axis=0, tiled=True))
        e1 = Gather(order, jnp.concatenate([e[:, : 2 * d], r[0], r[1], o], axis=1))
        e2 = Gather(order, jnp.concatenate([e[:, 2 * d :], r[2], r[3]], axis=1))
    joint.send()
    mark = advance(order, [joint])
    e1.send()
    mark = advance(order, [joint, e1], mark)
    e2.send()
    mark = advance(order, [joint, e1, e2], mark)
    bias = prepare(lens, seq, mark)
    mark = advance(order, [joint, e1, e2], (bias,))
    p0, ctx0, q0, kx0, vx0, first_in, w, gain = attend(order, me, 0, bias, tokens, joint.pair(), vec, mark)
    p1, ctx1, q1, kx1, vx1 = attend(order, me, 1, bias, first_in, (w,), vec, (ctx0,))
    mark = advance(order, [e1, e2], (ctx1,))
    *kept, lo, hi = ffn_first(
        order, me, lens, tokens, cotangent, ctx0, ctx1, e1.pair(), vec, ebias, mark
    )
    t1 = Scatter(order, (lo, hi))
    mark = advance(order, [e2], (lo,))
    t1.send()
    mark = advance(order, [t1], mark)
    mixed, hg, cg, lo, hi, olo, ohi, sums, esum, _, _ = ffn_second(
        order, me, lens, cotangent, kept, ctx0, ctx1, e1.pair(), e2.pair(), vec, ebias, mark
    )
    mark = advance(order, [t1], (cg,))
    t2 = Scatter(order.turned, (lo, hi))
    t2.send()
    lo, hi, fig = attend_back(order, me, 0, p0, q0, cg, kx0, vx0, first_in, w, (olo, ohi), mark)
    mark, hi = advance(order, [t1, t2], (fig,), hi)
    j0 = Scatter(order, (lo, hi))
    j0.send()
    mark = advance(order, [j0], mark)
    lo, hi, token_grad, tail_sums = attend_back(
        order, me, 1, p1, q1, cg, kx1, vx1, first_in, w, (tokens, fig, hg, gain), mark
    )
    mark, hi = advance(order, [t1, t2, j0], (tail_sums,), hi)
    j1 = Scatter(order.turned, (lo, hi))
    j1.send()
    mark = advance(order, [j1], mark)
    t2.absorb(j0)
    mark = advance(order, [t2, t1], mark)
    mark = advance(order, [j1], mark)
    mark = advance(order, [t2], mark)
    mark = advance(order, [j1], mark)
    mark = advance(order, [j1], mark)
    if order.stepped:
        advance(order, [t2], mark)
        expand_grad, reduce_grad, output_grad, *small = finish(t1.done, t2.done, mark)
        joint_grad, *first_small = close(t2.done, j1.pairs()[0], d)
        small = [*first_small, small[0], small[1], small[3], small[2]]
    else:
        parts = []
        for k in range(3):
            parts += [c.done[:, k * lanes : (k + 1) * lanes] for c in (j0, j1)]
        joint_grad = jnp.concatenate(parts, axis=1)
        one, two = t1.done, t2.done
        expand_grad = lax.psum_scatter(
            jnp.concatenate([one[:, : 2 * d], two[:, : 2 * d]], axis=1), AXES, scatter_dimension=0, tiled=True
        )
        reduce_grad = lax.psum_scatter(
            jnp.concatenate([t[:, k * d : (k + 1) * d] for t in (one, two) for k in (2, 3)], axis=0),
            AXES,
            scatter_dimension=0,
            tiled=True,
        )
        output_grad = lax.psum_scatter(j0.done[:, 3 * lanes :], AXES, scatter_dimension=0, tiled=True)
        joint_grad = lax.psum_scatter(joint_grad, AXES, scatter_dimension=0, tiled=True)
        esums = jnp.concatenate([kept[5][0], esum[0]])
        vectors = [tail_sums[0], tail_sums[1], sums[0], sums[1], esums, sums[2]]
        small = [lax.psum_scatter(v, AXES, scatter_dimension=0, tiled=True) for v in vectors]
    return (mixed, token_grad, joint_grad, output_grad, expand_grad, reduce_grad, *small)


def shards(order, *args):
    sub = lax.axis_size("sub")
    me = (lax.axis_index("dp") * sub + lax.axis_index("sub")).astype(jnp.int32).reshape(1)
    return local(order, me, *args)


def solution(mesh):
    order = Order(math.prod(mesh.shape[a] for a in AXES))
    wide = P(AXES, None)
    flat = P(AXES)
    return jax.shard_map(
        functools.partial(shards, order),
        mesh=mesh,
        in_specs=(wide,) * 7 + (flat,) * 6,
        out_specs=(wide,) * 6 + (flat,) * 6,
        check_vma=False,
    )
```

```python
import functools
import math

import jax
import jax.numpy as jnp
import numpy as np
from jax import lax
from jax.experimental import pallas as pl
from jax.experimental.pallas import tpu as pltpu
from jax.sharding import PartitionSpec as P

HEADS = 8
BLOCK = 16
LEVELS = 7
TILE = 64
POOL = 128
GROUPS = 2
DIM = 64
STEP = 8
LOG_TWO = math.log(2.0)
NEGATIVE = -1e30
ROOT_HALF = 1.0 / math.sqrt(2.0)
DENSITY = 1.0 / math.sqrt(2.0 * math.pi)
AXES = ("dp", "sub")
BF = jnp.bfloat16
F32 = jnp.float32
MIB = 1 << 20


class Level:
    def __init__(self, level, seq, base):
        self.level = level
        self.factor = 1 << level
        self.count = seq // self.factor
        self.width = BLOCK * self.factor
        self.blocks = seq // self.width
        self.pad = BLOCK if self.blocks > 2 else 0
        self.base = base
        self.rows = self.count + 2 * self.pad

    def pieces(self, tile):
        if self.width < TILE:
            return [(tile * (TILE // self.factor), TILE // self.factor + 2 * BLOCK)]
        block = tile // (self.width // TILE)
        if self.blocks > 2:
            return [(block * BLOCK, BLOCK), ((block + 2) * BLOCK, BLOCK)]
        return [((self.blocks - 1 - block) * BLOCK, BLOCK)]

    def spans(self, tile):
        return [(pl.multiple_of(self.base + first, BLOCK), n) for first, n in self.pieces(tile)]


def geometry(seq):
    levels, base = [], 0
    for level in range(LEVELS):
        levels.append(Level(level, seq, base))
        base += levels[-1].rows
    return levels, base, sum(n for v in levels for _, n in v.pieces(0))


def split_levels(seq):
    levels, _, _ = geometry(seq)
    near = [v for v in levels[1:] if v.width <= POOL]
    far = [v for v in levels[1:] if v.width > POOL]
    return near, far, far[0].base


def spreading(seq):
    levels, total, _ = geometry(seq)
    near, far, far_base = split_levels(seq)
    near_rows = sum(POOL // v.factor for v in near)
    spread = np.zeros((seq, near_rows + total - far_base), np.float32)
    at = 0
    for v in near:
        for t in range(seq):
            spread[t, at + t % POOL // v.factor] = 1.0 / v.factor
        at += POOL // v.factor
    for v in far:
        for t in range(seq):
            spread[t, near_rows + v.base - far_base + v.pad + t // v.factor] = 1.0 / v.factor
    return spread


class Order:
    def __init__(self, devices, turned=False):
        self.devices = devices
        self.bits = [1 << k for k in reversed(range(devices.bit_length() - 1))]
        self.stepped = devices == 32
        if not turned:
            self.turned = Order(devices, True)
        elif self.stepped:
            self.bits[-3:-1] = self.bits[-2], self.bits[-3]

    def flip(self, p):
        value = 0
        for k, bit in enumerate(self.bits):
            value = value + ((p >> k) & 1) * bit
        return value


def dot(left, right, contract=(1, 0)):
    return lax.dot_general(
        left, right, (((contract[0],), (contract[1],)), ((), ())), preferred_element_type=F32
    )


def iota(shape, axis):
    return lax.broadcasted_iota(jnp.int32, shape, axis)


def unpack_rows(order, me, halves, columns, target, chunk, places=slice(None)):
    rows = halves[0].shape[0]
    if not order.stepped:
        target[:rows, places] = halves[0][:, columns]
        target[rows:, places] = halves[1][:, columns]
        return
    for p in range(order.devices):
        half, at = divmod(p * chunk, rows)
        row = pl.multiple_of((me ^ order.flip(p)) * chunk, chunk)
        target[pl.ds(row, chunk), places] = halves[half][at : at + chunk, columns]


def pack_rows(order, me, source, halves, columns, chunk):
    rows = halves[0].shape[0]
    if not order.stepped:
        halves[0][:, columns] = source[:rows]
        halves[1][:, columns] = source[rows:]
        return
    for p in range(order.devices):
        half, at = divmod(p * chunk, rows)
        row = pl.multiple_of((me ^ order.flip(p)) * chunk, chunk)
        halves[half][at : at + chunk, columns] = source[pl.ds(row, chunk), :]


def owners(order, me, shape):
    return me ^ order.flip(iota(shape, 0))


def spread_lanes(order, me, halves, columns, row, offset, chunk, total):
    n = order.devices
    block = jnp.concatenate([half[:, columns] for half in halves], axis=0)
    step = block.shape[0] // n
    pick = (iota((n, block.shape[0]), 1) == iota((n, block.shape[0]), 0) * step + row).astype(BF)
    rows = dot(pick, block).astype(BF)
    lanes = block.shape[1]
    place = (iota((lanes, total), 0) == iota((lanes, total), 1) % chunk + offset).astype(BF)
    wide = dot(rows, place)
    mine = iota((n, total), 1) // chunk == owners(order, me, (n, total))
    return jnp.sum(jnp.where(mine, wide, 0.0), axis=0, keepdims=True)


def fold_lanes(order, me, vector, offset, chunk, lanes):
    n, total = order.devices, vector.shape[1]
    mine = iota((n, total), 1) // chunk == owners(order, me, (n, total))
    wide = jnp.where(mine, vector, 0.0).astype(BF)
    place = (iota((total, lanes), 1) == iota((total, lanes), 0) % chunk + offset).astype(BF)
    return dot(wide, place)


def place_rows(rows, row, step):
    n = rows.shape[0]
    pick = (iota((n * step, n), 0) == iota((n * step, n), 1) * step + row).astype(BF)
    return dot(pick, rows.astype(BF))


def live_column(lens, first, rows):
    position = first + iota((rows, 1), 0)
    start, live = 0, jnp.zeros((rows, 1), jnp.bool_)
    for i in range(lens.shape[1]):
        length = lens[0, i]
        live = live | ((position >= start) & (position < start + length))
        start = start + (length + BLOCK - 1) // BLOCK * BLOCK
    return live


def tile_bias(lens, tile, levels, copies):
    position = tile * TILE + iota((1, copies * TILE), 1) % TILE
    low, high, start = position, position + 1, 0
    for i in range(lens.shape[1]):
        length = lens[0, i]
        inside = (position >= start) & (position < start + length)
        low = jnp.where(inside, start, low)
        high = jnp.where(inside, start + length, high)
        start = start + (length + BLOCK - 1) // BLOCK * BLOCK
    parts = []
    for v in levels:
        reach = (position // v.width - 1) * v.width
        least = jnp.maximum(low, reach)
        most = jnp.minimum(high - v.factor, reach + 3 * v.width - 1)
        half = v.width // 2
        lower = (position // half - 1) * half
        for first, rows in v.pieces(tile):
            begin = (first - v.pad + iota((rows, copies * TILE), 0)) * v.factor
            valid = (begin >= least) & (begin <= most)
            if v.level > 0:
                valid = valid & ((begin < lower) | (begin >= lower + 3 * half))
            parts.append(jnp.where(valid, v.level * LOG_TWO, NEGATIVE))
    return jnp.concatenate(parts, axis=0)


def window_of(ref, tile, levels):
    return jnp.concatenate([ref[pl.ds(at, n), :] for v in levels for at, n in v.spans(tile)], axis=0)


def split_heads(rows):
    head = iota(rows.shape, 1) // DIM
    zero = jnp.zeros_like(rows)
    return jnp.concatenate([jnp.where(head == h, rows, zero) for h in range(rows.shape[1] // DIM)], axis=0)


def own_heads(full):
    heads = full.shape[1] // DIM
    head = iota((TILE, full.shape[1]), 1) // DIM
    own = full[:TILE]
    for h in range(1, heads):
        own = jnp.where(head == h, full[h * TILE : (h + 1) * TILE], own)
    return own


def normalize(values):
    centre = values - jnp.mean(values, axis=-1, keepdims=True)
    scale = lax.rsqrt(jnp.mean(centre * centre, axis=-1, keepdims=True) + 1e-05)
    return centre * scale, scale


def norm_back(grad, normed, scale, gain):
    scaled = grad * gain
    return scale * (
        scaled
        - jnp.mean(scaled, axis=-1, keepdims=True)
        - normed * jnp.mean(scaled * normed, axis=-1, keepdims=True)
    )


def prepare_kernel(seq, lens_ref, bias_ref):
    levels, _, _ = geometry(seq)
    step = pl.program_id(0)
    for t in range(STEP):
        bias_ref[t] = tile_bias(lens_ref, step * STEP + t, levels, bias_ref.shape[2] // TILE)


def means(seq, fine_ref, wide_ref):
    near, far, far_base = split_levels(seq)
    at = 0
    for v in near:
        n = POOL // v.factor
        same = iota((n, POOL), 1) // v.factor == iota((n, POOL), 0)
        fine_ref[at : at + n, :] = jnp.where(same, 1.0 / v.factor, 0.0).astype(BF)
        at += n
    for v in far:
        same = iota((v.rows, seq), 1) // v.factor == iota((v.rows, seq), 0) - v.pad
        base = v.base - far_base
        wide_ref[base : base + v.rows, :] = jnp.where(same, 1.0 / v.factor, 0.0).astype(BF)


def attend_kernel(order, seq, group, me_ref, bias_ref, x_ref, *refs):
    first_group = group == 0
    if first_group:
        lo_ref, hi_ref, vec_ref = refs[:3]
        p_ref, ctx_ref, q_ref, kx_ref, vx_ref, in_ref, w_ref, gain_ref = refs[3:11]
        fine_ref, wide_ref = refs[11:]
    else:
        w_ref, p_ref, ctx_ref, q_ref, kx_ref, vx_ref, fine_ref, wide_ref = refs
    levels, total, _ = geometry(seq)
    near, _, far_base = split_levels(seq)
    tile = pl.program_id(0)
    lanes = q_ref.shape[1]
    me = me_ref[0]

    @pl.when(tile == 0)
    def _():
        d = x_ref.shape[1]
        means(seq, fine_ref, wide_ref)
        if first_group:
            chunk = d // order.devices
            unpack_rows(order, me, (lo_ref, hi_ref), slice(0, 3 * d), w_ref, chunk)
            if order.stepped:
                tail = slice(3 * d, 3 * d + 128)
                gain = spread_lanes(order, me, (lo_ref, hi_ref), tail, 0, 0, chunk, d)
                shift = spread_lanes(order, me, (lo_ref, hi_ref), tail, 0, chunk, chunk, d)
            else:
                gain, shift = vec_ref[0:1, :], vec_ref[1:2, :]
            gain_ref[...] = jnp.broadcast_to(gain, gain_ref.shape)
        kx_ref[...] = jnp.zeros_like(kx_ref)
        vx_ref[...] = jnp.zeros_like(vx_ref)
        step = 256
        pad = levels[0].pad
        for r in range(0, seq, step):
            if first_group:
                hat, _ = normalize(x_ref[r : r + step, :].astype(F32))
                first_in = (hat * gain + shift).astype(BF)
                in_ref[r : r + step, :] = first_in
            else:
                first_in = x_ref[r : r + step, :]
            query, keys, vals = [
                dot(first_in, w_ref[:, k * d + group * lanes : k * d + (group + 1) * lanes]).astype(BF)
                for k in range(3)
            ]
            q_ref[r : r + step, :] = query * jnp.asarray(0.125, BF)
            kx_ref[pad + r : pad + r + step, :] = keys
            vx_ref[pad + r : pad + r + step, :] = vals
        for ref in (kx_ref, vx_ref):
            for t in range(seq // POOL):
                rows = ref[pad + t * POOL : pad + (t + 1) * POOL, :]
                pooled = dot(fine_ref[...], rows).astype(BF)
                at = 0
                for v in near:
                    n = POOL // v.factor
                    ref[v.base + v.pad + t * n : v.base + v.pad + (t + 1) * n, :] = pooled[at : at + n]
                    at += n
            ref[far_base:total, :] = dot(wide_ref[...], ref[pad : pad + seq, :]).astype(BF)

    tiles = range(STEP)
    scores = []
    for t in tiles:
        at = tile * STEP + t
        query = split_heads(q_ref[pl.ds(pl.multiple_of(at * TILE, TILE), TILE), :])
        scores.append(dot(window_of(kx_ref, at, levels), query, (1, 1)))
    probs = []
    for t in tiles:
        bias = jnp.concatenate([bias_ref[t]] * (scores[t].shape[1] // bias_ref.shape[2]), axis=1)
        score = scores[t] + bias
        peak = jnp.max(score, axis=0, keepdims=True)
        weight = jnp.exp(score - peak)
        share = 1.0 / jnp.sum(weight, axis=0, keepdims=True)
        probs.append((weight * share).astype(BF))
        p_ref[t] = probs[t]
    for t in tiles:
        context = dot(probs[t], window_of(vx_ref, tile * STEP + t, levels), (0, 0))
        ctx_ref[t * TILE : (t + 1) * TILE, :] = own_heads(context).astype(BF)


def ffn_block(rows, in_ref, og_ref, act_scr, eg_scr, mix_ref, sg_ref, we, wr, bias):
    for r in range(0, in_ref.shape[0], rows):
        part = slice(r, r + rows)
        expanded = dot(in_ref[part, :], we[...]) + bias
        phi = 0.5 * (1.0 + lax.erf(expanded * ROOT_HALF))
        activated = (expanded * phi).astype(BF)
        act_scr[part, :] = activated
        slope = phi + expanded * (jnp.exp(-0.5 * expanded * expanded) * DENSITY)
        expanded_grad = (dot(og_ref[part, :], wr[...], (1, 1)) * slope).astype(BF)
        eg_scr[part, :] = expanded_grad
        mix_ref[part, :] += dot(activated, wr[...])
        sg_ref[part, :] += dot(expanded_grad, we[...], (1, 1))


def ffn_kernel(order, part, me_ref, lens_ref, *refs):
    first = part == 0
    if first:
        x_ref, cot_ref, ctx0_ref, ctx1_ref, lo1_ref, hi1_ref, vec_ref, ebias_ref = refs[:8]
        hidden_ref, in_ref, og_ref, mix_ref, sg_ref, esum_ref, lo_ref, hi_ref = refs[8:16]
        own = (lo1_ref, hi1_ref)
        we_scr, wr_scr, wo_scr, eb_scr, in_scr, act_scr, eg_scr, grad_scr, vec_scr = refs[16:]
    else:
        cot_ref, hidden_ref, in_ref, og_ref, _, _, esum0_ref, ctx0_ref, ctx1_ref = refs[:9]
        lo1_ref, hi1_ref, lo2_ref, hi2_ref, vec_ref, ebias_ref = refs[9:15]
        mixed_ref, hg_ref, cg_ref, lo_ref, hi_ref, olo_ref, ohi_ref, sums_ref, esum_ref, mix_ref, sg_ref = refs[15:26]
        own = (lo2_ref, hi2_ref)
        we_scr, wr_scr, wo_scr, eb_scr, in_scr, act_scr, eg_scr, grad_scr, vec_scr, branch_scr = refs[26:]
    step = pl.program_id(0)
    me = me_ref[0]
    seq, d = cot_ref.shape
    rows = 512
    chunk = d // order.devices
    wide = 2 * d
    shared = (lo1_ref, hi1_ref)
    turned = order.turned
    half = ctx0_ref.shape[1]
    tail = slice(5 * d, 5 * d + 128)

    def bias_of(block, at):
        if order.stepped:
            return spread_lanes(order, me, shared, tail, 1, block * chunk, chunk, d)
        return ebias_ref[:, at : at + d]

    def live_rows(span):
        return live_column(lens_ref, span.start, rows).astype(F32)

    def open_rows(span):
        live = live_rows(span)
        out = dot(ctx0_ref[span, :], wo_scr[:half, :]) + dot(ctx1_ref[span, :], wo_scr[half:, :])
        hidden = x_ref[span, :].astype(F32) + live * out
        hidden_ref[span, :] = hidden
        hat, _ = normalize(hidden)
        in_ref[span, :] = (hat * vec_scr[0:1, :] + vec_scr[1:2, :]).astype(BF)
        og_ref[span, :] = (cot_ref[span, :].astype(F32) * live).astype(BF)

    def close_rows(span):
        live = live_rows(span)
        hidden = hidden_ref[span, :]
        mixed_ref[span, :] = (hidden + live * (mix_ref[span, :] + vec_scr[1:2, :])).astype(BF)
        hat, scale = normalize(hidden)
        second_grad = sg_ref[span, :]
        sums_ref[0:1, :] += jnp.sum(second_grad * hat, axis=0, keepdims=True)
        sums_ref[1:2, :] += jnp.sum(second_grad, axis=0, keepdims=True)
        sums_ref[2:3, :] += jnp.sum(og_ref[span, :].astype(F32), axis=0, keepdims=True)
        grad = cot_ref[span, :].astype(F32) + norm_back(second_grad, hat, scale, vec_scr[0:1, :])
        hg_ref[span, :] = grad
        branch = (grad * live).astype(BF)
        branch_scr[span, :] = branch
        cg_ref[span, :] = dot(branch, wo_scr[...], (1, 1)).astype(BF)

    @pl.when(step == 0)
    def _():
        unpack_rows(order, me, own, slice(0, wide), we_scr, chunk)
        unpack_rows(order, me, own, slice(wide, 2 * wide), wr_scr, chunk)
        unpack_rows(order, me, shared, slice(2 * wide, 2 * wide + d), wo_scr, chunk)
        for k in range(2):
            block = 2 * part + k
            eb_scr[:, k * d : (k + 1) * d] = bias_of(block, block * d)
        if first:
            if order.stepped:
                gain = spread_lanes(order, me, shared, tail, 0, 0, chunk, d)
                shift = spread_lanes(order, me, shared, tail, 0, chunk, chunk, d)
            else:
                gain, shift = vec_ref[2:3, :], vec_ref[3:4, :]
            vec_scr[0:1, :] = gain
            vec_scr[1:2, :] = shift
            mix_ref[...] = jnp.zeros_like(mix_ref)
            sg_ref[...] = jnp.zeros_like(sg_ref)
        else:
            in_scr[...] = in_ref[...].T
            if order.stepped:
                vec_scr[0:1, :] = spread_lanes(order, me, shared, tail, 0, 0, chunk, d)
                vec_scr[1:2, :] = spread_lanes(order, me, shared, tail, 0, 2 * chunk, chunk, d)
            else:
                vec_scr[0:1, :] = vec_ref[2:3, :]
                vec_scr[1:2, :] = vec_ref[4:5, :]
            sums_ref[...] = jnp.zeros_like(sums_ref)
        if first:
            for r in range(0, seq, rows):
                open_rows(slice(r, r + rows))
            in_scr[...] = in_ref[...].T

    now = pl.ds(pl.multiple_of(step * d, d), d)
    ffn_block(
        rows, in_ref, og_ref, act_scr, eg_scr, mix_ref, sg_ref, we_scr.at[:, now], wr_scr.at[:, now], eb_scr[:, now]
    )
    esum_ref[:, now] = jnp.sum(eg_scr[...].astype(F32), axis=0, keepdims=True)
    mine = order if first else turned
    grad_scr[...] = dot(in_scr[...], eg_scr[...]).astype(BF)
    pack_rows(mine, me, grad_scr, (lo_ref, hi_ref), now, chunk)
    grad_scr[...] = dot(act_scr[...], og_ref[...], (0, 0)).astype(BF)
    pack_rows(mine, me, grad_scr, (lo_ref, hi_ref), pl.ds(pl.multiple_of(wide + step * d, d), d), chunk)

    if first:
        return

    @pl.when(step == pl.num_programs(0) - 1)
    def _():
        for r in range(0, seq, rows):
            close_rows(slice(r, r + rows))
        grad_scr[:half, :] = dot(ctx0_ref[...], branch_scr[...], (0, 0)).astype(BF)
        grad_scr[half:, :] = dot(ctx1_ref[...], branch_scr[...], (0, 0)).astype(BF)
        pack_rows(order, me, grad_scr, (olo_ref, ohi_ref), slice(0, d), chunk)
        if order.stepped:
            small = jnp.zeros((order.devices, 128), F32)
            for k in range(3):
                small += fold_lanes(order, me, sums_ref[k : k + 1, :], k * chunk, chunk, 128)
            more = jnp.zeros((order.devices, 128), F32)
            for k in range(2):
                now = slice(k * d, (k + 1) * d)
                more += fold_lanes(order, me, esum0_ref[:, now], k * chunk, chunk, 128)
                more += fold_lanes(order, me, esum_ref[:, now], (2 + k) * chunk, chunk, 128)
            block = (place_rows(small, 0, chunk) + place_rows(more, 1, chunk)).astype(BF)
            olo_ref[:, d:] = block[: d // 2]
            ohi_ref[:, d:] = block[d // 2 :]


def attend_back_kernel(
    order,
    seq,
    group,
    me_ref,
    p_ref,
    q_ref,
    cg_ref,
    kx_ref,
    vx_ref,
    in_ref,
    w_ref,
    spread_ref,
    *refs,
):
    last = group == GROUPS - 1
    if last:
        x_ref, fig0_ref, lo_ref, hi_ref, fig_ref, sums_ref = refs[:6]
        dk_scr, dv_scr, dj_scr, j_scr = refs[6:]
    else:
        olo_ref, ohi_ref, lo_ref, hi_ref, fig_ref = refs[:5]
        dk_scr, dv_scr, dj_scr, j_scr = refs[5:]
    d = in_ref.shape[1]
    chunk = d // order.devices
    levels, total, _ = geometry(seq)
    near, _, far_base = split_levels(seq)
    tile = pl.program_id(0)
    lanes = q_ref.shape[1]
    me = me_ref[0]

    @pl.when(tile == 0)
    def _():
        dk_scr[...] = jnp.zeros_like(dk_scr)
        dv_scr[...] = jnp.zeros_like(dv_scr)
        if not last:
            lo_ref[:, 3 * lanes :] = olo_ref[...]
            hi_ref[:, 3 * lanes :] = ohi_ref[...]

    tiles = range(STEP)
    grads, prob_grads, score_grads = [], [], []
    for t in tiles:
        grads.append(split_heads(cg_ref[t * TILE : (t + 1) * TILE, :]))
        prob_grads.append(dot(window_of(vx_ref, tile * STEP + t, levels), grads[t], (1, 1)))
    for t in tiles:
        prob = p_ref[t].astype(F32)
        inner = jnp.sum(prob * prob_grads[t], axis=0, keepdims=True)
        score_grads.append((prob * (prob_grads[t] - inner)).astype(BF))
    for t in tiles:
        now = tile * STEP + t
        query_grad = own_heads(dot(score_grads[t], window_of(kx_ref, now, levels), (0, 0)))
        dj_scr[pl.ds(pl.multiple_of(now * TILE, TILE), TILE), :lanes] = (query_grad * 0.125).astype(BF)
    for t in tiles:
        now = tile * STEP + t
        key_grad = dot(score_grads[t], split_heads(q_ref[t * TILE : (t + 1) * TILE, :]))
        val_grad = dot(p_ref[t], grads[t])
        at = 0
        for v in levels:
            for row, n in v.spans(now):
                dk_scr[pl.ds(row, n), :] += key_grad[at : at + n]
                dv_scr[pl.ds(row, n), :] += val_grad[at : at + n]
                at += n

    @pl.when(tile == pl.num_programs(0) - 1)
    def _():
        pad = levels[0].pad
        for ref, at in ((dk_scr, lanes), (dv_scr, 2 * lanes)):
            far = ref[far_base:total, :].astype(BF)
            for t in range(seq // POOL):
                parts = []
                for v in near:
                    n = POOL // v.factor
                    base = v.base + v.pad + t * n
                    parts.append(ref[base : base + n, :].astype(BF))
                parts.append(far)
                spread = dot(spread_ref[t * POOL : (t + 1) * POOL, :], jnp.concatenate(parts, axis=0))
                whole = ref[pad + t * POOL : pad + (t + 1) * POOL, :] + spread
                dj_scr[t * POOL : (t + 1) * POOL, at : at + lanes] = whole.astype(BF)
        j_scr[...] = dot(in_ref[...], dj_scr[...], (0, 0)).astype(BF)
        mine = order.turned if last else order
        pack_rows(mine, me, j_scr, (lo_ref, hi_ref), slice(0, 3 * lanes), chunk)
        step = 256
        if last:
            gains = jnp.zeros((1, d), F32)
            shifts = jnp.zeros((1, d), F32)
        for r in range(0, seq, step):
            fig = sum(
                dot(
                    dj_scr[r : r + step, k * lanes : (k + 1) * lanes],
                    w_ref[:, k * d + group * lanes : k * d + (group + 1) * lanes],
                    (1, 1),
                )
                for k in range(3)
            )
            if last:
                fig = fig + fig0_ref[r : r + step, :]
            fig_ref[r : r + step, :] = fig
            if not last:
                continue
            hat, _ = normalize(x_ref[r : r + step, :].astype(F32))
            gains += jnp.sum(fig * hat, axis=0, keepdims=True)
            shifts += jnp.sum(fig, axis=0, keepdims=True)
        if last:
            sums_ref[0:1, :] = gains
            sums_ref[1:2, :] = shifts
            if order.stepped:
                folded = fold_lanes(mine, me, gains, 0, chunk, 128)
                folded += fold_lanes(mine, me, shifts, chunk, chunk, 128)
                block = place_rows(folded, 0, chunk).astype(BF)
                lo_ref[:, 3 * lanes :] = block[: d // 2]
                hi_ref[:, 3 * lanes :] = block[d // 2 :]


def whole(shape):
    return pl.BlockSpec(shape, lambda i: (0,) * len(shape))


def smem():
    return pl.BlockSpec(memory_space=pltpu.SMEM)


def launch(name, kernel, steps, ins, outs, scratch, after=(), mib=8, cost=2 * 10**10, aliases=()):
    n = len(ins)

    def body(*refs):
        kernel(*refs[:n], *refs[n + len(after) :])

    return pl.pallas_call(
        body,
        grid=(steps,),
        in_specs=[s for _, s in ins] + [pl.BlockSpec(memory_space=pl.ANY)] * len(after),
        out_specs=[s for _, s in outs],
        out_shape=[o for o, _ in outs],
        scratch_shapes=scratch,
        compiler_params=pltpu.CompilerParams(
            dimension_semantics=("arbitrary",), vmem_limit_bytes=mib * MIB
        ),
        cost_estimate=pl.CostEstimate(flops=cost, bytes_accessed=0, transcendentals=0),
        input_output_aliases=dict(aliases),
        name=name,
    )(*[a for a, _ in ins], *after)


def out(shape, dtype, spec=None):
    return jax.ShapeDtypeStruct(shape, dtype), whole(shape) if spec is None else spec


def from_hbm(array):
    return pltpu.with_memory_space_constraint(array, pltpu.HBM), whole(array.shape)


def full(array):
    return array, whole(array.shape)


def by_rows(rows, width, column=0):
    return pl.BlockSpec((rows, width), lambda i: (i, column))


def by_columns(rows, width):
    return pl.BlockSpec((rows, width), lambda i: (0, i))


def by_tiles(shape):
    return pl.BlockSpec((STEP, *shape[1:]), lambda i: (i, 0, 0))


def fixed_columns(rows, width, column):
    return pl.BlockSpec((rows, width), lambda i: (0, column))


def prepare(lens, seq, after=()):
    _, _, window = geometry(seq)
    shape = (seq // TILE, window, 128)
    return launch(
        "prepare",
        functools.partial(prepare_kernel, seq),
        seq // TILE // STEP,
        [(lens, smem())],
        [out(shape, F32, by_tiles(shape))],
        [],
        after,
        cost=0,
    )[0]


def by_blocks(source, width, chunk, blocks):
    group = 128 // chunk
    lane = iota((source.shape[0], 128), 1) // chunk
    columns = []
    for at in range(0, blocks * width, 128):
        column = None
        for k in range(group):
            device, block = (at % width) // chunk + k, at // width
            lanes = (device * blocks + block) * chunk
            piece = source[:, lanes // 128 * 128 : lanes // 128 * 128 + 128]
            shift = (k * chunk - lanes) % 128
            if shift:
                piece = pltpu.roll(piece, shift, 1)
            column = piece if column is None else jnp.where(lane == k, piece, column)
        columns.append(column)
    return columns


def from_blocks(parts, width, chunk, blocks):
    group = 128 // chunk
    lane = iota((parts[0].shape[0], 128), 1) // chunk
    columns = []
    for at in range(0, blocks * width, 128):
        column = None
        for k in range(group):
            device, block = divmod(at // chunk + k, blocks)
            lanes = device * chunk
            piece = parts[block][:, lanes // 128 * 128 : lanes // 128 * 128 + 128]
            shift = (k * chunk - lanes) % 128
            if shift:
                piece = pltpu.roll(piece, shift, 1)
            column = piece if column is None else jnp.where(lane == k, piece, column)
        columns.append(column)
    return columns


def pack_kernel(joint_ref, expand_ref, output_ref, reduce_ref, *refs):
    small, (a_ref, e1_ref, e2_ref) = refs[:6], refs[6:]
    chunk, d = output_ref.shape
    wide = joint_ref.shape[1]

    def line(vectors):
        flat = jnp.concatenate([v[...].reshape(1, v.shape[0]).astype(F32) for v in vectors], axis=1)
        gap = jnp.zeros((1, 128 - flat.shape[1]), F32)
        return jnp.concatenate([flat, gap], axis=1)

    def block(parts):
        gap = jnp.zeros((chunk - len(parts), 128), F32)
        return jnp.concatenate(parts + [gap], axis=0).astype(BF)

    a_ref[:, :wide] = joint_ref[...]
    a_ref[:, wide:] = block([line(small[:2])])
    columns = by_blocks(expand_ref[...].astype(F32), d, chunk, 4)
    for i, column in enumerate(columns):
        target = (e1_ref, e2_ref)[i * 128 // (2 * d)]
        at = i * 128 % (2 * d)
        target[:, at : at + 128] = column.astype(BF)
    for k in range(4):
        target = (e1_ref, e2_ref)[k // 2]
        target[:, (2 + k % 2) * d : (3 + k % 2) * d] = reduce_ref[k * chunk : (k + 1) * chunk, :]
    e1_ref[:, 4 * d : 5 * d] = output_ref[...]
    e1_ref[:, 5 * d :] = block([line(small[2:5]), line(small[5:])])


def pack(joint, expand, output, reduce, small):
    rows, wide = joint.shape
    d = output.shape[1]
    return launch(
        "pack",
        pack_kernel,
        1,
        [from_hbm(a) for a in (joint, expand, output, reduce, *small)],
        [out((rows, wide + 128), BF), out((rows, 5 * d + 128), BF), out((rows, 4 * d), BF)],
        [],
        mib=4,
        cost=0,
    )


def finish_kernel(one_ref, two_ref, expand_ref, reduce_ref, output_ref, *small):
    chunk, d = output_ref.shape
    parts = [one_ref[:, :d], one_ref[:, d : 2 * d], two_ref[:, :d], two_ref[:, d : 2 * d]]
    for i, column in enumerate(from_blocks(parts, d, chunk, 4)):
        expand_ref[:, i * 128 : (i + 1) * 128] = column
    for k in range(4):
        source = (one_ref, two_ref)[k // 2]
        reduce_ref[k * chunk : (k + 1) * chunk, :] = source[:, (2 + k % 2) * d : (3 + k % 2) * d]
    at = two_ref.shape[1] - 128
    output_ref[...] = two_ref[:, at - d : at]
    for k in range(3):
        small[k][...] = two_ref[0:1, at + k * chunk : at + (k + 1) * chunk].reshape(chunk)
    small[3][...] = two_ref[1:2, at : at + 4 * chunk].reshape(4 * chunk)


def finish(one, two, after):
    rows, d = one.shape[0], one.shape[1] // 4
    return launch(
        "finish",
        finish_kernel,
        1,
        [full(one), full(two)],
        [out((rows, 4 * d), F32), out((4 * rows, d), F32), out((rows, d), F32)]
        + [out((rows,), F32)] * 3
        + [out((4 * rows,), F32)],
        [],
        after,
    )


def close_kernel(lanes, before_ref, keep_ref, other_ref, joint_ref, gain_ref, shift_ref):
    total = keep_ref[...].astype(F32) + other_ref[...].astype(F32)
    chunk, d = joint_ref.shape[0], joint_ref.shape[1] // 3
    at = 4 * d
    for k in range(3):
        joint_ref[:, k * d : k * d + lanes] = before_ref[:, at + k * lanes : at + (k + 1) * lanes]
        joint_ref[:, k * d + lanes : (k + 1) * d] = total[:, k * lanes : (k + 1) * lanes]
    gain_ref[...] = total[0:1, 3 * lanes : 3 * lanes + chunk].reshape(chunk)
    shift_ref[...] = total[0:1, 3 * lanes + chunk : 3 * lanes + 2 * chunk].reshape(chunk)


def close(before, pair, d):
    rows = before.shape[0]
    return launch(
        "close",
        functools.partial(close_kernel, d // GROUPS),
        1,
        [full(before), full(pair[0]), full(pair[1])],
        [out((rows, 3 * d), F32)] + [out((rows,), F32)] * 2,
        [],
        cost=0,
    )


def merge_kernel(plan, *refs):
    n = sum(1 if kind == "carry" else 2 * count for kind, count in plan)
    ins, outs = list(refs[:n]), list(refs[n:])
    for kind, count in plan:
        if kind == "carry":
            outs.pop(0)[...] = ins.pop(0)[...]
            continue
        targets = [outs.pop(0) for _ in range(2 if kind == "add" else 1)]
        at = 0
        for _ in range(count):
            first, second = ins.pop(0), ins.pop(0)
            rows, width = first.shape
            columns = slice(at, at + width)
            at += width
            if kind == "join":
                targets[0][:rows, columns] = first[...]
                targets[0][rows:, columns] = second[...]
                continue
            total = first[...].astype(F32) + second[...].astype(F32)
            if kind == "last":
                targets[0][:, columns] = total
                continue
            targets[0][:, columns] = total[: rows // 2].astype(BF)
            targets[1][:, columns] = total[rows // 2 :].astype(BF)


def merge(plan, arrays, after):
    outs = []
    for (kind, _), pairs in zip(plan, arrays, strict=True):
        rows = pairs[0][0].shape[0]
        width = sum(p[0].shape[1] for p in pairs)
        if kind == "carry":
            outs.append(out((rows, width), pairs[0][0].dtype))
        elif kind == "join":
            outs.append(out((2 * rows, width), BF))
        elif kind == "last":
            outs.append(out((rows, width), F32))
        else:
            outs += [out((rows // 2, width), BF)] * 2
    return launch(
        "merge",
        functools.partial(merge_kernel, plan),
        1,
        [full(a) for pairs in arrays for pair in pairs for a in pair],
        outs,
        [],
        after,
        cost=0,
    )


def attend(order, me, group, bias, x, weights, vec, after=()):
    seq, d = x.shape
    lanes = d // GROUPS
    _, total, window = geometry(seq)
    tiles = seq // TILE
    cols = lanes // DIM * TILE
    near, _, far_base = split_levels(seq)
    scratch = [
        pltpu.VMEM((sum(POOL // v.factor for v in near), POOL), BF),
        pltpu.VMEM((total - far_base, seq), BF),
    ]
    ins = [(me, smem()), (bias, by_tiles(bias.shape))]
    if group == 0:
        ins.append(from_hbm(x))
    else:
        ins.append(full(x))
    ins += [full(w) for w in weights]
    outs = [
        out((tiles, window, cols), BF, by_tiles((tiles, window, cols))),
        out((seq, lanes), BF, by_rows(STEP * TILE, lanes)),
        out((seq, lanes), BF),
        out((total, lanes), BF),
        out((total, lanes), BF),
    ]
    if group == 0:
        ins.append(full(vec))
        outs += [out((seq, d), BF), out((d, 3 * d), BF), out((8, d), F32)]
    return launch(
        "attend",
        functools.partial(attend_kernel, order, seq, group),
        tiles // STEP,
        ins,
        outs,
        scratch,
        after,
        cost=2 * 10**10 if group == 0 else 0,
    )


def ffn_scratch(seq, d):
    return [
        pltpu.VMEM((d, 2 * d), BF),
        pltpu.VMEM((d, 2 * d), BF),
        pltpu.VMEM((d, d), BF),
        pltpu.VMEM((1, 2 * d), F32),
        pltpu.VMEM((d, seq), BF),
        pltpu.VMEM((seq, d), BF),
        pltpu.VMEM((seq, d), BF),
        pltpu.VMEM((d, d), BF),
        pltpu.VMEM((8, d), F32),
    ]


def ffn_first(order, me, lens, x, cot, ctx0, ctx1, e1, vec, ebias, after=()):
    seq, d = x.shape
    return launch(
        "ffn_first",
        functools.partial(ffn_kernel, order, 0),
        2,
        [(me, smem()), (lens, smem())]
        + [full(a) for a in (x, cot, ctx0, ctx1, *e1, vec, ebias)],
        [
            out((seq, d), F32),
            out((seq, d), BF),
            out((seq, d), BF),
            out((seq, d), F32),
            out((seq, d), F32),
            out((1, 2 * d), F32),
            out((d // 2, 4 * d), BF),
            out((d // 2, 4 * d), BF),
        ],
        ffn_scratch(seq, d),
        after,
        mib=12,
    )


def ffn_second(order, me, lens, cot, kept, ctx0, ctx1, e1, e2, vec, ebias, after=()):
    seq, d = cot.shape
    width = d + (128 if order.stepped else 0)
    return launch(
        "ffn_second",
        functools.partial(ffn_kernel, order, 1),
        2,
        [(me, smem()), (lens, smem())]
        + [full(a) for a in (cot, *kept, ctx0, ctx1, *e1, *e2, vec, ebias)],
        [
            out((seq, d), BF),
            out((seq, d), F32),
            out((seq, d), BF),
            out((d // 2, 4 * d), BF),
            out((d // 2, 4 * d), BF),
            out((d // 2, width), BF),
            out((d // 2, width), BF),
            out((8, d), F32),
            out((1, 2 * d), F32),
            out((seq, d), F32),
            out((seq, d), F32),
        ],
        ffn_scratch(seq, d) + [pltpu.VMEM((seq, d), BF)],
        after,
        aliases={3: 1, 6: 9, 7: 10},
        mib=14,
    )


def attend_back(order, me, group, prob, q, cg, kx, vx, first_in, weights, more, after=()):
    seq, d = first_in.shape
    lanes = d // GROUPS
    levels, total, _ = geometry(seq)
    spread = spreading(seq)
    last = group == GROUPS - 1
    extra = (128 if order.stepped else 0) if last else more[0].shape[1]
    ins = [
        (me, smem()),
        (prob, by_tiles(prob.shape)),
        (q, by_rows(STEP * TILE, lanes)),
        (cg, by_rows(STEP * TILE, lanes, group)),
        full(kx),
        full(vx),
        full(first_in),
        full(weights),
        full(jnp.asarray(spread, BF)),
    ]
    ins += [full(a) for a in more]
    outs = [out((d // 2, 3 * lanes + extra), BF)] * 2 + [out((seq, d), F32)]
    if last:
        outs.append(out((8, d), F32))
    return launch(
        "attend_back",
        functools.partial(attend_back_kernel, order, seq, group),
        prob.shape[0] // STEP,
        ins,
        outs,
        [
            pltpu.VMEM((total, lanes), F32),
            pltpu.VMEM((total, lanes), F32),
            pltpu.VMEM((seq, 3 * lanes), BF),
            pltpu.VMEM((d, 3 * lanes), BF),
        ],
        after,
        mib=17,
    )


def token_kernel(x_ref, fig_ref, hg_ref, gain_ref, kept_ref, tg_ref, mixed_ref, mark_ref):
    hat, scale = normalize(x_ref[...].astype(F32))
    grad = hg_ref[...] + norm_back(fig_ref[...], hat, scale, gain_ref[0:1, :])
    tg_ref[...] = grad.astype(BF)
    mixed_ref[...] = kept_ref[...]
    mark_ref[...] = jnp.zeros_like(mark_ref)


def token_grads(x, fig, hidden_grad, gain, kept, after=()):
    seq, d = x.shape
    rows = 512
    return launch(
        "token_grad",
        token_kernel,
        seq // rows,
        [(a, by_rows(rows, d)) for a in (x, fig, hidden_grad)] + [full(gain), (kept, by_rows(rows, d))],
        [(pltpu.HBM((seq, d), BF), by_rows(rows, d))] * 2 + [out((8, 128), F32)],
        [],
        after,
        cost=0,
    )


class Gather:
    def __init__(self, order, value):
        self.order, self.bits, self.have, self.other = order, list(order.bits), value, None
        if not order.stepped:
            half = value.shape[0] // 2
            self.have, self.other, self.bits = value[:half], value[half:], []

    def send(self):
        if self.bits:
            self.other = swap(self.order, self.have, self.bits.pop(0))

    def kind(self):
        return "join", 1

    def pairs(self):
        return [(self.have, self.other)]

    def pair(self):
        return self.have, self.other

    def take(self, outs):
        self.have = outs.pop(0)


class Scatter:
    def __init__(self, order, halves):
        self.order, self.bits, self.halves, self.other = order, order.bits[::-1], halves, None
        self.done = None
        self.beside = []
        if not order.stepped:
            self.done = jnp.concatenate(halves, axis=0).astype(F32)

    def send(self):
        if self.order.stepped:
            self.other = swap(self.order, self.halves[1], self.bits.pop(0))

    def kind(self):
        return "add" if self.bits else "last", 1 + len(self.beside)

    def pairs(self):
        return [(self.halves[0], self.other)] + self.beside

    def absorb(self, chain):
        if self.order.stepped:
            self.beside += chain.pairs()

    def take(self, outs):
        self.beside = []
        if self.bits:
            self.halves = outs.pop(0), outs.pop(0)
        else:
            self.done = outs.pop(0)


def swap(order, value, bit):
    return lax.ppermute(value, AXES, [(i, i ^ bit) for i in range(order.devices)])


def advance(order, chains, after=(), carry=None, hold=()):
    if not order.stepped:
        return () if carry is None else ((), carry)
    plan = [c.kind() for c in chains]
    arrays = [c.pairs() for c in chains]
    if carry is not None:
        plan.append(("carry", 1))
        arrays.append([(carry,)])
    outs = list(merge(plan, arrays, after))
    marks = tuple(outs)
    if carry is not None:
        carry = outs.pop()
    for c in chains:
        c.take(outs)
        if c.bits and c not in hold:
            c.send()
    return marks[:1] if carry is None else (marks[:1], carry)


def release(order, held, chains, after):
    mark, high = advance(order, chains, after, held.halves[1])
    held.halves = held.halves[0], high
    held.send()
    return mark


def local(order, me, tokens, cotangent, lens, joint_w, output_w, expand_w, reduce_w,
          attn_gain, attn_shift, ffn_gain, ffn_shift, expand_bias, reduce_bias):
    seq, d = tokens.shape
    lanes = d // GROUPS
    rows = joint_w.shape[0]
    ff = expand_w.shape[1]
    vec = jnp.zeros((8, d), F32)
    ebias = jnp.zeros((1, ff), F32)
    if order.stepped:
        small = [attn_gain, attn_shift, ffn_gain, ffn_shift, reduce_bias, expand_bias]
        first, second, third = pack(joint_w, expand_w, output_w, reduce_w, small)
        joint = Gather(order, first)
        e1 = Gather(order, second)
        e2 = Gather(order, third)
    else:
        small = [attn_gain, attn_shift, ffn_gain, ffn_shift, reduce_bias]
        small = [lax.all_gather(v, AXES, tiled=True) for v in small]
        vec = jnp.pad(jnp.stack(small), ((0, 3), (0, 0))).astype(F32)
        ebias = lax.all_gather(expand_bias, AXES, tiled=True)[None].astype(F32)
        e, o, r = [lax.all_gather(w, AXES, axis=0, tiled=True) for w in (expand_w, output_w, reduce_w)]
        r = [r[k * d : (k + 1) * d] for k in range(4)]
        joint = Gather(order, lax.all_gather(joint_w, AXES, axis=0, tiled=True))
        e1 = Gather(order, jnp.concatenate([e[:, : 2 * d], r[0], r[1], o], axis=1))
        e2 = Gather(order, jnp.concatenate([e[:, 2 * d :], r[2], r[3]], axis=1))
    joint.send()
    mark = advance(order, [joint])
    e1.send()
    mark = advance(order, [joint, e1], mark)
    e2.send()
    mark = advance(order, [joint, e1, e2], mark)
    bias = prepare(lens, seq, mark)
    mark = advance(order, [joint, e1, e2], (bias,))
    p0, ctx0, q0, kx0, vx0, first_in, w, gain = attend(order, me, 0, bias, tokens, joint.pair(), vec, mark)
    p1, ctx1, q1, kx1, vx1 = attend(order, me, 1, bias, first_in, (w,), vec, (ctx0,))
    mark = advance(order, [e1, e2], (ctx1,))
    *kept, lo, hi = ffn_first(
        order, me, lens, tokens, cotangent, ctx0, ctx1, e1.pair(), vec, ebias, mark
    )
    t1 = Scatter(order, (lo, hi))
    mark = advance(order, [e2], (lo,))
    t1.send()
    mark = advance(order, [t1], mark)
    mixed, hg, cg, lo, hi, olo, ohi, sums, esum, _, _ = ffn_second(
        order, me, lens, cotangent, kept, ctx0, ctx1, e1.pair(), e2.pair(), vec, ebias, mark
    )
    mark = advance(order, [t1], (cg,))
    t2 = Scatter(order.turned, (lo, hi))
    t2.send()
    lo, hi, fig = attend_back(order, me, 0, p0, q0, cg, kx0, vx0, first_in, w, (olo, ohi), mark)
    mark, hi = advance(order, [t1, t2], (fig,), hi, [t1])
    j0 = Scatter(order, (lo, hi))
    j0.send()
    mark = release(order, t1, [j0], mark)
    lo, hi, fig, tail_sums = attend_back(
        order, me, 1, p1, q1, cg, kx1, vx1, first_in, w, (tokens, fig), mark
    )
    mark, hi = advance(order, [t1, t2, j0], (tail_sums,), hi, [t1, j0])
    j1 = Scatter(order.turned, (lo, hi))
    j1.send()
    mark = release(order, j0, [j1], mark)
    t1.send()
    token_grad, mixed, mark = token_grads(tokens, fig, hg, gain, mixed, mark)
    t2.absorb(j0)
    mark = advance(order, [t2, t1], (mark,))
    mark = advance(order, [j1], mark)
    mark = advance(order, [t2], mark)
    mark = advance(order, [j1], mark)
    mark = advance(order, [j1], mark)
    if order.stepped:
        advance(order, [t2], mark)
        expand_grad, reduce_grad, output_grad, *small = finish(t1.done, t2.done, mark)
        joint_grad, *first_small = close(t2.done, j1.pairs()[0], d)
        small = [*first_small, small[0], small[1], small[3], small[2]]
    else:
        parts = []
        for k in range(3):
            parts += [c.done[:, k * lanes : (k + 1) * lanes] for c in (j0, j1)]
        joint_grad = jnp.concatenate(parts, axis=1)
        one, two = t1.done, t2.done
        expand_grad = lax.psum_scatter(
            jnp.concatenate([one[:, : 2 * d], two[:, : 2 * d]], axis=1), AXES, scatter_dimension=0, tiled=True
        )
        reduce_grad = lax.psum_scatter(
            jnp.concatenate([t[:, k * d : (k + 1) * d] for t in (one, two) for k in (2, 3)], axis=0),
            AXES,
            scatter_dimension=0,
            tiled=True,
        )
        output_grad = lax.psum_scatter(j0.done[:, 3 * lanes :], AXES, scatter_dimension=0, tiled=True)
        joint_grad = lax.psum_scatter(joint_grad, AXES, scatter_dimension=0, tiled=True)
        esums = jnp.concatenate([kept[5][0], esum[0]])
        vectors = [tail_sums[0], tail_sums[1], sums[0], sums[1], esums, sums[2]]
        small = [lax.psum_scatter(v, AXES, scatter_dimension=0, tiled=True) for v in vectors]
    return (mixed, token_grad, joint_grad, output_grad, expand_grad, reduce_grad, *small)


def shards(order, *args):
    sub = lax.axis_size("sub")
    me = (lax.axis_index("dp") * sub + lax.axis_index("sub")).astype(jnp.int32).reshape(1)
    return local(order, me, *args)


def solution(mesh):
    order = Order(math.prod(mesh.shape[a] for a in AXES))
    wide = P(AXES, None)
    flat = P(AXES)
    return jax.shard_map(
        functools.partial(shards, order),
        mesh=mesh,
        in_specs=(wide,) * 7 + (flat,) * 6,
        out_specs=(wide,) * 6 + (flat,) * 6,
        check_vma=False,
    )
```

```python
import functools
import math

import jax
import jax.numpy as jnp
import numpy as np
from jax import lax
from jax.experimental import pallas as pl
from jax.experimental.pallas import tpu as pltpu
from jax.sharding import PartitionSpec as P

HEADS = 8
BLOCK = 16
LEVELS = 7
TILE = 64
POOL = 128
GROUPS = 2
DIM = 64
STEP = 8
LOG_TWO = math.log(2.0)
NEGATIVE = -1e30
ROOT_HALF = 1.0 / math.sqrt(2.0)
DENSITY = 1.0 / math.sqrt(2.0 * math.pi)
AXES = ("dp", "sub")
BF = jnp.bfloat16
F32 = jnp.float32
MIB = 1 << 20


class Level:
    def __init__(self, level, seq, base):
        self.level = level
        self.factor = 1 << level
        self.count = seq // self.factor
        self.width = BLOCK * self.factor
        self.blocks = seq // self.width
        self.pad = BLOCK if self.blocks > 2 else 0
        self.base = base
        self.rows = self.count + 2 * self.pad

    def pieces(self, tile):
        if self.width < TILE:
            return [(tile * (TILE // self.factor), TILE // self.factor + 2 * BLOCK)]
        block = tile // (self.width // TILE)
        if self.blocks > 2:
            return [(block * BLOCK, BLOCK), ((block + 2) * BLOCK, BLOCK)]
        return [((self.blocks - 1 - block) * BLOCK, BLOCK)]

    def spans(self, tile):
        return [(pl.multiple_of(self.base + first, BLOCK), n) for first, n in self.pieces(tile)]


def geometry(seq):
    levels, base = [], 0
    for level in range(LEVELS):
        levels.append(Level(level, seq, base))
        base += levels[-1].rows
    return levels, base, sum(n for v in levels for _, n in v.pieces(0))


def split_levels(seq):
    levels, _, _ = geometry(seq)
    near = [v for v in levels[1:] if v.width <= POOL]
    far = [v for v in levels[1:] if v.width > POOL]
    return near, far, far[0].base


def spreading(seq):
    levels, total, _ = geometry(seq)
    near, far, far_base = split_levels(seq)
    near_rows = sum(POOL // v.factor for v in near)
    spread = np.zeros((seq, near_rows + total - far_base), np.float32)
    at = 0
    for v in near:
        for t in range(seq):
            spread[t, at + t % POOL // v.factor] = 1.0 / v.factor
        at += POOL // v.factor
    for v in far:
        for t in range(seq):
            spread[t, near_rows + v.base - far_base + v.pad + t // v.factor] = 1.0 / v.factor
    return spread


class Order:
    def __init__(self, devices, turned=False):
        self.devices = devices
        self.bits = [1 << k for k in reversed(range(devices.bit_length() - 1))]
        self.stepped = devices == 32
        if not turned:
            self.turned = Order(devices, True)
        elif self.stepped:
            self.bits[-3:-1] = self.bits[-2], self.bits[-3]

    def flip(self, p):
        value = 0
        for k, bit in enumerate(self.bits):
            value = value + ((p >> k) & 1) * bit
        return value


def dot(left, right, contract=(1, 0)):
    return lax.dot_general(
        left, right, (((contract[0],), (contract[1],)), ((), ())), preferred_element_type=F32
    )


def iota(shape, axis):
    return lax.broadcasted_iota(jnp.int32, shape, axis)


def unpack_rows(order, me, halves, columns, target, chunk, places=slice(None)):
    rows = halves[0].shape[0]
    if not order.stepped:
        target[:rows, places] = halves[0][:, columns]
        target[rows:, places] = halves[1][:, columns]
        return
    for p in range(order.devices):
        half, at = divmod(p * chunk, rows)
        row = pl.multiple_of((me ^ order.flip(p)) * chunk, chunk)
        target[pl.ds(row, chunk), places] = halves[half][at : at + chunk, columns]


def pack_rows(order, me, source, halves, columns, chunk):
    rows = halves[0].shape[0]
    if not order.stepped:
        halves[0][:, columns] = source[:rows]
        halves[1][:, columns] = source[rows:]
        return
    for p in range(order.devices):
        half, at = divmod(p * chunk, rows)
        row = pl.multiple_of((me ^ order.flip(p)) * chunk, chunk)
        halves[half][at : at + chunk, columns] = source[pl.ds(row, chunk), :]


def owners(order, me, shape):
    return me ^ order.flip(iota(shape, 0))


def spread_lanes(order, me, halves, columns, row, offset, chunk, total):
    n = order.devices
    block = jnp.concatenate([half[:, columns] for half in halves], axis=0)
    step = block.shape[0] // n
    pick = (iota((n, block.shape[0]), 1) == iota((n, block.shape[0]), 0) * step + row).astype(BF)
    rows = dot(pick, block).astype(BF)
    lanes = block.shape[1]
    place = (iota((lanes, total), 0) == iota((lanes, total), 1) % chunk + offset).astype(BF)
    wide = dot(rows, place)
    mine = iota((n, total), 1) // chunk == owners(order, me, (n, total))
    return jnp.sum(jnp.where(mine, wide, 0.0), axis=0, keepdims=True)


def fold_lanes(order, me, vector, offset, chunk, lanes):
    n, total = order.devices, vector.shape[1]
    mine = iota((n, total), 1) // chunk == owners(order, me, (n, total))
    wide = jnp.where(mine, vector, 0.0).astype(BF)
    place = (iota((total, lanes), 1) == iota((total, lanes), 0) % chunk + offset).astype(BF)
    return dot(wide, place)


def place_rows(rows, row, step):
    n = rows.shape[0]
    pick = (iota((n * step, n), 0) == iota((n * step, n), 1) * step + row).astype(BF)
    return dot(pick, rows.astype(BF))


def live_column(lens, first, rows):
    position = first + iota((rows, 1), 0)
    start, live = 0, jnp.zeros((rows, 1), jnp.bool_)
    for i in range(lens.shape[1]):
        length = lens[0, i]
        live = live | ((position >= start) & (position < start + length))
        start = start + (length + BLOCK - 1) // BLOCK * BLOCK
    return live


def tile_bias(lens, tile, levels, copies):
    position = tile * TILE + iota((1, copies * TILE), 1) % TILE
    low, high, start = position, position + 1, 0
    for i in range(lens.shape[1]):
        length = lens[0, i]
        inside = (position >= start) & (position < start + length)
        low = jnp.where(inside, start, low)
        high = jnp.where(inside, start + length, high)
        start = start + (length + BLOCK - 1) // BLOCK * BLOCK
    parts = []
    for v in levels:
        reach = (position // v.width - 1) * v.width
        least = jnp.maximum(low, reach)
        most = jnp.minimum(high - v.factor, reach + 3 * v.width - 1)
        half = v.width // 2
        lower = (position // half - 1) * half
        for first, rows in v.pieces(tile):
            begin = (first - v.pad + iota((rows, copies * TILE), 0)) * v.factor
            valid = (begin >= least) & (begin <= most)
            if v.level > 0:
                valid = valid & ((begin < lower) | (begin >= lower + 3 * half))
            parts.append(jnp.where(valid, v.level * LOG_TWO, NEGATIVE))
    return jnp.concatenate(parts, axis=0)


def window_of(ref, tile, levels):
    return jnp.concatenate([ref[pl.ds(at, n), :] for v in levels for at, n in v.spans(tile)], axis=0)


def split_heads(rows):
    head = iota(rows.shape, 1) // DIM
    zero = jnp.zeros_like(rows)
    return jnp.concatenate([jnp.where(head == h, rows, zero) for h in range(rows.shape[1] // DIM)], axis=0)


def own_heads(full):
    heads = full.shape[1] // DIM
    head = iota((TILE, full.shape[1]), 1) // DIM
    own = full[:TILE]
    for h in range(1, heads):
        own = jnp.where(head == h, full[h * TILE : (h + 1) * TILE], own)
    return own


def normalize(values):
    centre = values - jnp.mean(values, axis=-1, keepdims=True)
    scale = lax.rsqrt(jnp.mean(centre * centre, axis=-1, keepdims=True) + 1e-05)
    return centre * scale, scale


def norm_back(grad, normed, scale, gain):
    scaled = grad * gain
    return scale * (
        scaled
        - jnp.mean(scaled, axis=-1, keepdims=True)
        - normed * jnp.mean(scaled * normed, axis=-1, keepdims=True)
    )


def prepare_kernel(seq, lens_ref, bias_ref):
    levels, _, _ = geometry(seq)
    step = pl.program_id(0)
    for t in range(STEP):
        bias_ref[t] = tile_bias(lens_ref, step * STEP + t, levels, bias_ref.shape[2] // TILE)


def means(seq, fine_ref, wide_ref):
    near, far, far_base = split_levels(seq)
    at = 0
    for v in near:
        n = POOL // v.factor
        same = iota((n, POOL), 1) // v.factor == iota((n, POOL), 0)
        fine_ref[at : at + n, :] = jnp.where(same, 1.0 / v.factor, 0.0).astype(BF)
        at += n
    for v in far:
        same = iota((v.rows, seq), 1) // v.factor == iota((v.rows, seq), 0) - v.pad
        base = v.base - far_base
        wide_ref[base : base + v.rows, :] = jnp.where(same, 1.0 / v.factor, 0.0).astype(BF)


def attend_kernel(order, seq, group, me_ref, bias_ref, x_ref, *refs):
    first_group = group == 0
    if first_group:
        lo_ref, hi_ref, vec_ref = refs[:3]
        p_ref, ctx_ref, q_ref, kx_ref, vx_ref, in_ref, w_ref, gain_ref = refs[3:11]
        fine_ref, wide_ref = refs[11:]
    else:
        w_ref, p_ref, ctx_ref, q_ref, kx_ref, vx_ref, fine_ref, wide_ref = refs
    levels, total, _ = geometry(seq)
    near, _, far_base = split_levels(seq)
    tile = pl.program_id(0)
    lanes = q_ref.shape[1]
    me = me_ref[0]

    @pl.when(tile == 0)
    def _():
        d = x_ref.shape[1]
        means(seq, fine_ref, wide_ref)
        if first_group:
            chunk = d // order.devices
            unpack_rows(order, me, (lo_ref, hi_ref), slice(0, 3 * d), w_ref, chunk)
            if order.stepped:
                tail = slice(3 * d, 3 * d + 128)
                gain = spread_lanes(order, me, (lo_ref, hi_ref), tail, 0, 0, chunk, d)
                shift = spread_lanes(order, me, (lo_ref, hi_ref), tail, 0, chunk, chunk, d)
            else:
                gain, shift = vec_ref[0:1, :], vec_ref[1:2, :]
            gain_ref[0:1, :] = gain
            for k in range(7):
                if order.stepped:
                    row, at = (1, k * chunk) if k < 3 else (2, (k - 3) * chunk)
                    gain_ref[k + 1 : k + 2, :] = spread_lanes(order, me, (lo_ref, hi_ref), tail, row, at, chunk, d)
                else:
                    gain_ref[k + 1 : k + 2, :] = vec_ref[k + 2 : k + 3, :]
        kx_ref[...] = jnp.zeros_like(kx_ref)
        vx_ref[...] = jnp.zeros_like(vx_ref)
        step = 256
        pad = levels[0].pad
        for r in range(0, seq, step):
            if first_group:
                hat, _ = normalize(x_ref[r : r + step, :].astype(F32))
                first_in = (hat * gain + shift).astype(BF)
                in_ref[r : r + step, :] = first_in
            else:
                first_in = x_ref[r : r + step, :]
            query, keys, vals = [
                dot(first_in, w_ref[:, k * d + group * lanes : k * d + (group + 1) * lanes]).astype(BF)
                for k in range(3)
            ]
            q_ref[r : r + step, :] = query * jnp.asarray(0.125, BF)
            kx_ref[pad + r : pad + r + step, :] = keys
            vx_ref[pad + r : pad + r + step, :] = vals
        for ref in (kx_ref, vx_ref):
            for t in range(seq // POOL):
                rows = ref[pad + t * POOL : pad + (t + 1) * POOL, :]
                pooled = dot(fine_ref[...], rows).astype(BF)
                at = 0
                for v in near:
                    n = POOL // v.factor
                    ref[v.base + v.pad + t * n : v.base + v.pad + (t + 1) * n, :] = pooled[at : at + n]
                    at += n
            ref[far_base:total, :] = dot(wide_ref[...], ref[pad : pad + seq, :]).astype(BF)

    tiles = range(STEP)
    scores = []
    for t in tiles:
        at = tile * STEP + t
        query = split_heads(q_ref[pl.ds(pl.multiple_of(at * TILE, TILE), TILE), :])
        scores.append(dot(window_of(kx_ref, at, levels), query, (1, 1)))
    probs = []
    for t in tiles:
        bias = jnp.concatenate([bias_ref[t]] * (scores[t].shape[1] // bias_ref.shape[2]), axis=1)
        score = scores[t] + bias
        peak = jnp.max(score, axis=0, keepdims=True)
        weight = jnp.exp(score - peak)
        share = 1.0 / jnp.sum(weight, axis=0, keepdims=True)
        probs.append((weight * share).astype(BF))
        p_ref[t] = probs[t]
    for t in tiles:
        context = dot(probs[t], window_of(vx_ref, tile * STEP + t, levels), (0, 0))
        ctx_ref[t * TILE : (t + 1) * TILE, :] = own_heads(context).astype(BF)


def ffn_block(rows, in_ref, og_ref, act_scr, eg_scr, mix_ref, sg_ref, we, wr, bias):
    for r in range(0, in_ref.shape[0], rows):
        part = slice(r, r + rows)
        expanded = dot(in_ref[part, :], we[...]) + bias
        phi = 0.5 * (1.0 + lax.erf(expanded * ROOT_HALF))
        activated = (expanded * phi).astype(BF)
        act_scr[part, :] = activated
        slope = phi + expanded * (jnp.exp(-0.5 * expanded * expanded) * DENSITY)
        expanded_grad = (dot(og_ref[part, :], wr[...], (1, 1)) * slope).astype(BF)
        eg_scr[part, :] = expanded_grad
        mix_ref[part, :] += dot(activated, wr[...])
        sg_ref[part, :] += dot(expanded_grad, we[...], (1, 1))


def ffn_kernel(order, part, me_ref, lens_ref, *refs):
    first = part == 0
    if first:
        x_ref, cot_ref, ctx0_ref, ctx1_ref, lo1_ref, hi1_ref, vec_ref, ebias_ref = refs[:8]
        hidden_ref, in_ref, og_ref, mix_ref, sg_ref, esum_ref, lo_ref, hi_ref = refs[8:16]
        own = (lo1_ref, hi1_ref)
        we_scr, wr_scr, wo_scr, eb_scr, in_scr, act_scr, eg_scr, grad_scr, vec_scr = refs[16:]
    else:
        cot_ref, hidden_ref, in_ref, og_ref, _, _, esum0_ref, ctx0_ref, ctx1_ref = refs[:9]
        lo1_ref, hi1_ref, lo2_ref, hi2_ref, vec_ref, ebias_ref = refs[9:15]
        mixed_ref, hg_ref, cg_ref, lo_ref, hi_ref, olo_ref, ohi_ref, sums_ref, esum_ref, mix_ref, sg_ref = refs[15:26]
        own = (lo2_ref, hi2_ref)
        we_scr, wr_scr, wo_scr, eb_scr, in_scr, act_scr, eg_scr, grad_scr, vec_scr, branch_scr = refs[26:]
    step = pl.program_id(0)
    me = me_ref[0]
    seq, d = cot_ref.shape
    rows = 512
    chunk = d // order.devices
    wide = 2 * d
    shared = (lo1_ref, hi1_ref)
    turned = order.turned
    half = ctx0_ref.shape[1]

    def live_rows(span):
        return live_column(lens_ref, span.start, rows).astype(F32)

    def open_rows(span):
        live = live_rows(span)
        out = dot(ctx0_ref[span, :], wo_scr[:half, :]) + dot(ctx1_ref[span, :], wo_scr[half:, :])
        hidden = x_ref[span, :].astype(F32) + live * out
        hidden_ref[span, :] = hidden
        hat, _ = normalize(hidden)
        in_ref[span, :] = (hat * vec_scr[0:1, :] + vec_scr[1:2, :]).astype(BF)
        og_ref[span, :] = (cot_ref[span, :].astype(F32) * live).astype(BF)

    def close_rows(span):
        live = live_rows(span)
        hidden = hidden_ref[span, :]
        mixed_ref[span, :] = (hidden + live * (mix_ref[span, :] + vec_scr[1:2, :])).astype(BF)
        hat, scale = normalize(hidden)
        second_grad = sg_ref[span, :]
        sums_ref[0:1, :] += jnp.sum(second_grad * hat, axis=0, keepdims=True)
        sums_ref[1:2, :] += jnp.sum(second_grad, axis=0, keepdims=True)
        sums_ref[2:3, :] += jnp.sum(og_ref[span, :].astype(F32), axis=0, keepdims=True)
        grad = cot_ref[span, :].astype(F32) + norm_back(second_grad, hat, scale, vec_scr[0:1, :])
        hg_ref[span, :] = grad
        branch = (grad * live).astype(BF)
        branch_scr[span, :] = branch
        cg_ref[span, :] = dot(branch, wo_scr[...], (1, 1)).astype(BF)

    @pl.when(step == 0)
    def _():
        unpack_rows(order, me, own, slice(0, wide), we_scr, chunk)
        unpack_rows(order, me, own, slice(wide, 2 * wide), wr_scr, chunk)
        unpack_rows(order, me, shared, slice(2 * wide, 2 * wide + d), wo_scr, chunk)
        for k in range(2):
            block = 4 + 2 * part + k
            eb_scr[:, k * d : (k + 1) * d] = vec_ref[block : block + 1, :]
        vec_scr[0:1, :] = vec_ref[1:2, :]
        vec_scr[1:2, :] = vec_ref[2:3, :] if first else vec_ref[3:4, :]
        if first:
            mix_ref[...] = jnp.zeros_like(mix_ref)
            sg_ref[...] = jnp.zeros_like(sg_ref)
        else:
            in_scr[...] = in_ref[...].T
            sums_ref[...] = jnp.zeros_like(sums_ref)
        if first:
            for r in range(0, seq, rows):
                open_rows(slice(r, r + rows))
            in_scr[...] = in_ref[...].T

    now = pl.ds(pl.multiple_of(step * d, d), d)
    ffn_block(
        rows, in_ref, og_ref, act_scr, eg_scr, mix_ref, sg_ref, we_scr.at[:, now], wr_scr.at[:, now], eb_scr[:, now]
    )
    esum_ref[:, now] = jnp.sum(eg_scr[...].astype(F32), axis=0, keepdims=True)
    mine = order if first else turned
    grad_scr[...] = dot(in_scr[...], eg_scr[...]).astype(BF)
    pack_rows(mine, me, grad_scr, (lo_ref, hi_ref), now, chunk)
    grad_scr[...] = dot(act_scr[...], og_ref[...], (0, 0)).astype(BF)
    pack_rows(mine, me, grad_scr, (lo_ref, hi_ref), pl.ds(pl.multiple_of(wide + step * d, d), d), chunk)

    if first:
        return

    @pl.when(step == pl.num_programs(0) - 1)
    def _():
        for r in range(0, seq, rows):
            close_rows(slice(r, r + rows))
        grad_scr[:half, :] = dot(ctx0_ref[...], branch_scr[...], (0, 0)).astype(BF)
        grad_scr[half:, :] = dot(ctx1_ref[...], branch_scr[...], (0, 0)).astype(BF)
        pack_rows(order, me, grad_scr, (olo_ref, ohi_ref), slice(0, d), chunk)
        if order.stepped:
            small = jnp.zeros((order.devices, 128), F32)
            for k in range(3):
                small += fold_lanes(order, me, sums_ref[k : k + 1, :], k * chunk, chunk, 128)
            more = jnp.zeros((order.devices, 128), F32)
            for k in range(2):
                now = slice(k * d, (k + 1) * d)
                more += fold_lanes(order, me, esum0_ref[:, now], k * chunk, chunk, 128)
                more += fold_lanes(order, me, esum_ref[:, now], (2 + k) * chunk, chunk, 128)
            block = (place_rows(small, 0, chunk) + place_rows(more, 1, chunk)).astype(BF)
            olo_ref[:, d:] = block[: d // 2]
            ohi_ref[:, d:] = block[d // 2 :]


def attend_back_kernel(
    order,
    seq,
    group,
    me_ref,
    p_ref,
    q_ref,
    cg_ref,
    kx_ref,
    vx_ref,
    in_ref,
    w_ref,
    spread_ref,
    *refs,
):
    last = group == GROUPS - 1
    if last:
        x_ref, fig0_ref, lo_ref, hi_ref, fig_ref, sums_ref = refs[:6]
        dk_scr, dv_scr, dj_scr, j_scr = refs[6:]
    else:
        olo_ref, ohi_ref, lo_ref, hi_ref, fig_ref = refs[:5]
        dk_scr, dv_scr, dj_scr, j_scr = refs[5:]
    d = in_ref.shape[1]
    chunk = d // order.devices
    levels, total, _ = geometry(seq)
    near, _, far_base = split_levels(seq)
    tile = pl.program_id(0)
    lanes = q_ref.shape[1]
    me = me_ref[0]

    @pl.when(tile == 0)
    def _():
        dk_scr[...] = jnp.zeros_like(dk_scr)
        dv_scr[...] = jnp.zeros_like(dv_scr)
        if not last:
            lo_ref[:, 3 * lanes :] = olo_ref[...]
            hi_ref[:, 3 * lanes :] = ohi_ref[...]

    tiles = range(STEP)
    grads, prob_grads, score_grads = [], [], []
    for t in tiles:
        grads.append(split_heads(cg_ref[t * TILE : (t + 1) * TILE, :]))
        prob_grads.append(dot(window_of(vx_ref, tile * STEP + t, levels), grads[t], (1, 1)))
    for t in tiles:
        prob = p_ref[t].astype(F32)
        inner = jnp.sum(prob * prob_grads[t], axis=0, keepdims=True)
        score_grads.append((prob * (prob_grads[t] - inner)).astype(BF))
    for t in tiles:
        now = tile * STEP + t
        query_grad = own_heads(dot(score_grads[t], window_of(kx_ref, now, levels), (0, 0)))
        dj_scr[pl.ds(pl.multiple_of(now * TILE, TILE), TILE), :lanes] = (query_grad * 0.125).astype(BF)
    for t in tiles:
        now = tile * STEP + t
        key_grad = dot(score_grads[t], split_heads(q_ref[t * TILE : (t + 1) * TILE, :]))
        val_grad = dot(p_ref[t], grads[t])
        at = 0
        for v in levels:
            for row, n in v.spans(now):
                dk_scr[pl.ds(row, n), :] += key_grad[at : at + n]
                dv_scr[pl.ds(row, n), :] += val_grad[at : at + n]
                at += n

    @pl.when(tile == pl.num_programs(0) - 1)
    def _():
        pad = levels[0].pad
        for ref, at in ((dk_scr, lanes), (dv_scr, 2 * lanes)):
            far = ref[far_base:total, :].astype(BF)
            for t in range(seq // POOL):
                parts = []
                for v in near:
                    n = POOL // v.factor
                    base = v.base + v.pad + t * n
                    parts.append(ref[base : base + n, :].astype(BF))
                parts.append(far)
                spread = dot(spread_ref[t * POOL : (t + 1) * POOL, :], jnp.concatenate(parts, axis=0))
                whole = ref[pad + t * POOL : pad + (t + 1) * POOL, :] + spread
                dj_scr[t * POOL : (t + 1) * POOL, at : at + lanes] = whole.astype(BF)
        j_scr[...] = dot(in_ref[...], dj_scr[...], (0, 0)).astype(BF)
        mine = order.turned if last else order
        pack_rows(mine, me, j_scr, (lo_ref, hi_ref), slice(0, 3 * lanes), chunk)
        step = 256
        if last:
            gains = jnp.zeros((1, d), F32)
            shifts = jnp.zeros((1, d), F32)
        for r in range(0, seq, step):
            fig = sum(
                dot(
                    dj_scr[r : r + step, k * lanes : (k + 1) * lanes],
                    w_ref[:, k * d + group * lanes : k * d + (group + 1) * lanes],
                    (1, 1),
                )
                for k in range(3)
            )
            if last:
                fig = fig + fig0_ref[r : r + step, :]
            fig_ref[r : r + step, :] = fig
            if not last:
                continue
            hat, _ = normalize(x_ref[r : r + step, :].astype(F32))
            gains += jnp.sum(fig * hat, axis=0, keepdims=True)
            shifts += jnp.sum(fig, axis=0, keepdims=True)
        if last:
            sums_ref[0:1, :] = gains
            sums_ref[1:2, :] = shifts
            if order.stepped:
                folded = fold_lanes(mine, me, gains, 0, chunk, 128)
                folded += fold_lanes(mine, me, shifts, chunk, chunk, 128)
                block = place_rows(folded, 0, chunk).astype(BF)
                lo_ref[:, 3 * lanes :] = block[: d // 2]
                hi_ref[:, 3 * lanes :] = block[d // 2 :]


def whole(shape):
    return pl.BlockSpec(shape, lambda i: (0,) * len(shape))


def smem():
    return pl.BlockSpec(memory_space=pltpu.SMEM)


def launch(name, kernel, steps, ins, outs, scratch, after=(), mib=8, cost=2 * 10**10, aliases=()):
    n = len(ins)

    def body(*refs):
        kernel(*refs[:n], *refs[n + len(after) :])

    return pl.pallas_call(
        body,
        grid=(steps,),
        in_specs=[s for _, s in ins] + [pl.BlockSpec(memory_space=pl.ANY)] * len(after),
        out_specs=[s for _, s in outs],
        out_shape=[o for o, _ in outs],
        scratch_shapes=scratch,
        compiler_params=pltpu.CompilerParams(
            dimension_semantics=("arbitrary",), vmem_limit_bytes=mib * MIB
        ),
        cost_estimate=pl.CostEstimate(flops=cost, bytes_accessed=0, transcendentals=0),
        input_output_aliases=dict(aliases),
        name=name,
    )(*[a for a, _ in ins], *after)


def out(shape, dtype, spec=None):
    return jax.ShapeDtypeStruct(shape, dtype), whole(shape) if spec is None else spec


def from_hbm(array):
    return pltpu.with_memory_space_constraint(array, pltpu.HBM), whole(array.shape)


def full(array):
    return array, whole(array.shape)


def by_rows(rows, width, column=0):
    return pl.BlockSpec((rows, width), lambda i: (i, column))


def by_columns(rows, width):
    return pl.BlockSpec((rows, width), lambda i: (0, i))


def by_tiles(shape):
    return pl.BlockSpec((STEP, *shape[1:]), lambda i: (i, 0, 0))


def fixed_columns(rows, width, column):
    return pl.BlockSpec((rows, width), lambda i: (0, column))


def prepare(lens, seq, after=()):
    _, _, window = geometry(seq)
    shape = (seq // TILE, window, 128)
    return launch(
        "prepare",
        functools.partial(prepare_kernel, seq),
        seq // TILE // STEP,
        [(lens, smem())],
        [out(shape, F32, by_tiles(shape))],
        [],
        after,
        cost=0,
    )[0]


def by_blocks(source, width, chunk, blocks):
    group = 128 // chunk
    lane = iota((source.shape[0], 128), 1) // chunk
    columns = []
    for at in range(0, blocks * width, 128):
        column = None
        for k in range(group):
            device, block = (at % width) // chunk + k, at // width
            lanes = (device * blocks + block) * chunk
            piece = source[:, lanes // 128 * 128 : lanes // 128 * 128 + 128]
            shift = (k * chunk - lanes) % 128
            if shift:
                piece = pltpu.roll(piece, shift, 1)
            column = piece if column is None else jnp.where(lane == k, piece, column)
        columns.append(column)
    return columns


def from_blocks(parts, width, chunk, blocks):
    group = 128 // chunk
    lane = iota((parts[0].shape[0], 128), 1) // chunk
    columns = []
    for at in range(0, blocks * width, 128):
        column = None
        for k in range(group):
            device, block = divmod(at // chunk + k, blocks)
            lanes = device * chunk
            piece = parts[block][:, lanes // 128 * 128 : lanes // 128 * 128 + 128]
            shift = (k * chunk - lanes) % 128
            if shift:
                piece = pltpu.roll(piece, shift, 1)
            column = piece if column is None else jnp.where(lane == k, piece, column)
        columns.append(column)
    return columns


def pack_kernel(joint_ref, expand_ref, output_ref, reduce_ref, *refs):
    small, (a_ref, e1_ref, e2_ref) = refs[:6], refs[6:]
    chunk, d = output_ref.shape
    wide = joint_ref.shape[1]

    def line(vectors):
        flat = jnp.concatenate([v[...].reshape(1, v.shape[0]).astype(F32) for v in vectors], axis=1)
        gap = jnp.zeros((1, 128 - flat.shape[1]), F32)
        return jnp.concatenate([flat, gap], axis=1)

    def block(parts):
        gap = jnp.zeros((chunk - len(parts), 128), F32)
        return jnp.concatenate(parts + [gap], axis=0).astype(BF)

    a_ref[:, :wide] = joint_ref[...]
    a_ref[:, wide:] = block([line(small[:2]), line(small[2:5]), line(small[5:])])
    columns = by_blocks(expand_ref[...].astype(F32), d, chunk, 4)
    for i, column in enumerate(columns):
        target = (e1_ref, e2_ref)[i * 128 // (2 * d)]
        at = i * 128 % (2 * d)
        target[:, at : at + 128] = column.astype(BF)
    for k in range(4):
        target = (e1_ref, e2_ref)[k // 2]
        target[:, (2 + k % 2) * d : (3 + k % 2) * d] = reduce_ref[k * chunk : (k + 1) * chunk, :]
    e1_ref[:, 4 * d : 5 * d] = output_ref[...]


def pack(joint, expand, output, reduce, small):
    rows, wide = joint.shape
    d = output.shape[1]
    return launch(
        "pack",
        pack_kernel,
        1,
        [from_hbm(a) for a in (joint, expand, output, reduce, *small)],
        [out((rows, wide + 128), BF), out((rows, 5 * d), BF), out((rows, 4 * d), BF)],
        [],
        mib=4,
        cost=0,
    )


def finish_kernel(one_ref, two_ref, expand_ref, reduce_ref, output_ref, *small):
    chunk, d = output_ref.shape
    parts = [one_ref[:, :d], one_ref[:, d : 2 * d], two_ref[:, :d], two_ref[:, d : 2 * d]]
    for i, column in enumerate(from_blocks(parts, d, chunk, 4)):
        expand_ref[:, i * 128 : (i + 1) * 128] = column
    for k in range(4):
        source = (one_ref, two_ref)[k // 2]
        reduce_ref[k * chunk : (k + 1) * chunk, :] = source[:, (2 + k % 2) * d : (3 + k % 2) * d]
    at = two_ref.shape[1] - 128
    output_ref[...] = two_ref[:, at - d : at]
    for k in range(3):
        small[k][...] = two_ref[0:1, at + k * chunk : at + (k + 1) * chunk].reshape(chunk)
    small[3][...] = two_ref[1:2, at : at + 4 * chunk].reshape(4 * chunk)


def finish(one, two, after):
    rows, d = one.shape[0], one.shape[1] // 4
    return launch(
        "finish",
        finish_kernel,
        1,
        [full(one), full(two)],
        [out((rows, 4 * d), F32), out((4 * rows, d), F32), out((rows, d), F32)]
        + [out((rows,), F32)] * 3
        + [out((4 * rows,), F32)],
        [],
        after,
    )


def close_kernel(lanes, before_ref, keep_ref, other_ref, joint_ref, gain_ref, shift_ref):
    total = keep_ref[...].astype(F32) + other_ref[...].astype(F32)
    chunk, d = joint_ref.shape[0], joint_ref.shape[1] // 3
    at = 4 * d
    for k in range(3):
        joint_ref[:, k * d : k * d + lanes] = before_ref[:, at + k * lanes : at + (k + 1) * lanes]
        joint_ref[:, k * d + lanes : (k + 1) * d] = total[:, k * lanes : (k + 1) * lanes]
    gain_ref[...] = total[0:1, 3 * lanes : 3 * lanes + chunk].reshape(chunk)
    shift_ref[...] = total[0:1, 3 * lanes + chunk : 3 * lanes + 2 * chunk].reshape(chunk)


def close(before, pair, d):
    rows = before.shape[0]
    return launch(
        "close",
        functools.partial(close_kernel, d // GROUPS),
        1,
        [full(before), full(pair[0]), full(pair[1])],
        [out((rows, 3 * d), F32)] + [out((rows,), F32)] * 2,
        [],
        cost=0,
    )


def merge_kernel(plan, *refs):
    n = sum(1 if kind == "carry" else 2 * count for kind, count in plan)
    ins, outs = list(refs[:n]), list(refs[n:])
    for kind, count in plan:
        if kind == "carry":
            outs.pop(0)[...] = ins.pop(0)[...]
            continue
        targets = [outs.pop(0) for _ in range(2 if kind == "add" else 1)]
        at = 0
        for _ in range(count):
            first, second = ins.pop(0), ins.pop(0)
            rows, width = first.shape
            columns = slice(at, at + width)
            at += width
            if kind == "join":
                targets[0][:rows, columns] = first[...]
                targets[0][rows:, columns] = second[...]
                continue
            total = first[...].astype(F32) + second[...].astype(F32)
            if kind == "last":
                targets[0][:, columns] = total
                continue
            targets[0][:, columns] = total[: rows // 2].astype(BF)
            targets[1][:, columns] = total[rows // 2 :].astype(BF)


def merge(plan, arrays, after):
    outs = []
    for (kind, _), pairs in zip(plan, arrays, strict=True):
        rows = pairs[0][0].shape[0]
        width = sum(p[0].shape[1] for p in pairs)
        if kind == "carry":
            outs.append(out((rows, width), pairs[0][0].dtype))
        elif kind == "join":
            outs.append(out((2 * rows, width), BF))
        elif kind == "last":
            outs.append(out((rows, width), F32))
        else:
            outs += [out((rows // 2, width), BF)] * 2
    return launch(
        "merge",
        functools.partial(merge_kernel, plan),
        1,
        [full(a) for pairs in arrays for pair in pairs for a in pair],
        outs,
        [],
        after,
        cost=0,
    )


def attend(order, me, group, bias, x, weights, vec, after=()):
    seq, d = x.shape
    lanes = d // GROUPS
    _, total, window = geometry(seq)
    tiles = seq // TILE
    cols = lanes // DIM * TILE
    near, _, far_base = split_levels(seq)
    scratch = [
        pltpu.VMEM((sum(POOL // v.factor for v in near), POOL), BF),
        pltpu.VMEM((total - far_base, seq), BF),
    ]
    ins = [(me, smem()), (bias, by_tiles(bias.shape))]
    if group == 0:
        ins.append(from_hbm(x))
    else:
        ins.append(full(x))
    ins += [full(w) for w in weights]
    outs = [
        out((tiles, window, cols), BF, by_tiles((tiles, window, cols))),
        out((seq, lanes), BF, by_rows(STEP * TILE, lanes)),
        out((seq, lanes), BF),
        out((total, lanes), BF),
        out((total, lanes), BF),
    ]
    if group == 0:
        ins.append(full(vec))
        outs += [out((seq, d), BF), out((d, 3 * d), BF), out((8, d), F32)]
    return launch(
        "attend",
        functools.partial(attend_kernel, order, seq, group),
        tiles // STEP,
        ins,
        outs,
        scratch,
        after,
        cost=2 * 10**10 if group == 0 else 0,
    )


def ffn_scratch(seq, d):
    return [
        pltpu.VMEM((d, 2 * d), BF),
        pltpu.VMEM((d, 2 * d), BF),
        pltpu.VMEM((d, d), BF),
        pltpu.VMEM((1, 2 * d), F32),
        pltpu.VMEM((d, seq), BF),
        pltpu.VMEM((seq, d), BF),
        pltpu.VMEM((seq, d), BF),
        pltpu.VMEM((d, d), BF),
        pltpu.VMEM((8, d), F32),
    ]


def ffn_first(order, me, lens, x, cot, ctx0, ctx1, e1, vec, ebias, after=()):
    seq, d = x.shape
    return launch(
        "ffn_first",
        functools.partial(ffn_kernel, order, 0),
        2,
        [(me, smem()), (lens, smem())]
        + [full(a) for a in (x, cot, ctx0, ctx1, *e1, vec, ebias)],
        [
            out((seq, d), F32),
            out((seq, d), BF),
            out((seq, d), BF),
            out((seq, d), F32),
            out((seq, d), F32),
            out((1, 2 * d), F32),
            out((d // 2, 4 * d), BF),
            out((d // 2, 4 * d), BF),
        ],
        ffn_scratch(seq, d),
        after,
        mib=12,
    )


def ffn_second(order, me, lens, cot, kept, ctx0, ctx1, e1, e2, vec, ebias, after=()):
    seq, d = cot.shape
    width = d + (128 if order.stepped else 0)
    return launch(
        "ffn_second",
        functools.partial(ffn_kernel, order, 1),
        2,
        [(me, smem()), (lens, smem())]
        + [full(a) for a in (cot, *kept, ctx0, ctx1, *e1, *e2, vec, ebias)],
        [
            out((seq, d), BF),
            out((seq, d), F32),
            out((seq, d), BF),
            out((d // 2, 4 * d), BF),
            out((d // 2, 4 * d), BF),
            out((d // 2, width), BF),
            out((d // 2, width), BF),
            out((8, d), F32),
            out((1, 2 * d), F32),
            out((seq, d), F32),
            out((seq, d), F32),
        ],
        ffn_scratch(seq, d) + [pltpu.VMEM((seq, d), BF)],
        after,
        aliases={3: 1, 6: 9, 7: 10},
        mib=14,
    )


def attend_back(order, me, group, prob, q, cg, kx, vx, first_in, weights, more, after=()):
    seq, d = first_in.shape
    lanes = d // GROUPS
    levels, total, _ = geometry(seq)
    spread = spreading(seq)
    last = group == GROUPS - 1
    extra = (128 if order.stepped else 0) if last else more[0].shape[1]
    ins = [
        (me, smem()),
        (prob, by_tiles(prob.shape)),
        (q, by_rows(STEP * TILE, lanes)),
        (cg, by_rows(STEP * TILE, lanes, group)),
        full(kx),
        full(vx),
        full(first_in),
        full(weights),
        full(jnp.asarray(spread, BF)),
    ]
    ins += [full(a) for a in more]
    outs = [out((d // 2, 3 * lanes + extra), BF)] * 2 + [out((seq, d), F32)]
    if last:
        outs.append(out((8, d), F32))
    return launch(
        "attend_back",
        functools.partial(attend_back_kernel, order, seq, group),
        prob.shape[0] // STEP,
        ins,
        outs,
        [
            pltpu.VMEM((total, lanes), F32),
            pltpu.VMEM((total, lanes), F32),
            pltpu.VMEM((seq, 3 * lanes), BF),
            pltpu.VMEM((d, 3 * lanes), BF),
        ],
        after,
        mib=17,
    )


def token_kernel(x_ref, fig_ref, hg_ref, gain_ref, kept_ref, tg_ref, mixed_ref, mark_ref):
    hat, scale = normalize(x_ref[...].astype(F32))
    grad = hg_ref[...] + norm_back(fig_ref[...], hat, scale, gain_ref[0:1, :])
    tg_ref[...] = grad.astype(BF)
    mixed_ref[...] = kept_ref[...]
    mark_ref[...] = jnp.zeros_like(mark_ref)


def token_grads(x, fig, hidden_grad, gain, kept, after=()):
    seq, d = x.shape
    rows = 512
    return launch(
        "token_grad",
        token_kernel,
        seq // rows,
        [(a, by_rows(rows, d)) for a in (x, fig, hidden_grad)] + [full(gain), (kept, by_rows(rows, d))],
        [(pltpu.HBM((seq, d), BF), by_rows(rows, d))] * 2 + [out((8, 128), F32)],
        [],
        after,
        cost=0,
    )


class Gather:
    def __init__(self, order, value):
        self.order, self.bits, self.have, self.other = order, list(order.bits), value, None
        if not order.stepped:
            half = value.shape[0] // 2
            self.have, self.other, self.bits = value[:half], value[half:], []

    def send(self):
        if self.bits:
            self.other = swap(self.order, self.have, self.bits.pop(0))

    def kind(self):
        return "join", 1

    def pairs(self):
        return [(self.have, self.other)]

    def pair(self):
        return self.have, self.other

    def take(self, outs):
        self.have = outs.pop(0)


class Scatter:
    def __init__(self, order, halves):
        self.order, self.bits, self.halves, self.other = order, order.bits[::-1], halves, None
        self.done = None
        self.beside = []
        if not order.stepped:
            self.done = jnp.concatenate(halves, axis=0).astype(F32)

    def send(self):
        if self.order.stepped:
            self.other = swap(self.order, self.halves[1], self.bits.pop(0))

    def kind(self):
        return "add" if self.bits else "last", 1 + len(self.beside)

    def pairs(self):
        return [(self.halves[0], self.other)] + self.beside

    def absorb(self, chain):
        if self.order.stepped:
            self.beside += chain.pairs()

    def take(self, outs):
        self.beside = []
        if self.bits:
            self.halves = outs.pop(0), outs.pop(0)
        else:
            self.done = outs.pop(0)


def swap(order, value, bit):
    return lax.ppermute(value, AXES, [(i, i ^ bit) for i in range(order.devices)])


def advance(order, chains, after=(), carry=None, hold=()):
    if not order.stepped:
        return () if carry is None else ((), carry)
    plan = [c.kind() for c in chains]
    arrays = [c.pairs() for c in chains]
    if carry is not None:
        plan.append(("carry", 1))
        arrays.append([(carry,)])
    outs = list(merge(plan, arrays, after))
    marks = tuple(outs)
    if carry is not None:
        carry = outs.pop()
    for c in chains:
        c.take(outs)
        if c.bits and c not in hold:
            c.send()
    return marks[:1] if carry is None else (marks[:1], carry)


def release(order, held, chains, after):
    mark, high = advance(order, chains, after, held.halves[1])
    held.halves = held.halves[0], high
    held.send()
    return mark


def local(order, me, tokens, cotangent, lens, joint_w, output_w, expand_w, reduce_w,
          attn_gain, attn_shift, ffn_gain, ffn_shift, expand_bias, reduce_bias):
    seq, d = tokens.shape
    lanes = d // GROUPS
    rows = joint_w.shape[0]
    ff = expand_w.shape[1]
    vec = jnp.zeros((16, d), F32)
    ebias = jnp.zeros((1, ff), F32)
    if order.stepped:
        small = [attn_gain, attn_shift, ffn_gain, ffn_shift, reduce_bias, expand_bias]
        first, second, third = pack(joint_w, expand_w, output_w, reduce_w, small)
        joint = Gather(order, first)
        e1 = Gather(order, second)
        e2 = Gather(order, third)
    else:
        small = [attn_gain, attn_shift, ffn_gain, ffn_shift, reduce_bias]
        small = [lax.all_gather(v, AXES, tiled=True) for v in small]
        small += list(lax.all_gather(expand_bias, AXES, tiled=True).reshape(4, d))
        vec = jnp.pad(jnp.stack(small), ((0, 7), (0, 0))).astype(F32)
        e, o, r = [lax.all_gather(w, AXES, axis=0, tiled=True) for w in (expand_w, output_w, reduce_w)]
        r = [r[k * d : (k + 1) * d] for k in range(4)]
        joint = Gather(order, lax.all_gather(joint_w, AXES, axis=0, tiled=True))
        e1 = Gather(order, jnp.concatenate([e[:, : 2 * d], r[0], r[1], o], axis=1))
        e2 = Gather(order, jnp.concatenate([e[:, 2 * d :], r[2], r[3]], axis=1))
    joint.send()
    mark = advance(order, [joint])
    e1.send()
    mark = advance(order, [joint, e1], mark)
    e2.send()
    mark = advance(order, [joint, e1, e2], mark)
    bias = prepare(lens, seq, mark)
    mark = advance(order, [joint, e1, e2], (bias,))
    p0, ctx0, q0, kx0, vx0, first_in, w, gain = attend(order, me, 0, bias, tokens, joint.pair(), vec, mark)
    p1, ctx1, q1, kx1, vx1 = attend(order, me, 1, bias, first_in, (w,), vec, (ctx0,))
    mark = advance(order, [e1, e2], (ctx1,))
    *kept, lo, hi = ffn_first(
        order, me, lens, tokens, cotangent, ctx0, ctx1, e1.pair(), gain, ebias, mark
    )
    t1 = Scatter(order, (lo, hi))
    mark = advance(order, [e2], (lo,))
    t1.send()
    mark = advance(order, [t1], mark)
    mixed, hg, cg, lo, hi, olo, ohi, sums, esum, _, _ = ffn_second(
        order, me, lens, cotangent, kept, ctx0, ctx1, e1.pair(), e2.pair(), gain, ebias, mark
    )
    mark = advance(order, [t1], (cg,))
    t2 = Scatter(order.turned, (lo, hi))
    t2.send()
    lo, hi, fig = attend_back(order, me, 0, p0, q0, cg, kx0, vx0, first_in, w, (olo, ohi), mark)
    mark, hi = advance(order, [t1, t2], (fig,), hi, [t1])
    j0 = Scatter(order, (lo, hi))
    j0.send()
    mark = release(order, t1, [j0], mark)
    lo, hi, fig, tail_sums = attend_back(
        order, me, 1, p1, q1, cg, kx1, vx1, first_in, w, (tokens, fig), mark
    )
    mark, hi = advance(order, [t1, t2, j0], (tail_sums,), hi, [t1, j0])
    j1 = Scatter(order.turned, (lo, hi))
    j1.send()
    mark = release(order, j0, [j1], mark)
    t1.send()
    token_grad, mixed, mark = token_grads(tokens, fig, hg, gain, mixed, mark)
    t2.absorb(j0)
    mark = advance(order, [t2, t1], (mark,))
    mark = advance(order, [j1], mark)
    mark = advance(order, [t2], mark)
    mark = advance(order, [j1], mark)
    mark = advance(order, [j1], mark)
    if order.stepped:
        advance(order, [t2], mark)
        expand_grad, reduce_grad, output_grad, *small = finish(t1.done, t2.done, mark)
        joint_grad, *first_small = close(t2.done, j1.pairs()[0], d)
        small = [*first_small, small[0], small[1], small[3], small[2]]
    else:
        parts = []
        for k in range(3):
            parts += [c.done[:, k * lanes : (k + 1) * lanes] for c in (j0, j1)]
        joint_grad = jnp.concatenate(parts, axis=1)
        one, two = t1.done, t2.done
        expand_grad = lax.psum_scatter(
            jnp.concatenate([one[:, : 2 * d], two[:, : 2 * d]], axis=1), AXES, scatter_dimension=0, tiled=True
        )
        reduce_grad = lax.psum_scatter(
            jnp.concatenate([t[:, k * d : (k + 1) * d] for t in (one, two) for k in (2, 3)], axis=0),
            AXES,
            scatter_dimension=0,
            tiled=True,
        )
        output_grad = lax.psum_scatter(j0.done[:, 3 * lanes :], AXES, scatter_dimension=0, tiled=True)
        joint_grad = lax.psum_scatter(joint_grad, AXES, scatter_dimension=0, tiled=True)
        esums = jnp.concatenate([kept[5][0], esum[0]])
        vectors = [tail_sums[0], tail_sums[1], sums[0], sums[1], esums, sums[2]]
        small = [lax.psum_scatter(v, AXES, scatter_dimension=0, tiled=True) for v in vectors]
    return (mixed, token_grad, joint_grad, output_grad, expand_grad, reduce_grad, *small)


def shards(order, *args):
    sub = lax.axis_size("sub")
    me = (lax.axis_index("dp") * sub + lax.axis_index("sub")).astype(jnp.int32).reshape(1)
    return local(order, me, *args)


def solution(mesh):
    order = Order(math.prod(mesh.shape[a] for a in AXES))
    wide = P(AXES, None)
    flat = P(AXES)
    return jax.shard_map(
        functools.partial(shards, order),
        mesh=mesh,
        in_specs=(wide,) * 7 + (flat,) * 6,
        out_specs=(wide,) * 6 + (flat,) * 6,
        check_vma=False,
    )
```
